32 devices in a mesh: seq: 8 (over z, x), fsdp: 4 (over y, core).
Axes of the slice: x: 2, y: 2, z: 4, core: 2. Of those that a mesh axis runs over, the one named last changes fastest.
Arguments:
- hidden: bfloat16 [4, 2048, 1536], P('fsdp', 'seq'), may hold values from -6 to 6
- lengths: int32 [4], P('fsdp'), may hold values from 512 to 2048, as said below
- norm_gain: bfloat16 [1536], P('fsdp'), may hold values from 0.5 to 1.5
- in_weight: bfloat16 [1536, 6448], P('fsdp'), may hold values from -0.15625 to 0.15625
- conv_weight: bfloat16 [4, 3328], P(None, 'fsdp'), may hold values from -3 to 3
- conv_bias: bfloat16 [3328], P('fsdp'), may hold values from -3 to 3
- dt_bias: bfloat16 [48], P('fsdp'), may hold values from -5 to -3
- a_log: bfloat16 [48], P('fsdp'), may hold values from -9 to 1
- skip_d: bfloat16 [48], P('fsdp'), may hold values from 0.5 to 1.5
- gate_gain: bfloat16 [3072], P('fsdp'), may hold values from 0.5 to 1.5
- out_weight: bfloat16 [3072, 1536], P('fsdp'), may hold values from -0.109375 to 0.109375
- out_grad: bfloat16 [4, 2048, 1536], P('fsdp', 'seq'), may hold values from -6 to 6
Outputs:
- output: bfloat16 [4, 2048, 1536], P('fsdp', 'seq')
- hidden_grad: bfloat16 [4, 2048, 1536], P('fsdp', 'seq')
- norm_gain_grad: float32 [1536], P('fsdp')
- in_weight_grad: float32 [1536, 6448], P('fsdp')
- conv_weight_grad: float32 [4, 3328], P(None, 'fsdp')
- conv_bias_grad: float32 [3328], P('fsdp')
- dt_bias_grad: float32 [48], P('fsdp')
- a_log_grad: float32 [48], P('fsdp')
- skip_d_grad: float32 [48], P('fsdp')
- gate_gain_grad: float32 [3072], P('fsdp')
- out_weight_grad: float32 [3072, 1536], P('fsdp')
The draws below stay inside these ranges and needn't reach their ends.
Inputs may be any that keep to these rules, and one draw needn't show every extreme that they name: `lengths`: a slot's live tokens are its first ones; in every draw one slot is full and one holds 512 tokens.
All inputs are finite; a program needn't handle non-finite values.
Results may differ from the reference program's by a relative error of at most 0.0075.
The reference program's roundings to bfloat16 on the way count: a program that leaves them out, or rounds other values in their place, can miss the bound.
Values may be sent and summed in bfloat16 or wider, within the bound.
No kernel may reach another device: no remote copies, remote signals or barrier semaphores. Data moves between devices by JAX's collectives and lax.ppermute only.
A program may use at most 256 MiB of HBM per device.

```python
import jax
import jax.numpy as jnp
from jax import lax

D = 1536
HEADS = 48
HEADDIM = 64
STATE = 128
CONV = 4
SPAN = 256
INNER = 3072
CHANNELS = 3328
PROJ = 6448
SEQ_LEN = 2048
SLOTS = 4


def draw_lengths(key, part):
    first_key, second_key = jax.random.split(jax.random.fold_in(key, 17))
    drawn = jax.random.randint(first_key, (SLOTS,), SEQ_LEN // 4, SEQ_LEN + 1)
    order = jax.random.permutation(second_key, SLOTS)
    filled = jnp.where(order == 0, SEQ_LEN, drawn)
    return jnp.where(order == 1, SEQ_LEN // 4, filled).astype(jnp.int32)


def levels(stream_key, extent, cuts, least, largest):
    def one(dim, parts):
        draws = jax.random.uniform(jax.random.fold_in(jax.random.fold_in(stream_key, 6), dim), (parts,), jnp.float32, least / len(cuts), largest / len(cuts))
        return jnp.repeat(jnp.exp(draws), extent[dim] // parts).reshape((-1,) + (1,) * (len(extent) - dim - 1))

    factor_of = one(*cuts[0])
    for cut in cuts[1:]:
        factor_of = factor_of * one(*cut)
    return factor_of


def centred(own_key, dims, deviation, reach, pieces=(), held_as=jnp.bfloat16):
    entries = jax.random.normal(own_key, dims, jnp.float32) * deviation
    if len(pieces) > 0:
        entries = levels(own_key, dims, pieces, -0.22, 0.18) * entries
    return jnp.clip(entries, min=-reach, max=reach).astype(held_as)


def setup_inputs(seed: int = 0) -> dict:
    key_list = jax.random.split(jax.random.key(seed), 13)
    return {
        "hidden": centred(key_list[0], (SLOTS, SEQ_LEN, D), 1.0, 6.0, ((0, 4), (1, 8))),
        "lengths": draw_lengths(jax.random.fold_in(key_list[12], 71), 0),
        "norm_gain": jnp.clip(1.0 + 0.1 * jax.random.normal(key_list[2], (D,), jnp.float32), 0.5, 1.5).astype(jnp.bfloat16),
        "in_weight": centred(key_list[3], (D, PROJ), D ** -0.5, 0.15625, ((0, 4),)),
        "conv_weight": centred(key_list[4], (CONV, CHANNELS), CONV ** -0.5, 3.0, ((1, 4),)),
        "conv_bias": centred(key_list[5], (CHANNELS,), 0.5, 3.0, ((0, 4),)),
        "dt_bias": jnp.clip(-5.0 + 2.0 * jax.random.uniform(key_list[6], (HEADS,), jnp.float32) ** levels(key_list[6], (HEADS,), ((0, 4),), -0.2, 0.2), -5.0, -3.0).astype(jnp.bfloat16),
        "a_log": jnp.clip(-9.0 + 10.0 * jax.random.uniform(key_list[7], (HEADS,), jnp.float32) ** levels(key_list[7], (HEADS,), ((0, 4),), -0.2, 0.2), -9.0, 1.0).astype(jnp.bfloat16),
        "skip_d": jnp.clip(0.5 + 1.0 * jax.random.uniform(key_list[8], (HEADS,), jnp.float32) ** levels(key_list[8], (HEADS,), ((0, 4),), -0.2, 0.2), 0.5, 1.5).astype(jnp.bfloat16),
        "gate_gain": jnp.clip(1.0 + 0.1 * jax.random.normal(key_list[9], (INNER,), jnp.float32), 0.5, 1.5).astype(jnp.bfloat16),
        "out_weight": centred(key_list[10], (INNER, D), INNER ** -0.5, 0.109375, ((0, 4),)),
        "out_grad": centred(key_list[11], (SLOTS, SEQ_LEN, D), 1.0, 6.0, ((0, 4), (1, 8))),
    }


epsilon = 1e-05
highest = lax.Precision.HIGHEST

@jax.custom_vjp
def low(v):
    return lax.optimization_barrier(v.astype(jnp.bfloat16)).astype(jnp.float32)

@jax.custom_vjp
def low_back(v):
    return v

def low_keep(v):
    return (low(v), None)

def low_pass(kept, grad):
    return (grad,)

def back_keep(v):
    return (v, None)

def back_low(kept, grad):
    return (low(grad),)
low.defvjp(low_keep, low_pass)
low_back.defvjp(back_keep, back_low)

def rms_scale(values, gain):
    return values * lax.rsqrt(lax.optimization_barrier(jnp.mean(values * values, axis=-1, keepdims=True)) + epsilon) * gain

def slot_forward(tokens, params):
    norm_gain, in_weight, conv_weight, conv_bias, dt_bias, a_log, skip_d, gate_gain, out_weight = params
    length = tokens.shape[0]
    spans = length // SPAN
    normed = low(rms_scale(tokens, norm_gain))
    projected = low(low_back(jnp.dot(normed, in_weight, precision=highest)))
    gate_part = projected[:, :INNER]
    conv_in = projected[:, INNER:INNER + CHANNELS]
    dt_raw = projected[:, INNER + CHANNELS:]
    padded = jnp.concatenate([jnp.zeros((CONV - 1, CHANNELS), jnp.float32), conv_in], axis=0)
    summed = conv_bias
    for offset in range(CONV):
        summed = summed + conv_weight[offset] * padded[offset:offset + length]
    conv_out = jax.nn.silu(summed)
    heads_x = low(conv_out[:, :INNER]).reshape(spans, SPAN, HEADS, HEADDIM)
    proj_b = low(conv_out[:, INNER:INNER + STATE]).reshape(spans, SPAN, STATE)
    proj_c = low(conv_out[:, INNER + STATE:]).reshape(spans, SPAN, STATE)
    step_size = jax.nn.softplus(dt_raw + dt_bias).reshape(spans, SPAN, HEADS)
    log_decay = jnp.cumsum(step_size * -jnp.exp(a_log), axis=1)
    scores = low_back(jnp.einsum('ktn,ksn->kts', proj_c, proj_b, precision=highest))
    later = lax.broadcasted_iota(jnp.int32, (SPAN, SPAN), 0)
    earlier = lax.broadcasted_iota(jnp.int32, (SPAN, SPAN), 1)
    causal = (later >= earlier)[None, :, :, None]
    exponent = log_decay[:, :, None, :] - log_decay[:, None, :, :]
    decays = jnp.where(causal, jnp.exp(jnp.where(causal, exponent, 0.0)), 0.0)
    mixing = low(scores[:, :, :, None] * decays * step_size[:, None, :, :])
    intra = jnp.einsum('ktsh,kshp->kthp', mixing, heads_x, precision=highest)
    to_end = jnp.exp(log_decay[:, -1:, :] - log_decay)
    weighted = low(heads_x * (to_end * step_size)[:, :, :, None])
    fresh_state = low_back(jnp.einsum('kthp,ktn->khpn', weighted, proj_b, precision=highest))
    through = jnp.exp(log_decay[:, -1, :])

    def carry_step(state, element):
        factor, added = element
        return (factor[:, None, None] * state + added, state)
    start_state = jnp.zeros((HEADS, HEADDIM, STATE), jnp.float32)
    final_state, incoming = lax.scan(carry_step, start_state, (through, fresh_state))
    reached = low_back(jnp.einsum('ktn,khpn->kthp', proj_c, low(incoming), precision=highest))
    mixer = low_back(intra + jnp.exp(log_decay)[:, :, :, None] * reached + skip_d[:, None] * heads_x)
    gated = mixer.reshape(length, INNER) * jax.nn.silu(gate_part)
    mixed = low(rms_scale(gated, gate_gain))
    return tokens + jnp.dot(mixed, out_weight, precision=highest)

def reference(hidden, lengths, norm_gain, in_weight, conv_weight, conv_bias, dt_bias, a_log, skip_d, gate_gain, out_weight, out_grad):
    params = tuple((weight_arg.astype(jnp.float32) for weight_arg in (norm_gain, in_weight, conv_weight, conv_bias, dt_bias, a_log, skip_d, gate_gain, out_weight)))
    position = lax.broadcasted_iota(jnp.int32, (SEQ_LEN,), 0)

    def one_slot(running, bundle):
        tokens, length, cotangent = bundle
        live_mask = (position < length).astype(jnp.float32)
        result, pullback = jax.vjp(slot_forward, tokens.astype(jnp.float32), params)
        grad_tokens, grad_params = pullback(cotangent.astype(jnp.float32) * live_mask[:, None])
        running = jax.tree.map(jnp.add, running, grad_params)
        return (running, (result.astype(jnp.bfloat16), grad_tokens.astype(jnp.bfloat16)))
    zero_grads = tuple((jnp.zeros_like(weight_arg) for weight_arg in params))
    grad_sums, (outputs, grad_hidden) = lax.scan(one_slot, zero_grads, (hidden, lengths, out_grad))
    return (outputs, grad_hidden, grad_sums[0], grad_sums[1], grad_sums[2], grad_sums[3], grad_sums[4], grad_sums[5], grad_sums[6], grad_sums[7], grad_sums[8])
```

```python
import jax
import jax.numpy as jnp
from jax import lax
from jax.sharding import PartitionSpec as P

HEADS = 48
HEADDIM = 64
STATE = 128
CONV = 4
INNER = 3072
CHANNELS = 3328
PROJ = 6448
PLANES = 2
CORES = 2

f32 = jnp.float32
bf16 = jnp.bfloat16
epsilon = 1e-05


class Ring:
    def __init__(self, seq, fsdp):
        self.seq, self.fsdp = seq, fsdp
        self.clock = None
        self.line, self.row = seq // PLANES, fsdp // CORES

    def send(self, block, move):
        route = []
        for s in range(self.seq):
            for f in range(self.fsdp):
                there = move(s // PLANES, s % PLANES, f // CORES, f % CORES)
                if there is None:
                    continue
                z, x, y, c = there
                route.append((s * self.fsdp + f, (z * PLANES + x) * self.fsdp + y * CORES + c))
        arrived = lax.ppermute(block, ("seq", "fsdp"), route)
        self.clock.pending.append(arrived)
        return arrived

    def core(self, block):
        return self.send(block, lambda z, x, y, c: (z, x, y, 1 - c))

    def plane(self, block):
        return self.send(block, lambda z, x, y, c: (z, 1 - x, y, c))

    def from_row(self, block, distance):
        return self.send(block, lambda z, x, y, c: (z, x, (y - distance) % self.row, c))

    def far(self, block, distance):
        return self.send(block, lambda z, x, y, c: (z ^ distance, x, y, c))

    def next_block(self, block, distance):
        def move(z, x, y, c):
            s = z * PLANES + x + distance
            return (s // PLANES, s % PLANES, y, c) if 0 <= s < self.seq else None

        return self.send(block, move)


def rows_of(block, index, count):
    return lax.dynamic_slice_in_dim(block, index * count, count, axis=0)


def swapped(ring, distance):
    seq_index = lax.axis_index("seq")
    if distance == 0:
        return seq_index % PLANES, ring.plane
    bit = (seq_index // PLANES // distance) % 2
    return bit, lambda block: ring.far(block, distance)


def cube(ring):
    distances, distance = [0], 1
    while distance < ring.line:
        distances.append(distance)
        distance *= 2
    return distances


def halve(ring, distance, block):
    bit, send = swapped(ring, distance)
    half = block.shape[0] // 2
    arrived = send(rows_of(block, 1 - bit, half).astype(bf16))
    return rows_of(block, bit, half) + arrived.astype(f32)


def double(ring, distance, block):
    bit, send = swapped(ring, distance)
    other = send(block)
    low = jnp.where(bit == 0, block, other)
    high = jnp.where(bit == 0, other, block)
    return jnp.concatenate([low, high], axis=0)


class Total:
    def __init__(self, ring, grad):
        self.ring, self.value = ring, grad
        self.steps = [(halve, d) for d in cube(ring)] + [(double, d) for d in reversed(cube(ring))]

    def step(self):
        if self.steps:
            kind, distance = self.steps.pop(0)
            if kind is double and self.value.dtype != bf16:
                self.value = self.value.astype(bf16)
            self.value = kind(self.ring, distance, self.ring.clock.now(self.value))

    def finish(self):
        while self.steps:
            self.step()
        return self.value.astype(f32)

    def halves(self):
        while len(self.steps) > 1:
            self.step()
        if self.steps:
            self.steps = []
            self.value = (self.value, self.ring.plane(self.ring.clock.now(self.value)))
        return self.value


class Clock:
    def __init__(self, value):
        self.token = value
        self.pending = []
        self.later = []

    def tick(self, *values):
        out = lax.optimization_barrier((self.token,) + values + tuple(self.pending))
        self.token = out[0]
        self.pending, self.later = self.later, []
        return out[1 : 1 + len(values)]

    def now(self, value):
        return lax.optimization_barrier((value, self.token))[0]


class Spread:
    def __init__(self, ring, block):
        self.ring, self.block = ring, block
        self.quarter = -(-block.shape[0] // 64) * 16
        self.cut = -(-self.quarter // 32) * 16
        seq_index = lax.axis_index("seq")
        self.place = seq_index % 2 + 2 * ((seq_index // PLANES) % 2)
        self.found = {(0, 0): block, (0, 1): ring.core(block)}
        for d in range(1, ring.row):
            for e in range(CORES):
                self.found[d, e] = jnp.zeros_like(block)

    def start(self, index):
        return jnp.minimum((self.place ^ index) * self.quarter, self.block.shape[0] - self.quarter)

    def put(self, pieces, index, offset=0):
        for d in range(1, self.ring.row):
            for e in range(CORES):
                piece = pieces[d - 1]
                self.found[d, e] = lax.dynamic_update_slice_in_dim(
                    self.found[d, e],
                    self.ring.core(piece) if e else piece,
                    self.start(index) + offset,
                    axis=0,
                )

    def first(self):
        ring = self.ring
        mine = lax.dynamic_slice_in_dim(self.block, self.start(0), self.quarter, axis=0)
        mine = ring.clock.now(mine)
        self.mine = [ring.from_row(mine, d) for d in range(1, ring.row)]

    def second(self):
        ring = self.ring
        mine = [ring.clock.now(part) for part in self.mine]
        self.beside = [ring.plane(part) for part in mine]
        self.behind = [ring.far(part, 1) for part in mine]
        self.put(mine, 0)

    def third(self):
        ring, cut = self.ring, self.cut
        beside = [ring.clock.now(part) for part in self.beside]
        behind = [ring.clock.now(part) for part in self.behind]
        self.corner = (
            [ring.plane(part[:cut]) for part in behind],
            [ring.far(part[cut:], 1) for part in beside],
        )
        self.put(beside, 1)
        self.put(behind, 2)

    def fourth(self):
        now = self.ring.clock.now
        self.put([now(part) for part in self.corner[0]], 3)
        self.put([now(part) for part in self.corner[1]], 3, self.cut)
        return self.found


class Pieces:
    def __init__(self, ring, block, count=1):
        self.ring, self.block = ring, block
        self.rows = block.shape[0] // count
        self.parts = []

    def near(self):
        self.beside = self.ring.core(self.ring.clock.now(self.block))

    def send(self, later=False):
        clock = self.ring.clock
        at = len(self.parts) * self.rows
        piece = clock.now(self.block[at : at + self.rows])
        self.parts.append([self.ring.from_row(piece, d) for d in range(1, self.ring.row)])
        if later:
            for _ in range(1, self.ring.row):
                clock.later.append(clock.pending.pop())

    def whole(self):
        found = {(0, 0): self.block, (0, 1): self.beside}
        for d in range(1, self.ring.row):
            parts = [self.ring.clock.now(part[d - 1]) for part in self.parts]
            found[d, 0] = jnp.concatenate(parts, axis=0) if len(parts) > 1 else parts[0]
            found[d, 1] = self.ring.core(found[d, 0])
        return found


def gather_rows(ring, block):
    found = {}
    for d in range(ring.row):
        found[d, 0] = block if d == 0 else ring.from_row(block, d)
        found[d, 1] = ring.core(found[d, 0])
    return found


def places(ring):
    index = lax.axis_index("fsdp")
    y, c = index // CORES, index % CORES
    return {
        (d, e): ((y + d) % ring.row) * CORES + (c + e) % CORES
        for d in range(ring.row)
        for e in range(CORES)
    }


def trade_columns(ring, block):
    index = lax.axis_index("fsdp")
    y, c = index // CORES, index % CORES
    width = block.shape[1] // ring.fsdp
    found = {}
    for d in range(ring.row):
        for e in range(CORES):
            target = ((y - d) % ring.row) * CORES + (c + e) % CORES
            piece = lax.dynamic_slice_in_dim(block, target * width, width, axis=1)
            if d or e:
                piece = ring.send(
                    piece,
                    lambda z, x, y, c, d=d, e=e: (z, x, (y - d) % ring.row, (c + e) % CORES),
                )
            found[d, e] = piece
    return found


class SmallSum:
    def __init__(self, ring, vector):
        self.ring, self.value = ring, vector
        self.steps = ["core", "row"] + cube(ring)

    def step(self):
        if not self.steps:
            return
        kind = self.steps.pop(0)
        vector = self.ring.clock.now(self.value)
        if kind == "core":
            self.value = vector + self.ring.core(vector)
        elif kind == "row":
            self.value = sum([self.ring.from_row(vector, d) for d in range(1, self.ring.row)], vector)
        else:
            self.value = vector + swapped(self.ring, kind)[1](vector)

    def finish(self):
        while self.steps:
            self.step()
        return self.value


def spread_factors(ring, through):
    factor = jnp.repeat(through, HEADDIM).reshape(ring.seq, -1)
    size = 8 * STATE
    return jnp.pad(factor, ((0, 0), (0, size - factor.shape[1]))).reshape(ring.seq, 8, STATE)


def traded(ring, added, through=None):
    part = added.shape[0] // ring.seq
    added = added.reshape(ring.seq, part, STATE)
    if through is None:
        return lax.all_to_all(added, "seq", 0, 0, tiled=True)
    added = jnp.concatenate([added, spread_factors(ring, through)], axis=1)
    blocks = lax.all_to_all(added, "seq", 0, 0, tiled=True)
    factor = blocks[:, part:].reshape(ring.seq, 8 * STATE)[:, :part, None]
    return blocks[:, :part], factor


def carried(ring, blocks, factor, reverse):
    part = blocks.shape[1]
    state = jnp.zeros((part, STATE), f32)
    states = [None] * ring.seq
    order = range(ring.seq - 1, -1, -1) if reverse else range(ring.seq)
    for k in order:
        states[k] = state.astype(bf16)
        state = factor[k] * state + blocks[k]
    return jnp.stack(states)


def returned(ring, states):
    states = lax.all_to_all(states, "seq", 0, 0, tiled=True)
    return states.reshape(HEADS, HEADDIM, STATE)


def place_rows(whole, sides, start, rows):
    mine, other = sides
    first = (lax.axis_index("seq") % PLANES) == 0
    half = mine.shape[0]
    low = jnp.where(first, mine, other).astype(f32)
    high = jnp.where(first, other, mine)[: rows - half].astype(f32)
    whole = lax.dynamic_update_slice_in_dim(whole, low, start, axis=0)
    return lax.dynamic_update_slice_in_dim(whole, high, start + half, axis=0)


def rms_scale(values, gain):
    return values * lax.rsqrt(jnp.mean(values * values, axis=-1, keepdims=True) + epsilon) * gain


def conv_silu(window, conv_weight, conv_bias):
    count = window.shape[0] - CONV + 1
    summed = conv_bias
    for offset in range(CONV):
        summed = summed + conv_weight[offset] * window[offset : offset + count]
    return jax.nn.silu(summed)


def step_sizes(dt_raw, dt_bias, a_log):
    step_size = jax.nn.softplus(dt_raw + dt_bias)
    return (step_size, jnp.cumsum(step_size * -jnp.exp(a_log), axis=0))


def gated_norm(mixer, gate_part, gate_gain):
    return rms_scale(mixer * jax.nn.silu(gate_part), gate_gain)


def decay_table(head_decay):
    length = head_decay.shape[1]
    later = lax.broadcasted_iota(jnp.int32, (length, length), 0)
    earlier = lax.broadcasted_iota(jnp.int32, (length, length), 1)
    causal = (later >= earlier)[None]
    exponent = head_decay[:, :, None] - head_decay[:, None, :]
    return jnp.where(causal, jnp.exp(jnp.where(causal, exponent, 0.0)), 0.0)


def state_slot(heads_x, proj_b, step_size, log_decay):
    to_end = jnp.exp(log_decay[-1:] - log_decay)
    weighted = (heads_x.astype(f32) * (to_end * step_size)[:, :, None]).astype(bf16)
    return jnp.einsum("thp,tn->hpn", weighted, proj_b, preferred_element_type=f32)


def mix_slot(heads_x, proj_b, proj_c, step_size, log_decay, incoming, skip_gain):
    scores = jnp.einsum("tn,sn->ts", proj_c, proj_b, preferred_element_type=f32)
    decays = decay_table(log_decay.T)
    mixing = (scores[None] * decays * step_size.T[:, None, :]).astype(bf16)
    intra = jnp.einsum("hts,shp->thp", mixing, heads_x, preferred_element_type=f32)
    reached = jnp.einsum("tn,hpn->thp", proj_c, incoming, preferred_element_type=f32)
    return (
        intra
        + jnp.exp(log_decay)[:, :, None] * reached
        + skip_gain[:, None] * heads_x.astype(f32)
    )


def slot_back(
    heads_x, proj_b, proj_c, step_size, log_decay, incoming_b, grad_y, grad_reach, grad_fresh, skip_gain
):
    grad_yf = grad_y.astype(f32)
    x_float = heads_x.astype(f32)
    grad_skip = jnp.sum(grad_yf * x_float, axis=(0, 2))
    grad_x = skip_gain[:, None] * grad_yf
    from_start = jnp.exp(log_decay)
    reached = jnp.einsum("tn,hpn->thp", proj_c, incoming_b, preferred_element_type=f32)
    grad_cum = from_start * jnp.sum(grad_yf * reached, axis=2)
    grad_c = jnp.einsum("thp,hpn->tn", grad_reach, incoming_b, preferred_element_type=f32)
    scores = jnp.einsum("tn,sn->ts", proj_c, proj_b, preferred_element_type=f32)
    decays = decay_table(log_decay.T)
    step_heads = step_size.T[:, None, :]
    mixing = (scores[None] * decays * step_heads).astype(bf16)
    grad_mix = jnp.einsum("thp,shp->hts", grad_y, heads_x, preferred_element_type=f32)
    grad_x = grad_x + jnp.einsum("hts,thp->shp", mixing, grad_y, preferred_element_type=f32)
    grad_scores = jnp.sum(grad_mix * decays * step_heads, axis=0).astype(bf16)
    grad_step = jnp.sum(grad_mix * scores[None] * decays, axis=1).T
    grad_exp = grad_mix * scores[None] * step_heads * decays
    grad_cum = grad_cum + (jnp.sum(grad_exp, axis=2) - jnp.sum(grad_exp, axis=1)).T
    grad_c = grad_c + jnp.einsum("ts,sn->tn", grad_scores, proj_b, preferred_element_type=f32)
    grad_b = jnp.einsum("ts,tn->sn", grad_scores, proj_c, preferred_element_type=f32)
    to_end = jnp.exp(log_decay[-1:] - log_decay)
    factor = to_end * step_size
    weighted = (x_float * factor[:, :, None]).astype(bf16)
    grad_weighted = jnp.einsum("hpn,tn->thp", grad_fresh, proj_b, preferred_element_type=f32)
    grad_b = grad_b + jnp.einsum("thp,hpn->tn", weighted, grad_fresh, preferred_element_type=f32)
    grad_x = grad_x + grad_weighted * factor[:, :, None]
    grad_factor = jnp.sum(grad_weighted * x_float, axis=2)
    grad_step = grad_step + grad_factor * to_end
    grad_tail = grad_factor * step_size * to_end
    through = jnp.exp(log_decay[-1])
    crossed = jnp.sum(grad_fresh.astype(f32) * incoming_b.astype(f32), axis=(1, 2))
    grad_end = jnp.sum(grad_tail, axis=0) + through * crossed
    last_row = lax.broadcasted_iota(jnp.int32, log_decay.shape, 0) == log_decay.shape[0] - 1
    grad_cum = grad_cum - grad_tail + jnp.where(last_row, grad_end[None, :], 0.0)
    return (grad_x, grad_b, grad_c, grad_step, grad_cum, grad_skip)


def pack(arrays):
    flat = jnp.concatenate([a.reshape(-1) for a in arrays])
    pad = -flat.shape[0] % 1024
    return jnp.pad(flat, (0, pad)).reshape(-1, 128)


def local(
    hidden,
    lengths,
    norm_gain,
    in_weight,
    conv_weight,
    conv_bias,
    dt_bias,
    a_log,
    skip_d,
    gate_gain,
    out_weight,
    out_grad,
):
    ring = Ring(lax.axis_size("seq"), lax.axis_size("fsdp"))
    ring.clock = clock = Clock(hidden[0, :8, :128])
    _, row_count, model_width = hidden.shape
    fsdp_index = lax.axis_index("fsdp")
    where = places(ring)
    tokens = hidden[0].astype(f32)

    small = [norm_gain, conv_weight, conv_bias, dt_bias, a_log, skip_d, gate_gain]
    packed = pack(small)
    gathered = gather_rows(ring, packed)
    spread = jnp.zeros((ring.fsdp,) + packed.shape, bf16)
    for key, block in gathered.items():
        spread = lax.dynamic_update_slice_in_dim(spread, block[None], where[key], axis=0)
    spread = spread.reshape(ring.fsdp, -1)
    whole_small, at = [], 0
    for part in small:
        piece = spread[:, at : at + part.size]
        at += part.size
        if part.ndim == 2:
            piece = piece.reshape((ring.fsdp,) + part.shape).transpose(1, 0, 2)
            whole_small.append(piece.reshape(part.shape[0], -1).astype(f32))
        else:
            whole_small.append(piece.reshape(-1).astype(f32))
    gain_norm, conv_taps, conv_shift, step_bias, rate_log, skip_gain, gain_gate = whole_small

    in_rows = in_weight.T
    shared = Spread(ring, in_rows[INNER:])
    (spread,) = clock.tick(spread)
    gate_pieces = Pieces(ring, in_rows[:INNER], 3)
    out_pieces = Pieces(ring, out_weight, 2)
    shared.first()
    gate_pieces.near()
    out_pieces.near()
    clock.tick()
    shared.second()
    gate_pieces.send()
    clock.tick()
    shared.third()
    gate_pieces.send(later=True)
    clock.tick()
    gate_pieces.send(later=True)
    weight_conv = shared.fourth()

    position = lax.axis_index("seq") * row_count + lax.broadcasted_iota(
        jnp.int32, (row_count, 1), 0
    )
    grad_out = jnp.where(position < lengths[0], out_grad[0], jnp.zeros_like(out_grad[0]))

    normed, pull_norm = jax.vjp(rms_scale, tokens, gain_norm)
    normed = normed.astype(bf16)
    depth = in_weight.shape[0]

    def project(weights):
        total = None
        for key, weight in weights.items():
            columns = lax.dynamic_slice_in_dim(normed, where[key] * depth, depth, axis=1)
            term = jnp.einsum("td,jd->tj", columns, weight, preferred_element_type=f32)
            total = term if total is None else total + term
        return total.astype(bf16)

    projected = project(weight_conv)
    (projected,) = clock.tick(projected)
    out_pieces.send(later=True)
    conv_in = projected[:, :CHANNELS]
    dt_raw = projected[:, CHANNELS:]
    edge_rows = ring.next_block(conv_in[row_count - CONV + 1 :], 1)
    window = jnp.concatenate([edge_rows, conv_in], axis=0).astype(f32)
    conv_out, pull_conv = jax.vjp(conv_silu, window, conv_taps, conv_shift)
    conv_low = conv_out.astype(bf16)
    heads_x = conv_low[:, :INNER].reshape(row_count, HEADS, HEADDIM)
    proj_b = conv_low[:, INNER : INNER + STATE]
    proj_c = conv_low[:, INNER + STATE :]
    (step_size, log_decay), pull_steps = jax.vjp(
        step_sizes, dt_raw.astype(f32), step_bias, rate_log
    )
    through = jnp.exp(log_decay[-1])
    fresh_state = state_slot(heads_x, proj_b, step_size, log_decay)
    (fresh_state,) = clock.tick(fresh_state)
    blocks, factor = traded(ring, fresh_state.reshape(INNER, STATE), through)
    out_pieces.send()
    weight_gate = gate_pieces.whole()
    gate_part = project(weight_gate)
    blocks, factor, gate_part = clock.tick(blocks, factor, gate_part)
    incoming = returned(ring, carried(ring, blocks, factor, False))
    weight_out = out_pieces.whole()
    grad_pieces = Pieces(ring, grad_out)
    grad_pieces.send()
    grad_pieces.near()
    (incoming,) = clock.tick(incoming)
    mixer = mix_slot(heads_x, proj_b, proj_c, step_size, log_decay, incoming, skip_gain)
    mixed, pull_gate = jax.vjp(
        gated_norm, mixer.reshape(row_count, INNER), gate_part.astype(f32), gain_gate
    )
    mixed = mixed.astype(bf16)
    normed_all = trade_columns(ring, clock.now(normed))
    (mixed,) = clock.tick(mixed)
    mixed_all = trade_columns(ring, mixed)
    grad_out_all = grad_pieces.whole()
    wide = out_weight.shape[0]

    grad_mixed = jnp.zeros((row_count, INNER), f32)
    for key, weight in weight_out.items():
        term = jnp.einsum("td,id->ti", grad_out, weight, preferred_element_type=f32)
        grad_mixed = lax.dynamic_update_slice_in_dim(grad_mixed, term, where[key] * wide, axis=1)
    grad_mixer, grad_gate, grad_g_gate = pull_gate(grad_mixed)
    grad_y = grad_mixer.astype(bf16).reshape(row_count, HEADS, HEADDIM)
    grad_reach = (grad_y.astype(f32) * jnp.exp(log_decay)[:, :, None]).astype(bf16)
    direct = jnp.einsum("thp,tn->hpn", grad_reach, proj_c, preferred_element_type=f32)
    direct, grad_y, grad_reach, grad_gate = clock.tick(
        direct, grad_y, grad_reach, grad_gate.astype(bf16)
    )
    blocks = traded(ring, direct.reshape(INNER, STATE))
    gate_grads = Pieces(ring, grad_gate)
    gate_grads.send()
    gate_grads.near()

    def weight_grad(rows_all, columns_all):
        return sum(
            jnp.einsum(
                "ti,tj->ij", rows_all[key], columns_all[key], preferred_element_type=f32
            )
            for key in where
        )

    mixed_all = {key: clock.now(block) for key, block in mixed_all.items()}
    total_w_out = Total(ring, weight_grad(mixed_all, grad_out_all))
    total_w_out.step()
    (blocks,) = clock.tick(blocks)
    chain_grad = returned(ring, carried(ring, blocks, factor, True))
    total_w_out.step()
    total_w_gate = Total(ring, weight_grad(gate_grads.whole(), normed_all))
    chain_grad, total_w_gate.value = clock.tick(chain_grad, total_w_gate.value)
    total_w_out.step()
    total_w_gate.step()

    grad_x, grad_b, grad_c, grad_step, grad_cum, grad_skip = slot_back(
        heads_x,
        proj_b,
        proj_c,
        step_size,
        log_decay,
        incoming,
        grad_y,
        grad_reach,
        chain_grad,
        skip_gain,
    )
    (grad_x,) = clock.tick(grad_x)
    total_w_out.step()
    total_w_gate.step()
    grad_dt_raw, grad_step_bias, grad_rate = pull_steps((grad_step, grad_cum))
    grad_conv_out = jnp.concatenate([grad_x.reshape(row_count, INNER), grad_b, grad_c], axis=1)
    grad_window, grad_taps, grad_shift = pull_conv(grad_conv_out)
    back_edge = ring.next_block(grad_window[: CONV - 1], -1)
    grad_conv_in = grad_window[CONV - 1 :] + jnp.concatenate(
        [jnp.zeros((row_count - CONV + 1, CHANNELS), f32), back_edge], axis=0
    )
    grad_tail = jnp.concatenate([grad_conv_in, grad_dt_raw], axis=1).astype(bf16)
    (grad_tail,) = clock.tick(grad_tail)

    cut = 1792
    first = Pieces(ring, grad_tail[:, :cut])
    last = Pieces(ring, jnp.pad(grad_tail[:, cut:], ((0, 0), (0, 80))))
    first.send()
    first.near()
    last.near()
    total_w_out.step()
    total_w_gate.step()
    clock.tick()
    last.send()
    total_first = Total(ring, weight_grad(first.whole(), normed_all))
    total_first.step()
    total_w_gate.step()
    clock.tick()
    total_last = Total(ring, weight_grad(last.whole(), normed_all))
    total_last.step()
    total_first.step()
    (grad_gate, grad_tail, mixed) = clock.tick(grad_gate, grad_tail, mixed)
    total_first.step()
    total_w_out.step()
    total_w_gate.step()
    summed_out = tokens
    for key, weight in weight_out.items():
        columns = lax.dynamic_slice_in_dim(mixed, where[key] * wide, wide, axis=1)
        summed_out = summed_out + jnp.dot(columns, weight, preferred_element_type=f32)
    output = summed_out.astype(bf16)

    grad_normed = jnp.zeros((row_count, model_width), f32)
    for key in where:
        term = jnp.einsum(
            "tj,jd->td", grad_gate, weight_gate[key], preferred_element_type=f32
        ) + jnp.einsum("tj,jd->td", grad_tail, weight_conv[key], preferred_element_type=f32)
        grad_normed = lax.dynamic_update_slice_in_dim(grad_normed, term, where[key] * depth, axis=1)
    grad_tokens, grad_g_norm = pull_norm(grad_normed)
    hidden_grad = (grad_tokens + grad_out.astype(f32)).astype(bf16)

    parts = [grad_g_norm, grad_taps, grad_shift, grad_step_bias, grad_rate, grad_skip, grad_g_gate]
    small_total = SmallSum(ring, pack(parts))
    clock.tick()
    total_last.step()
    total_first.step()
    total_w_gate.halves()
    small_total.step()
    clock.tick()
    total_last.step()
    total_first.step()
    small_total.step()
    clock.tick()
    total_last.step()
    total_first.halves()
    small_total.step()
    clock.tick()
    total_last.step()
    small_total.step()
    clock.tick()
    total_last.halves()
    small_total.step()
    summed = small_total.finish().reshape(-1)
    shares, at = [], 0
    for part in parts:
        piece = summed[at : at + part.size].reshape(part.shape)
        at += part.size
        width = part.shape[-1] // ring.fsdp
        shares.append(
            lax.dynamic_slice_in_dim(piece, fsdp_index * width, width, axis=part.ndim - 1)
        )
    total_w_in = jnp.zeros((PROJ, depth), f32)
    total_w_in = place_rows(total_w_in, total_w_gate.halves(), 0, INNER)
    total_w_in = place_rows(total_w_in, total_first.halves(), INNER, cut)
    total_w_in = place_rows(total_w_in, total_last.halves(), INNER + cut, PROJ - INNER - cut)
    total_w_in = total_w_in.T
    total_w_out = total_w_out.finish()
    return (
        output[None],
        hidden_grad[None],
        shares[0],
        total_w_in,
        shares[1],
        shares[2],
        shares[3],
        shares[4],
        shares[5],
        shares[6],
        total_w_out,
    )


def solution(mesh):
    placed = (
        P("fsdp", "seq", None),
        P("fsdp"),
        P("fsdp"),
        P("fsdp", None),
        P(None, "fsdp"),
        P("fsdp"),
        P("fsdp"),
        P("fsdp"),
        P("fsdp"),
        P("fsdp"),
        P("fsdp", None),
        P("fsdp", "seq", None),
    )
    return jax.shard_map(
        local,
        mesh=mesh,
        in_specs=placed,
        out_specs=(
            P("fsdp", "seq", None),
            P("fsdp", "seq", None),
            P("fsdp"),
            P("fsdp", None),
            P(None, "fsdp"),
            P("fsdp"),
            P("fsdp"),
            P("fsdp"),
            P("fsdp"),
            P("fsdp"),
            P("fsdp", None),
        ),
        check_vma=False,
    )
```

```python
import functools

import jax
import jax.numpy as jnp
from jax import lax
from jax.experimental import pallas as pl
from jax.experimental.pallas import tpu as pltpu
from jax.sharding import PartitionSpec as P

HEADS = 48
HEADDIM = 64
STATE = 128
CONV = 4
INNER = 3072
CHANNELS = 3328
PROJ = 6448
PLANES = 2
CORES = 2

f32 = jnp.float32
bf16 = jnp.bfloat16
epsilon = 1e-05
no_cost = pl.CostEstimate(flops=0, bytes_accessed=0, transcendentals=0)


class Ring:
    def __init__(self, seq, fsdp):
        self.seq, self.fsdp = seq, fsdp
        self.clock = None
        self.line, self.row = seq // PLANES, fsdp // CORES

    def send(self, block, move):
        route = []
        for s in range(self.seq):
            for f in range(self.fsdp):
                there = move(s // PLANES, s % PLANES, f // CORES, f % CORES)
                if there is None:
                    continue
                z, x, y, c = there
                route.append((s * self.fsdp + f, (z * PLANES + x) * self.fsdp + y * CORES + c))
        arrived = lax.ppermute(block, ("seq", "fsdp"), route)
        self.clock.sent(arrived)
        return arrived

    def core(self, block):
        return self.send(block, lambda z, x, y, c: (z, x, y, 1 - c))

    def plane(self, block):
        return self.send(block, lambda z, x, y, c: (z, 1 - x, y, c))

    def from_row(self, block, distance):
        return self.send(block, lambda z, x, y, c: (z, x, (y - distance) % self.row, c))

    def far(self, block, distance):
        return self.send(block, lambda z, x, y, c: (z ^ distance, x, y, c))

    def relative(self, block, d, e):
        if not d and not e:
            return block
        return self.send(
            block, lambda z, x, y, c: (z, x, (y - d) % self.row, (c + e) % CORES)
        )

    def relative_back(self, block, d, e):
        return self.relative(block, d, e)

    def next_block(self, block, distance):
        def move(z, x, y, c):
            s = z * PLANES + x + distance
            return (s // PLANES, s % PLANES, y, c) if 0 <= s < self.seq else None

        return self.send(block, move)


def rows_of(block, index, count):
    return lax.dynamic_slice_in_dim(block, index * count, count, axis=0)


def swapped(ring, distance):
    seq_index = lax.axis_index("seq")
    if distance == 0:
        return seq_index % PLANES, ring.plane
    bit = (seq_index // PLANES // distance) % 2
    return bit, lambda block: ring.far(block, distance)


def cube(ring):
    distances, distance = [0], 1
    while distance < ring.line:
        distances.append(distance)
        distance *= 2
    return distances


def halve(ring, distance, block):
    bit, send = swapped(ring, distance)
    half = block.shape[0] // 2
    arrived = send(rows_of(block, 1 - bit, half).astype(bf16))
    return rows_of(block, bit, half) + arrived.astype(f32)


def double(ring, distance, block):
    bit, send = swapped(ring, distance)
    other = send(block)
    low = jnp.where(bit == 0, block, other)
    high = jnp.where(bit == 0, other, block)
    return jnp.concatenate([low, high], axis=0)


class Total:
    def __init__(self, ring, grad):
        self.ring, self.value = ring, grad
        self.steps = [(halve, d) for d in cube(ring)] + [(double, d) for d in reversed(cube(ring))]

    def step(self):
        if self.steps:
            kind, distance = self.steps.pop(0)
            if kind is double and self.value.dtype != bf16:
                self.value = self.value.astype(bf16)
            self.value = kind(self.ring, distance, self.ring.clock.now(self.value))

    def finish(self):
        while self.steps:
            self.step()
        return self.value.astype(f32)

    def halves(self):
        while len(self.steps) > 1:
            self.step()
        if self.steps:
            self.steps = []
            self.value = (self.value, self.ring.plane(self.ring.clock.now(self.value)))
        return self.value


class Clock:
    def __init__(self, value):
        self.token = value
        self.pending = []

    def sent(self, value):
        self.pending.append([1, value])

    def tick(self, *values):
        due = [value for ticks, value in self.pending if ticks == 1]
        out = lax.optimization_barrier((self.token,) + values + tuple(due))
        self.token = out[0]
        self.pending = [[ticks - 1, value] for ticks, value in self.pending if ticks > 1]
        return out[1 : 1 + len(values)]

    def defer(self, count=1, ticks=1):
        for entry in self.pending[len(self.pending) - count :]:
            entry[0] += ticks

    def now(self, value):
        return lax.optimization_barrier((value, self.token))[0]


class Spread:
    def __init__(self, ring, source, origin=0, whole_only=False):
        self.ring, self.source, self.origin, self.whole_only = ring, source, origin, whole_only
        block = self.block = source[origin:]
        self.quarter = -(-block.shape[0] // 64) * 16
        self.cut = -(-self.quarter // 32) * 16
        seq_index = lax.axis_index("seq")
        self.place = seq_index % 2 + 2 * ((seq_index // PLANES) % 2)
        self.arrived = []

    def start(self, index):
        return jnp.minimum((self.place ^ index) * self.quarter, self.block.shape[0] - self.quarter)

    def put(self, pieces):
        sides = (pieces,)
        if not self.whole_only:
            sides += ([self.ring.core(piece) for piece in pieces],)
        self.arrived.append(sides)

    def near(self):
        self.beside_it = self.ring.core(self.ring.clock.now(self.block))

    def first(self, at_once=False):
        ring = self.ring
        mine = lax.dynamic_slice_in_dim(self.source, self.origin + self.start(0), self.quarter, axis=0)
        mine = mine if at_once else ring.clock.now(mine)
        self.mine = [ring.from_row(mine, d) for d in range(1, ring.row)]

    def second(self):
        ring = self.ring
        mine = [ring.clock.now(part) for part in self.mine]
        self.beside = [ring.plane(part) for part in mine]
        self.behind = [ring.far(part, 1) for part in mine]
        self.put(mine)

    def third(self):
        ring, cut = self.ring, self.cut
        beside = [ring.clock.now(part) for part in self.beside]
        behind = [ring.clock.now(part) for part in self.behind]
        self.corner = (
            [ring.plane(part[:cut]) for part in behind],
            [ring.far(part[cut:], 1) for part in beside],
        )
        self.put(beside)
        self.put(behind)

    def fourth(self):
        now = self.ring.clock.now
        self.put([now(part) for part in self.corner[0]])
        self.put([now(part) for part in self.corner[1]])

    def whole(self):
        found = {(0, 0): self.block, (0, 1): self.beside_it}
        index = jnp.stack([self.place ^ k for k in range(4)]).astype(jnp.int32)
        for d in range(1, self.ring.row):
            sides = [[side[d - 1] for side in pieces] for pieces in zip(*self.arrived)]
            shards = laid(self.block, self.quarter, self.cut, index, sides)
            found[d, 0] = shards[0]
            found[d, 1] = self.ring.core(shards[0]) if self.whole_only else shards[1]
        return found


def sum_body(count, *refs):
    out_ref = refs[-1]
    total = None
    for left, right in zip(refs[:count], refs[count:-1]):
        term = lax.dot_general(
            left[...], right[...], (((0,), (0,)), ((), ())), preferred_element_type=f32
        )
        total = term if total is None else total + term
    out_ref[...] = total


def weight_grad(rows_all, columns_all, tile):
    keys = list(rows_all)
    tokens, rows = rows_all[keys[0]].shape
    width = columns_all[keys[0]].shape[1]
    return pl.pallas_call(
        functools.partial(sum_body, len(keys)),
        grid=(rows // tile,),
        in_specs=[pl.BlockSpec((tokens, tile), lambda i: (0, i))] * len(keys)
        + [pl.BlockSpec((tokens, width), lambda i: (0, 0))] * len(keys),
        out_specs=pl.BlockSpec((tile, width), lambda i: (i, 0)),
        out_shape=jax.ShapeDtypeStruct((rows, width), f32),
        name="weight_grad",
        cost_estimate=no_cost,
        compiler_params=pltpu.CompilerParams(vmem_limit_bytes=40 * 2**20),
    )(*[rows_all[key] for key in keys], *[columns_all[key] for key in keys])


def to_inner_body(tiles, place_ref, grad_ref, *refs):
    out_ref = refs[-1]
    shard = pl.program_id(0) // tiles
    for k, weight in enumerate(refs[:-1]):

        @pl.when(shard == k)
        def _(weight=weight):
            out_ref[...] = dot_last(grad_ref[...], weight[...])


def to_inner(grad, weights, places):
    tokens, width = grad.shape
    rows = weights[0].shape[0]
    tile = 384
    tiles = rows // tile
    return pl.pallas_call(
        functools.partial(to_inner_body, tiles),
        grid_spec=pltpu.PrefetchScalarGridSpec(
            num_scalar_prefetch=1,
            grid=(len(weights) * tiles,),
            in_specs=[pl.BlockSpec((tokens, width), lambda i, place: (0, 0))]
            + [
                pl.BlockSpec(
                    (tile, width), lambda i, place, k=k: (jnp.clip(i - k * tiles, 0, tiles - 1), 0)
                )
                for k in range(len(weights))
            ],
            out_specs=pl.BlockSpec(
                (tokens, tile), lambda i, place: (0, place[i // tiles] * tiles + i % tiles)
            ),
        ),
        out_shape=jax.ShapeDtypeStruct((tokens, rows * len(weights)), f32),
        name="to_inner",
        cost_estimate=no_cost,
        compiler_params=pltpu.CompilerParams(vmem_limit_bytes=40 * 2**20),
    )(places, grad, *weights)


def to_model_body(layout, gate_ref, tail_ref, *refs):
    out_ref = refs[-1]
    at = 0
    for k, (blocks, rows) in enumerate(layout):
        total = jnp.dot(tail_ref[...], refs[at][...], preferred_element_type=f32)
        at += 1
        for piece, block in enumerate(blocks):
            columns = gate_ref[:, piece * rows : (piece + 1) * rows]
            weight = refs[at][block * rows : (block + 1) * rows]
            at += 1
            total = total + jnp.dot(columns, weight, preferred_element_type=f32)
        out_ref[k] = total


def to_model(grad_gate, grad_tail, gate_weights, tail_weights):
    rows = grad_gate.shape[1] // len(gate_weights[0])
    flat, layout = [], []
    for pieces, tail in zip(gate_weights, tail_weights):
        if all(array is pieces[0][0] for array, _ in pieces):
            layout.append(([0], grad_gate.shape[1]))
            flat += [tail, pieces[0][0]]
        else:
            layout.append(([block for _, block in pieces], rows))
            flat += [tail] + [array for array, _ in pieces]
    inside = pl.BlockSpec(memory_space=pltpu.VMEM)
    return pl.pallas_call(
        functools.partial(to_model_body, layout),
        in_specs=[inside] * (2 + len(flat)),
        out_specs=inside,
        out_shape=jax.ShapeDtypeStruct(
            (len(layout), grad_gate.shape[0], tail_weights[0].shape[1]), f32
        ),
        name="to_model",
        cost_estimate=no_cost,
        compiler_params=pltpu.CompilerParams(vmem_limit_bytes=48 * 2**20),
    )(grad_gate, grad_tail, *flat)


def output_body(count, token_ref, *refs):
    out_ref = refs[-1]
    total = token_ref[...].astype(f32)
    for columns, weight in zip(refs[:count], refs[count:-1]):
        total = total + jnp.dot(columns[...], weight[...], preferred_element_type=f32)
    out_ref[...] = total.astype(bf16)


def output_rows(tokens, columns, weights):
    inside = pl.BlockSpec(memory_space=pltpu.VMEM)
    return pl.pallas_call(
        functools.partial(output_body, len(columns)),
        in_specs=[inside] * (1 + 2 * len(columns)),
        out_specs=inside,
        out_shape=jax.ShapeDtypeStruct(tokens.shape, bf16),
        name="output_rows",
        cost_estimate=no_cost,
        compiler_params=pltpu.CompilerParams(vmem_limit_bytes=48 * 2**20),
    )(tokens, *columns, *weights)


def laid_body(quarter, cut, index_ref, *refs):
    count = len(refs) // 6
    pieces, shards = refs[:-count], refs[-count:]
    for e, shard in enumerate(shards):
        own = pieces[e * 5 : e * 5 + 5]
        for piece, quarter_of, offset in zip(own, (0, 1, 2, 3, 3), (0, 0, 0, 0, cut)):
            start = jnp.minimum(index_ref[quarter_of] * quarter, shard.shape[0] - quarter)
            start = pl.multiple_of(start + offset, 16)
            shard[pl.ds(start, piece.shape[0]), :] = piece[...]


def laid(block, quarter, cut, index, sides):
    flat = [piece for side in sides for piece in side]
    inside = pl.BlockSpec(memory_space=pltpu.VMEM)
    return pl.pallas_call(
        functools.partial(laid_body, quarter, cut),
        grid_spec=pltpu.PrefetchScalarGridSpec(
            num_scalar_prefetch=1,
            grid=(),
            in_specs=[inside] * len(flat),
            out_specs=[inside] * len(sides),
        ),
        out_shape=[jax.ShapeDtypeStruct(block.shape, block.dtype)] * len(sides),
        name="laid",
        cost_estimate=no_cost,
        compiler_params=pltpu.CompilerParams(vmem_limit_bytes=40 * 2**20),
    )(index, *flat)


def project_body(count, *refs):
    out_ref = refs[-1]
    total = None
    for columns, weight in zip(refs[:count], refs[count:-1]):
        term = lax.dot_general(
            columns[...], weight[...], (((1,), (1,)), ((), ())), preferred_element_type=f32
        )
        total = term if total is None else total + term
    out_ref[...] = total.astype(out_ref.dtype)


def project(columns, weights, tile, width=None):
    count = len(columns)
    tokens, depth = columns[0].shape
    at = [0] * count
    if width is not None:
        at = [block for _, block in weights]
        weights = [array for array, _ in weights]
    else:
        width = weights[0].shape[0]
    return pl.pallas_call(
        functools.partial(project_body, count),
        grid=(pl.cdiv(width, tile),),
        in_specs=[pl.BlockSpec((tokens, depth), lambda i: (0, 0))] * count
        + [pl.BlockSpec((tile, depth), lambda i, k=k: (i + k, 0)) for k in at],
        out_specs=pl.BlockSpec((tokens, tile), lambda i: (0, i)),
        out_shape=jax.ShapeDtypeStruct((tokens, width), bf16),
        name="project",
        cost_estimate=no_cost,
        compiler_params=pltpu.CompilerParams(vmem_limit_bytes=40 * 2**20),
    )(*columns, *weights)


class Pieces:
    def __init__(self, ring, block, count=1):
        self.ring, self.block = ring, block
        self.rows = block.shape[0] // count
        self.parts = []

    def near(self):
        self.beside = self.ring.core(self.ring.clock.now(self.block))

    def send(self, later=0):
        clock = self.ring.clock
        at = len(self.parts) * self.rows
        piece = clock.now(self.block[at : at + self.rows])
        self.parts.append([self.ring.from_row(piece, d) for d in range(1, self.ring.row)])
        clock.defer(self.ring.row - 1, later)

    def pass_on(self, at):
        far = [self.ring.clock.now(piece) for piece in self.parts[at]]
        self.parts[at] = [(piece, self.ring.core(piece)) for piece in far]

    def pieces(self):
        count = len(self.parts)
        found = {
            (0, 0): [(self.block, at) for at in range(count)],
            (0, 1): [(self.beside, at) for at in range(count)],
        }
        for d in range(1, self.ring.row):
            for e in range(CORES):
                found[d, e] = [(part[d - 1][e], 0) for part in self.parts]
        return found

    def whole(self):
        found = {(0, 0): self.block, (0, 1): self.beside}
        for d in range(1, self.ring.row):
            found[d, 0] = self.ring.clock.now(self.parts[0][d - 1])
            found[d, 1] = self.ring.core(found[d, 0])
        return found


def gather_rows(ring, block):
    found = {}
    for d in range(ring.row):
        found[d, 0] = block if d == 0 else ring.from_row(block, d)
        found[d, 1] = ring.core(found[d, 0])
    return found


def places(ring):
    index = lax.axis_index("fsdp")
    y, c = index // CORES, index % CORES
    return {
        (d, e): ((y + d) % ring.row) * CORES + (c + e) % CORES
        for d in range(ring.row)
        for e in range(CORES)
    }


def columns_for(ring, block):
    index = lax.axis_index("fsdp")
    y, c = index // CORES, index % CORES
    width = block.shape[1] // ring.fsdp
    return {
        (d, e): lax.dynamic_slice_in_dim(
            block, (((y - d) % ring.row) * CORES + (c + e) % CORES) * width, width, axis=1
        )
        for d in range(ring.row)
        for e in range(CORES)
    }


def trade_columns(ring, pieces):
    return {key: ring.relative_back(piece, *key) for key, piece in pieces.items()}


class SmallSum:
    def __init__(self, ring, vector):
        self.ring, self.value = ring, vector
        self.steps = ["core", "row"] + cube(ring)

    def step(self):
        if not self.steps:
            return
        kind = self.steps.pop(0)
        vector = self.ring.clock.now(self.value)
        if kind == "core":
            self.value = vector + self.ring.core(vector)
        elif kind == "row":
            self.value = sum([self.ring.from_row(vector, d) for d in range(1, self.ring.row)], vector)
        else:
            self.value = vector + swapped(self.ring, kind)[1](vector)

    def finish(self):
        while self.steps:
            self.step()
        return self.value


def head_rows(ring):
    part = INNER // ring.seq
    run = HEADDIM
    while part % run:
        run //= 2
    return part, run


def spread_factors(ring, through):
    part, run = head_rows(ring)
    factor = jnp.repeat(through, HEADDIM // run).reshape(ring.seq, part // run)
    factor = jnp.pad(factor, ((0, 0), (0, 8 - part // run)))
    return jnp.broadcast_to(factor[:, :, None], (ring.seq, 8, STATE))


def carried_body(reverse, run, blocks_ref, factor_ref, out_ref):
    count, part = out_ref.shape[0], out_ref.shape[1]
    state = jnp.zeros((part, STATE), f32)
    for k in reversed(range(count)) if reverse else range(count):
        out_ref[k] = state.astype(bf16)
        factor = factor_ref[k]
        spread = [jnp.broadcast_to(factor[j : j + 1], (run, STATE)) for j in range(part // run)]
        state = jnp.concatenate(spread, axis=0) * state + blocks_ref[k, :part]


def carried(ring, blocks, factor, reverse):
    part, run = head_rows(ring)
    return pl.pallas_call(
        functools.partial(carried_body, reverse, run),
        out_shape=jax.ShapeDtypeStruct((ring.seq, part, STATE), bf16),
        name="carried",
        cost_estimate=no_cost,
    )(blocks, factor)


def returned(ring, states):
    states = lax.all_to_all(states, "seq", 0, 0, tiled=True)
    return states.reshape(HEADS, HEADDIM, STATE)


def place_rows(whole, sides, start, rows):
    mine, other = sides
    first = (lax.axis_index("seq") % PLANES) == 0
    half = mine.shape[0]
    low = jnp.where(first, mine, other).astype(f32)
    high = jnp.where(first, other, mine)[: rows - half].astype(f32)
    whole = lax.dynamic_update_slice_in_dim(whole, low, start, axis=0)
    return lax.dynamic_update_slice_in_dim(whole, high, start + half, axis=0)


def steps_body(dt_ref, bias_ref, rate_ref, cum_ref, weigh_ref, decay_ref, cum_rows, step_rows, through_ref):
    raw = dt_ref[...].astype(f32) + bias_ref[...]
    step = jnp.maximum(raw, 0.0) + jnp.log1p(jnp.exp(-jnp.abs(raw)))
    tokens = step.shape[0]
    row = lax.broadcasted_iota(jnp.int32, step.shape, 0)
    cum = step * -jnp.exp(rate_ref[...])
    distance = 1
    while distance < tokens:
        cum = cum + jnp.where(row >= distance, pltpu.roll(cum, distance, 0), 0.0)
        distance *= 2
    end = cum[tokens - 1 :]
    cum_ref[...] = cum
    weigh_ref[...] = jnp.exp(end - cum) * step
    decay_ref[...] = jnp.exp(cum)
    cum_rows[...] = cum.T[:HEADS]
    step_rows[...] = step.T[:HEADS]
    through_ref[...] = jnp.exp(end)


def steps(projected, bias, rate):
    tokens = projected.shape[0]
    row = pl.BlockSpec((1, STATE), lambda i: (0, 0))
    by_token = pl.BlockSpec((tokens, STATE), lambda i: (0, 0))
    by_head = pl.BlockSpec((HEADS, tokens), lambda i: (0, 0))
    pad = lambda v: jnp.pad(v, (0, STATE - HEADS))[None]
    return pl.pallas_call(
        steps_body,
        grid=(1,),
        in_specs=[pl.BlockSpec((tokens, STATE), lambda i: (0, CHANNELS // STATE)), row, row],
        out_specs=[by_token] * 3 + [by_head] * 2 + [row],
        out_shape=[jax.ShapeDtypeStruct((tokens, STATE), f32)] * 3
        + [jax.ShapeDtypeStruct((HEADS, tokens), f32)] * 2
        + [jax.ShapeDtypeStruct((1, STATE), f32)],
        name="steps",
        cost_estimate=no_cost,
    )(projected, pad(bias), pad(rate))


def steps_back_body(
    dt_ref, bias_ref, rate_ref, step_ref, cum_ref, grad_step_ref, grad_cum_ref, factor_ref, crossed_ref,
    grad_ref, bias_grad_ref, rate_grad_ref,
):
    step, cum, factor = step_ref[...], cum_ref[...], factor_ref[...]
    tokens = step.shape[1]
    lane = lax.broadcasted_iota(jnp.int32, step.shape, 1)
    end = cum[:, tokens - 1 :]
    to_end = jnp.exp(end - cum)
    tail = factor * step * to_end
    grad_end = jnp.sum(tail, axis=1, keepdims=True) + jnp.exp(end) * jnp.sum(
        crossed_ref[...], axis=1, keepdims=True
    )
    total = grad_cum_ref[...] - tail + jnp.where(lane == tokens - 1, grad_end, 0.0)
    distance = 1
    while distance < tokens:
        moved = pltpu.roll(total, tokens - distance, 1)
        total = total + jnp.where(lane < tokens - distance, moved, 0.0)
        distance *= 2
    rate = -jnp.exp(rate_ref[...])
    rate_grad_ref[...] = rate * jnp.sum(total * step, axis=1, keepdims=True)
    raw = dt_ref[...].astype(f32).T[:HEADS] + bias_ref[...]
    grad = (grad_step_ref[...] + factor * to_end + total * rate) * jax.nn.sigmoid(raw)
    bias_grad_ref[...] = jnp.sum(grad, axis=1, keepdims=True)
    none = jnp.zeros((STATE - HEADS, tokens), f32)
    grad_ref[...] = jnp.concatenate([grad, none], axis=0).T.astype(bf16)


def steps_back(projected, bias, rate, step_rows, cum_rows, grad_step, grad_cum, factor, crossed):
    tokens = projected.shape[0]
    column = pl.BlockSpec((HEADS, 1), lambda i: (0, 0))
    by_head = pl.BlockSpec((HEADS, tokens), lambda i: (0, 0))
    return pl.pallas_call(
        steps_back_body,
        grid=(1,),
        in_specs=[pl.BlockSpec((tokens, STATE), lambda i: (0, CHANNELS // STATE)), column, column]
        + [by_head] * 5
        + [pl.BlockSpec((HEADS, STATE), lambda i: (0, 0))],
        out_specs=[pl.BlockSpec((tokens, STATE), lambda i: (0, 0)), column, column],
        out_shape=[
            jax.ShapeDtypeStruct((tokens, STATE), bf16),
            jax.ShapeDtypeStruct((HEADS, 1), f32),
            jax.ShapeDtypeStruct((HEADS, 1), f32),
        ],
        name="steps_back",
        cost_estimate=no_cost,
    )(
        projected, bias[:, None], rate[:, None], step_rows, cum_rows, grad_step, grad_cum, factor,
        crossed,
    )


def group_columns(wide_ref, group, heads):
    shift = lax.rem(STATE - heads * group, STATE)
    return pltpu.roll(wide_ref[...], shift, 1)[:, :heads]


def keep_columns(wide_ref, at, columns):
    wide = wide_ref[...]
    lane = lax.broadcasted_iota(jnp.int32, wide.shape, 1)
    for k, column in enumerate(columns):
        wide = jnp.where(lane == at + k, column, wide)
    wide_ref[...] = wide


def along(column_pair):
    lane = lax.broadcasted_iota(jnp.int32, (column_pair.shape[0], 2 * HEADDIM), 1)
    return jnp.where(lane < HEADDIM, column_pair[:, :1], column_pair[:, 1:2])


def conv_sum(edge, rows, taps, shift):
    window = jnp.concatenate([edge, rows], axis=0)
    total = shift
    for k in range(CONV):
        moved = window if k == CONV - 1 else pltpu.roll(window, CONV - 1 - k, 0)
        total = total + taps[k : k + 1] * moved[8:]
    return total


def enter_body(part, proj_ref, edge_ref, taps_ref, shift_ref, weigh_ref, factor_ref, low_ref, fresh_ref):
    def conv(at, width):
        columns = slice(at, at + width)
        total = conv_sum(
            edge_ref[:, columns].astype(f32),
            proj_ref[:, columns].astype(f32),
            taps_ref[:, columns],
            shift_ref[:, columns],
        )
        low = (total * jax.nn.sigmoid(total)).astype(bf16)
        low_ref[:, columns] = low
        return low

    proj_b = conv(INNER, 2 * STATE)[:, :STATE]
    fresh_ref[:, part:] = factor_ref[...]
    for at in range(0, INNER, 2 * HEADDIM):
        low = conv(at, 2 * HEADDIM)
        head = at // HEADDIM
        weighted = (low.astype(f32) * along(weigh_ref[:, head : head + 2])).astype(bf16)
        fresh = lax.dot_general(
            weighted, proj_b, (((0,), (0,)), ((), ())), preferred_element_type=f32
        )
        row = at
        while row < at + 2 * HEADDIM:
            device, offset = row // part, row % part
            count = min(part - offset, at + 2 * HEADDIM - row)
            fresh_ref[device, offset : offset + count] = fresh[row - at : row - at + count]
            row += count


def enter(ring, projected, edge, taps, shift, weigh, factor):
    part, _ = head_rows(ring)
    return pl.pallas_call(
        functools.partial(enter_body, part),
        out_shape=[
            jax.ShapeDtypeStruct((projected.shape[0], CHANNELS), bf16),
            jax.ShapeDtypeStruct((ring.seq, part + 8, STATE), f32),
        ],
        name="enter",
        cost_estimate=no_cost,
        compiler_params=pltpu.CompilerParams(vmem_limit_bytes=40 * 2**20),
    )(projected, edge, taps, shift[None], weigh, factor)


def pairs_along(columns):
    return jnp.concatenate(
        [along(columns[:, i : i + 2]) for i in range(0, columns.shape[1], 2)], axis=1
    )


def turn_body(
    base_ref, incoming_ref, c_ref, decay_ref, grad_ref, gain_ref, *refs,
):
    count = len(refs) - 10
    gate_refs = refs[:count]
    (
    mixed_ref, grad_y_ref, grad_gate_ref, grad_reach_ref, direct_ref, gain_grad_ref,
    mixer, grads, squares, products,
    ) = refs[count:]
    later, j = pl.program_id(0), pl.program_id(1)
    gate = gate_refs[0][...]
    for k in range(1, count):
        gate = jnp.where(j * count >= k * pl.num_programs(1), gate_refs[k][...], gate)
    gate = gate.astype(f32)
    sig = jax.nn.sigmoid(gate)
    silu = gate * sig
    gain = gain_ref[...]

    @pl.when((later == 0) & (j == 0))
    def _():
        squares[...] = jnp.zeros_like(squares)
        products[...] = jnp.zeros_like(products)

    @pl.when(later == 0)
    def _():
        reached = lax.dot_general(
            c_ref[...], incoming_ref[...], (((1,), (1,)), ((), ())), preferred_element_type=f32
        )
        ssd = base_ref[...] + pairs_along(group_columns(decay_ref, j, gain.shape[1] // HEADDIM)) * reached
        gated = ssd * silu
        mixer[j] = ssd
        grads[j] = grad_ref[...]
        squares[...] += jnp.sum(gated * gated, axis=1, keepdims=True)
        products[...] += jnp.sum(gated * grad_ref[...] * gain, axis=1, keepdims=True)

    @pl.when(later == 1)
    def _():
        scale = lax.rsqrt(squares[...] / INNER + epsilon)
        ssd = mixer[j]
        grad = grads[j]
        normal = ssd * silu * scale
        mixed_ref[...] = (normal * gain).astype(bf16)
        gain_grad_ref[...] = jnp.sum(grad * normal, axis=0, keepdims=True)
        grad_gated = scale * (grad * gain - normal * (scale * products[...] / INNER))
        grad_y = (grad_gated * silu).astype(bf16)
        grad_y_ref[...] = grad_y
        grad_gate_ref[...] = (grad_gated * ssd * (sig + silu * (1.0 - sig))).astype(bf16)
        grad_reach = (grad_y.astype(f32) * pairs_along(group_columns(decay_ref, j, gain.shape[1] // HEADDIM))).astype(bf16)
        grad_reach_ref[...] = grad_reach
        direct_ref[...] = lax.dot_general(
            grad_reach, c_ref[...], (((0,), (0,)), ((), ())), preferred_element_type=f32
        )


def later_or_same(tokens):
    t = lax.broadcasted_iota(jnp.int32, (tokens, tokens), 0)
    return t >= lax.broadcasted_iota(jnp.int32, (tokens, tokens), 1)


def dot_last(a, b):
    return lax.dot_general(a, b, (((1,), (1,)), ((), ())), preferred_element_type=f32)


def dot_first(a, b):
    return lax.dot_general(a, b, (((0,), (0,)), ((), ())), preferred_element_type=f32)


def inside_body(x_ref, b_ref, c_ref, cum_ref, cum_rows_ref, step_rows_ref, skip_ref, out_ref, scores):
    tokens = x_ref.shape[0]

    @pl.when(pl.program_id(0) == 0)
    def _():
        table = dot_last(c_ref[...], b_ref[...])
        scores[...] = jnp.where(later_or_same(tokens), table, 0.0)

    x = x_ref[...]
    j = pl.program_id(0)
    same = later_or_same(tokens)
    cum = group_columns(cum_ref, j, 2)
    parts = []
    for head in range(2):
        row = pl.ds(2 * j + head, 1)
        exponent = cum[:, head : head + 1] - cum_rows_ref[row, :]
        decay = jnp.exp(jnp.where(same, exponent, 0.0))
        mixing = (scores[...] * decay * step_rows_ref[row, :]).astype(bf16)
        parts.append(jnp.dot(mixing, x, preferred_element_type=f32))
    first = lax.broadcasted_iota(jnp.int32, x.shape, 1) < HEADDIM
    out_ref[...] = jnp.where(first, parts[0], parts[1]) + skip_ref[...] * x.astype(f32)


def pair_specs(tokens):
    columns = pl.BlockSpec((tokens, 2 * HEADDIM), lambda j: (0, j))
    by_token = pl.BlockSpec((tokens, STATE), lambda j: (0, 0))
    by_head = pl.BlockSpec((HEADS, tokens), lambda j: (0, 0))
    row = pl.BlockSpec((1, 2 * HEADDIM), lambda j: (0, j))
    proj_b = pl.BlockSpec((tokens, STATE), lambda j: (0, INNER // STATE))
    proj_c = pl.BlockSpec((tokens, STATE), lambda j: (0, INNER // STATE + 1))
    return columns, by_token, by_head, row, proj_b, proj_c


def inside(conv_low, cum_pairs, cum_rows, step_rows, skip_row):
    tokens = conv_low.shape[0]
    columns, by_token, by_head, row, proj_b, proj_c = pair_specs(tokens)
    return pl.pallas_call(
        inside_body,
        grid=(HEADS // 2,),
        in_specs=[columns, proj_b, proj_c, by_token, by_head, by_head, row],
        out_specs=columns,
        out_shape=jax.ShapeDtypeStruct((tokens, INNER), f32),
        scratch_shapes=[pltpu.VMEM((tokens, tokens), f32)],
        name="inside",
        cost_estimate=no_cost,
        compiler_params=pltpu.CompilerParams(vmem_limit_bytes=40 * 2**20),
    )(conv_low, conv_low, conv_low, cum_pairs, cum_rows, step_rows, skip_row)


def inside_back_body(
    y_ref, reach_ref, x_ref, b_ref, c_ref, incoming_ref, cum_ref, cum_rows_ref, step_rows_ref, skip_ref,
    x_out, b_out, c_out, step_out, cum_out, skip_out,
    scores, grad_scores, wide_sums,
):
    tokens = x_ref.shape[0]
    j = pl.program_id(0)

    @pl.when(j == 0)
    def _():
        table = dot_last(c_ref[...], b_ref[...])
        scores[...] = jnp.where(later_or_same(tokens), table, 0.0)
        grad_scores[...] = jnp.zeros_like(grad_scores)
        c_out[...] = jnp.zeros_like(c_out)

    x, y = x_ref[...], y_ref[...]
    wide = y.astype(f32)
    incoming = incoming_ref[...]
    reached = wide * dot_last(c_ref[...], incoming)
    c_out[...] += jnp.dot(reach_ref[...], incoming, preferred_element_type=f32)
    skip_out[...] = jnp.sum(wide * x.astype(f32), axis=0, keepdims=True)
    same = later_or_same(tokens)
    first = lax.broadcasted_iota(jnp.int32, x.shape, 1) < HEADDIM
    parts, total, sums = [], 0.0, []
    wide_cum = group_columns(cum_ref, j, 2)
    for head in range(2):
        cum = wide_cum[:, head : head + 1]
        row = pl.ds(2 * j + head, 1)
        step = step_rows_ref[row, :]
        decay = jnp.exp(jnp.where(same, cum - cum_rows_ref[row, :], 0.0))
        both = scores[...] * decay
        own = jnp.where(first == (head == 0), y, jnp.zeros_like(y))
        grad_mix = dot_last(own, x)
        total = total + grad_mix * decay * step
        by_source = grad_mix * both
        step_out[row, :] = jnp.sum(by_source, axis=0, keepdims=True)
        mine = reached[:, head * HEADDIM : (head + 1) * HEADDIM]
        sums.append(
            jnp.sum(by_source * step, axis=1, keepdims=True)
            + jnp.exp(cum) * jnp.sum(mine, axis=1, keepdims=True)
        )
        parts.append(dot_first((both * step).astype(bf16), y))
    keep_columns(wide_sums, 2 * j, sums)
    grad_scores[...] += total
    x_out[...] = jnp.where(first, parts[0], parts[1]) + skip_ref[...] * wide

    @pl.when(j == pl.num_programs(0) - 1)
    def _():
        grad = jnp.where(same, grad_scores[...], 0.0).astype(bf16)
        c_out[...] += jnp.dot(grad, b_ref[...], preferred_element_type=f32)
        b_out[...] = dot_first(grad, c_ref[...])
        cum_out[...] = wide_sums[...].T[:HEADS] - step_out[...] * step_rows_ref[...]


def inside_back(grad_y, grad_reach, conv_low, incoming, cum_pairs, cum_rows, step_rows, skip_row):
    tokens = conv_low.shape[0]
    columns, by_token, by_head, row, proj_b, proj_c = pair_specs(tokens)
    whole = pl.BlockSpec((tokens, STATE), lambda j: (0, 0))
    pairs = HEADS // 2
    return pl.pallas_call(
        inside_back_body,
        grid=(pairs,),
        in_specs=[columns, columns, columns, proj_b, proj_c]
        + [pl.BlockSpec((2 * HEADDIM, STATE), lambda j: (j, 0)), by_token, by_head, by_head, row],
        out_specs=[columns, whole, whole, by_head, by_head, row],
        out_shape=[
            jax.ShapeDtypeStruct((tokens, INNER), f32),
            jax.ShapeDtypeStruct((tokens, STATE), f32),
            jax.ShapeDtypeStruct((tokens, STATE), f32),
            jax.ShapeDtypeStruct((HEADS, tokens), f32),
            jax.ShapeDtypeStruct((HEADS, tokens), f32),
            jax.ShapeDtypeStruct((1, INNER), f32),
        ],
        scratch_shapes=[
            pltpu.VMEM((tokens, tokens), f32),
            pltpu.VMEM((tokens, tokens), f32),
            pltpu.VMEM((tokens, STATE), f32),
        ],
        name="inside_back",
        cost_estimate=no_cost,
        compiler_params=pltpu.CompilerParams(vmem_limit_bytes=40 * 2**20),
    )(
        grad_y, grad_reach, conv_low, conv_low, conv_low, incoming, cum_pairs, cum_rows, step_rows,
        skip_row,
    )


def turn(base, incoming, proj_c, decay, gate_parts, grad_mixed, gain):
    tokens, heads = base.shape[0], 8
    width = heads * HEADDIM
    groups = INNER // width
    share = groups // len(gate_parts)
    once = lambda p, j: (0, jnp.where(p == 0, j, groups - 1))
    last = lambda p, j: (0, jnp.where(p == 0, 0, j))
    wide = jax.ShapeDtypeStruct((tokens, INNER), bf16)
    return pl.pallas_call(
        turn_body,
        grid=(2, groups),
        in_specs=[
            pl.BlockSpec((tokens, width), once),
            pl.BlockSpec((width, STATE), lambda p, j: (jnp.where(p == 0, j, groups - 1), 0)),
            pl.BlockSpec((tokens, STATE), lambda p, j: (0, 0)),
            pl.BlockSpec((tokens, STATE), lambda p, j: (0, 0)),
            pl.BlockSpec((tokens, width), once),
            pl.BlockSpec((1, width), lambda p, j: (0, j)),
        ]
        + [
            pl.BlockSpec(
                (tokens, width), lambda p, j, k=k: (0, jnp.clip(j - k * share, 0, share - 1))
            )
            for k in range(len(gate_parts))
        ],
        out_specs=[pl.BlockSpec((tokens, width), last)] * 4
        + [
            pl.BlockSpec((width, STATE), lambda p, j: (jnp.where(p == 0, 0, j), 0)),
            pl.BlockSpec((1, width), last),
        ],
        out_shape=[wide] * 4
        + [jax.ShapeDtypeStruct((INNER, STATE), f32), jax.ShapeDtypeStruct((1, INNER), f32)],
        scratch_shapes=[
            pltpu.VMEM((groups, tokens, width), f32),
            pltpu.VMEM((groups, tokens, width), f32),
            pltpu.VMEM((tokens, 1), f32),
            pltpu.VMEM((tokens, 1), f32),
        ],
        name="turn",
        cost_estimate=no_cost,
        compiler_params=pltpu.CompilerParams(vmem_limit_bytes=40 * 2**20),
    )(base, incoming, proj_c, decay, grad_mixed, gain[None], *gate_parts)


def ahead(rows, count, distance):
    return (pltpu.roll(rows, rows.shape[0] - distance, 0) if distance else rows)[:count]


def leave_body(
    steps, proj_ref, edge_ref, taps_ref, shift_ref, low_ref, part_ref, fresh_ref, incoming_ref, b_ref,
    weigh_ref, b_part_ref, c_part_ref,
    grad_ref, first_ref, last_ref, taps_grad_ref, shift_grad_ref, factor_ref, crossed_ref,
    b_total, wide_factor,
):
    j = pl.program_id(0)

    def conv_back(grad_out):
        rows = proj_ref[...].astype(f32)
        window = jnp.concatenate([edge_ref[...].astype(f32), rows], axis=0)
        taps = taps_ref[...]
        moved = [
            (pltpu.roll(window, CONV - 1 - k, 0) if k < CONV - 1 else window)[8:]
            for k in range(CONV)
        ]
        total = shift_ref[...]
        for k in range(CONV):
            total = total + taps[k : k + 1] * moved[k]
        sig = jax.nn.sigmoid(total)
        grad = grad_out * (sig * (1.0 + total * (1.0 - sig)))
        shift_grad_ref[...] = jnp.sum(grad, axis=0, keepdims=True)
        taps_grad_ref[...] = jnp.concatenate(
            [jnp.sum(grad * part, axis=0, keepdims=True) for part in moved], axis=0
        )
        none = jnp.zeros((8, grad.shape[1]), f32)
        after_it = jnp.concatenate([grad, none], axis=0)
        before_it = jnp.concatenate([none, grad[:8]], axis=0)
        inner, outer = 0.0, 0.0
        for k in range(CONV):
            tap = taps[k : k + 1]
            inner = inner + tap * ahead(after_it, grad.shape[0], CONV - 1 - k)
            outer = outer + tap * ahead(before_it, 8, CONV - 1 - k)
        grad_ref[...] = inner.astype(bf16)
        last_ref[...] = inner[grad.shape[0] - 8 :]
        first_ref[...] = outer

    @pl.when(j == 0)
    def _():
        b_total[...] = b_part_ref[...]

    @pl.when(j < steps)
    def _():
        fresh = fresh_ref[...]
        x = low_ref[...].astype(f32)
        heads = x.shape[1] // HEADDIM
        weigh = pairs_along(group_columns(weigh_ref, j, heads))
        grad_weighted = lax.dot_general(
            b_ref[...], fresh, (((1,), (1,)), ((), ())), preferred_element_type=f32
        )
        weighted = (x * weigh).astype(bf16)
        b_total[...] += jnp.dot(weighted, fresh, preferred_element_type=f32)
        product = grad_weighted * x
        keep_columns(
            wide_factor,
            heads * j,
            [
                jnp.sum(product[:, i * HEADDIM : (i + 1) * HEADDIM], axis=1, keepdims=True)
                for i in range(heads)
            ],
        )
        both = fresh.astype(f32) * incoming_ref[...].astype(f32)
        for i in range(heads):
            row = pl.ds(heads * j + i, 1)
            crossed_ref[row, :] = jnp.sum(
                both[i * HEADDIM : (i + 1) * HEADDIM], axis=0, keepdims=True
            )
        conv_back(part_ref[...] + grad_weighted * weigh)

    @pl.when(j == steps)
    def _():
        factor_ref[...] = wide_factor[...].T[:HEADS]
        conv_back(jnp.concatenate([b_total[...], c_part_ref[...]], axis=1))


def leave(projected, edge, taps, shift, conv_low, part, grad_fresh, incoming, weigh, b_part, c_part):
    tokens, heads = part.shape[0], 4
    width = heads * HEADDIM
    steps = INNER // width
    inside = lambda j: jnp.minimum(j, steps - 1)
    block = lambda rows: pl.BlockSpec((rows, width), lambda j: (0, j))
    whole = lambda rows: pl.BlockSpec((rows, STATE), lambda j: (0, 0))
    state = pl.BlockSpec((width, STATE), lambda j: (inside(j), 0))
    return pl.pallas_call(
        functools.partial(leave_body, steps),
        grid=(steps + 1,),
        in_specs=[
            block(tokens),
            block(8),
            block(CONV),
            block(1),
            block(tokens),
            pl.BlockSpec((tokens, width), lambda j: (0, inside(j))),
            state,
            state,
            pl.BlockSpec((tokens, STATE), lambda j: (0, INNER // STATE)),
            whole(tokens),
            whole(tokens),
            whole(tokens),
        ],
        out_specs=[
            block(tokens),
            block(8),
            block(8),
            block(CONV),
            block(1),
            pl.BlockSpec((HEADS, tokens), lambda j: (0, 0)),
            whole(HEADS),
        ],
        out_shape=[
            jax.ShapeDtypeStruct((tokens, CHANNELS), bf16),
            jax.ShapeDtypeStruct((8, CHANNELS), f32),
            jax.ShapeDtypeStruct((8, CHANNELS), f32),
            jax.ShapeDtypeStruct((CONV, CHANNELS), f32),
            jax.ShapeDtypeStruct((1, CHANNELS), f32),
            jax.ShapeDtypeStruct((HEADS, tokens), f32),
            jax.ShapeDtypeStruct((HEADS, STATE), f32),
        ],
        scratch_shapes=[pltpu.VMEM((tokens, STATE), f32), pltpu.VMEM((tokens, STATE), f32)],
        name="leave",
        cost_estimate=no_cost,
        compiler_params=pltpu.CompilerParams(vmem_limit_bytes=40 * 2**20),
    )(
        projected, edge, taps, shift[None], conv_low, part, grad_fresh, incoming, conv_low,
        weigh, b_part, c_part,
    )


def rms_scale(values, gain):
    return values * lax.rsqrt(jnp.mean(values * values, axis=-1, keepdims=True) + epsilon) * gain


def pack(arrays):
    flat = jnp.concatenate([a.reshape(-1) for a in arrays])
    pad = -flat.shape[0] % 1024
    return jnp.pad(flat, (0, pad)).reshape(-1, 128)


def local(
    hidden,
    lengths,
    norm_gain,
    in_weight,
    conv_weight,
    conv_bias,
    dt_bias,
    a_log,
    skip_d,
    gate_gain,
    out_weight,
    out_grad,
):
    ring = Ring(lax.axis_size("seq"), lax.axis_size("fsdp"))
    ring.clock = clock = Clock(hidden[0, :8, :128])
    _, row_count, model_width = hidden.shape
    fsdp_index = lax.axis_index("fsdp")
    where = places(ring)
    tokens = hidden[0].astype(f32)

    small = [norm_gain, conv_weight, conv_bias, dt_bias, a_log, skip_d, gate_gain]
    in_rows = in_weight.T
    shared = Spread(ring, in_rows, INNER)
    shared.first(at_once=True)
    shared.near()
    packed = pack(small)
    spread = jnp.zeros((ring.fsdp,) + packed.shape, bf16)
    for (d, e), place in where.items():
        block = ring.relative(packed, d, e)
        spread = lax.dynamic_update_slice_in_dim(spread, block[None], place, axis=0)
    spread = spread.reshape(ring.fsdp, -1)
    whole_small, at = [], 0
    for part in small:
        piece = spread[:, at : at + part.size]
        at += part.size
        if part.ndim == 2:
            piece = piece.reshape((ring.fsdp,) + part.shape).transpose(1, 0, 2)
            whole_small.append(piece.reshape(part.shape[0], -1).astype(f32))
        else:
            whole_small.append(piece.reshape(-1).astype(f32))
    gain_norm, conv_taps, conv_shift, step_bias, rate_log, skip_gain, gain_gate = whole_small

    gate_pieces = Pieces(ring, in_rows[:INNER], 3)
    out_spread = Spread(ring, out_weight, 0, whole_only=True)
    (spread,) = clock.tick(spread)
    shared.second()
    out_spread.first()
    clock.tick()
    shared.third()
    gate_pieces.send(later=1)
    clock.tick()
    shared.fourth()
    gate_pieces.send(later=1)
    out_spread.second()
    clock.tick()
    weight_conv = shared.whole()

    position = lax.axis_index("seq") * row_count + lax.broadcasted_iota(
        jnp.int32, (row_count, 1), 0
    )
    grad_out = jnp.where(position < lengths[0], out_grad[0], jnp.zeros_like(out_grad[0]))

    normed, pull_norm = jax.vjp(rms_scale, tokens, gain_norm)
    normed = normed.astype(bf16)
    depth = in_weight.shape[0]

    normed_columns = [
        lax.dynamic_slice_in_dim(normed, place * depth, depth, axis=1) for place in where.values()
    ]
    normed_for = columns_for(ring, normed)
    projected = project(normed_columns, list(weight_conv.values()), 896)
    (projected,) = clock.tick(projected)
    gate_pieces.send(later=1)
    out_spread.third()
    edge_rows = ring.next_block(projected[row_count - 8 :, :CHANNELS], 1)
    cum, weigh, decay, cum_rows, step_rows, through = steps(projected, step_bias, rate_log)
    conv_low, fresh_state = enter(
        ring,
        projected,
        edge_rows,
        conv_taps,
        conv_shift,
        weigh,
        spread_factors(ring, through[0, :HEADS]),
    )
    proj_b = conv_low[:, INNER : INNER + STATE]
    proj_c = conv_low[:, INNER + STATE :]
    (fresh_state,) = clock.tick(fresh_state)
    blocks = lax.all_to_all(fresh_state, "seq", 0, 0, tiled=True)
    gate_pieces.pass_on(0)
    gate_pieces.pass_on(1)
    out_spread.fourth()
    gate_pieces.near()
    out_spread.near()
    skip_row = jnp.repeat(skip_gain, HEADDIM)[None]
    base = inside(conv_low, cum, cum_rows, step_rows, skip_row)
    blocks, base = clock.tick(blocks, base)
    factor = blocks[:, INNER // ring.seq :]
    (states,) = clock.tick(carried(ring, blocks, factor, False))
    incoming = returned(ring, states).reshape(INNER, STATE)
    gate_pieces.pass_on(2)
    weight_gate = gate_pieces.pieces()
    weight_out = out_spread.whole()
    grad_pieces = Pieces(ring, grad_out)
    grad_pieces.send()
    gate_rows = gate_pieces.rows
    gate_parts = [
        project(normed_columns, [weight_gate[key][at] for key in where], gate_rows, gate_rows)
        for at in range(3)
    ]
    wide = out_weight.shape[0]
    place_row = jnp.stack(list(where.values())).astype(jnp.int32)
    grad_mixed = to_inner(grad_out, list(weight_out.values()), place_row)
    incoming, grad_mixed, *gate_parts = clock.tick(incoming, grad_mixed, *gate_parts)
    normed_all = trade_columns(ring, {key: clock.now(part) for key, part in normed_for.items()})
    grad_pieces.near()
    mixed, grad_y, grad_gate, grad_reach, direct, grad_g_gate = turn(
        base, incoming, proj_c, decay, gate_parts, grad_mixed, gain_gate
    )
    direct, mixed, grad_y, grad_reach, grad_gate = clock.tick(
        direct, mixed, grad_y, grad_reach, grad_gate
    )
    blocks = lax.all_to_all(direct.reshape(ring.seq, -1, STATE), "seq", 0, 0, tiled=True)
    mixed_all = trade_columns(ring, columns_for(ring, mixed))
    grad_out_all = grad_pieces.whole()
    x_part, b_part, c_part, grad_step, grad_cum, grad_skip = inside_back(
        grad_y, grad_reach, conv_low, incoming, cum, cum_rows, step_rows, skip_row
    )
    gate_grads = Pieces(ring, grad_gate)
    gate_grads.send()
    gate_grads.near()
    total_w_out = Total(ring, weight_grad(mixed_all, grad_out_all, 384))
    blocks, x_part, total_w_out.value = clock.tick(blocks, x_part, total_w_out.value)
    (states,) = clock.tick(carried(ring, blocks, factor, True))
    chain_grad = returned(ring, states)
    total_w_out.step()
    clock.defer()
    total_w_gate = Total(ring, weight_grad(gate_grads.whole(), normed_all, 768))
    (total_w_gate.value,) = clock.tick(total_w_gate.value)
    total_w_gate.step()
    clock.defer(1, 2)
    chain_grad, b_part, c_part = clock.tick(chain_grad, b_part, c_part)
    total_w_out.step()
    grad_conv, first_rows, last_rows, grad_taps, grad_shift, grad_factor, crossed = leave(
        projected,
        edge_rows,
        conv_taps,
        conv_shift,
        conv_low,
        x_part,
        chain_grad.reshape(INNER, STATE),
        incoming,
        weigh,
        b_part,
        c_part,
    )
    grad_conv, last_rows, first_rows = clock.tick(grad_conv, last_rows, first_rows)
    back_rows = ring.next_block(first_rows, -1)
    grad_conv = lax.dynamic_update_slice_in_dim(
        grad_conv, (last_rows + back_rows).astype(bf16), row_count - 8, axis=0
    )
    (grad_conv,) = clock.tick(grad_conv)
    grad_dt_raw, grad_step_bias, grad_rate = steps_back(
        projected,
        step_bias,
        rate_log,
        step_rows,
        cum_rows,
        grad_step,
        grad_cum,
        clock.now(grad_factor),
        crossed,
    )
    grad_tail = jnp.concatenate([grad_conv, grad_dt_raw[:, :HEADS]], axis=1)

    cut = 1792
    first = Pieces(ring, grad_conv[:, :cut])
    last = Pieces(ring, jnp.concatenate([grad_conv[:, cut:], grad_dt_raw], axis=1))
    first.send()
    first.near()
    total_w_out.step()
    total_w_gate.step()
    clock.tick()
    last.send(later=1)
    last.near()
    total_w_out.step()
    clock.defer()
    total_first = Total(ring, weight_grad(first.whole(), normed_all, 896))
    (total_first.value,) = clock.tick(total_first.value)
    total_first.step()
    total_w_gate.step()
    clock.tick()
    total_first.step()
    total_w_out.step()
    total_w_gate.step()
    clock.defer(3)
    total_last = Total(ring, weight_grad(last.whole(), normed_all, 1664))
    (total_last.value,) = clock.tick(total_last.value)
    total_last.step()
    (grad_gate, grad_tail, mixed) = clock.tick(grad_gate, grad_tail, mixed)
    total_w_out.step()
    clock.defer()
    total_first.step()
    total_last.step()
    total_w_gate.step()
    grad_shards = to_model(
        grad_gate, grad_tail, list(weight_gate.values()), list(weight_conv.values())
    )
    mixed_columns = [
        lax.dynamic_slice_in_dim(mixed, place * wide, wide, axis=1) for place in where.values()
    ]
    (grad_shards,) = clock.tick(grad_shards)
    grad_normed = jnp.zeros((row_count, model_width), f32)
    for k, place in enumerate(where.values()):
        grad_normed = lax.dynamic_update_slice_in_dim(
            grad_normed, grad_shards[k], place * depth, axis=1
        )
    grad_skip = jnp.sum(clock.now(grad_skip).reshape(HEADS, HEADDIM), axis=1)
    grad_tokens, grad_g_norm = pull_norm(grad_normed)
    hidden_grad = (grad_tokens + grad_out.astype(f32)).astype(bf16)

    parts = [grad_g_norm, grad_taps, grad_shift[0], grad_step_bias[:, 0], grad_rate[:, 0]]
    parts += [grad_skip, grad_g_gate[0]]
    output = output_rows(
        clock.now(hidden[0]), mixed_columns, list(weight_out.values())
    )
    total_first.step()
    total_last.step()
    total_w_gate.halves()
    clock.defer()
    (output,) = clock.tick(output)
    small_total = SmallSum(ring, pack(parts))
    small_total.step()
    small_total.step()
    total_first.step()
    total_last.step()
    clock.tick()
    small_total.step()
    small_total.step()
    total_first.halves()
    clock.defer()
    total_last.step()
    clock.tick()
    small_total.step()
    total_last.halves()
    summed = small_total.finish().reshape(-1)
    shares, at = [], 0
    for part in parts:
        piece = summed[at : at + part.size].reshape(part.shape)
        at += part.size
        width = part.shape[-1] // ring.fsdp
        shares.append(
            lax.dynamic_slice_in_dim(piece, fsdp_index * width, width, axis=part.ndim - 1)
        )
    total_w_in = jnp.zeros((PROJ, depth), f32)
    total_w_in = place_rows(total_w_in, total_w_gate.halves(), 0, INNER)
    total_w_in = place_rows(total_w_in, total_first.halves(), INNER, cut)
    total_w_in = place_rows(total_w_in, total_last.halves(), INNER + cut, PROJ - INNER - cut)
    total_w_in = total_w_in.T
    total_w_out = total_w_out.finish()
    return (
        output[None],
        hidden_grad[None],
        shares[0],
        total_w_in,
        shares[1],
        shares[2],
        shares[3],
        shares[4],
        shares[5],
        shares[6],
        total_w_out,
    )


def solution(mesh):
    placed = (
        P("fsdp", "seq", None),
        P("fsdp"),
        P("fsdp"),
        P("fsdp", None),
        P(None, "fsdp"),
        P("fsdp"),
        P("fsdp"),
        P("fsdp"),
        P("fsdp"),
        P("fsdp"),
        P("fsdp", None),
        P("fsdp", "seq", None),
    )
    return jax.shard_map(
        local,
        mesh=mesh,
        in_specs=placed,
        out_specs=(
            P("fsdp", "seq", None),
            P("fsdp", "seq", None),
            P("fsdp"),
            P("fsdp", None),
            P(None, "fsdp"),
            P("fsdp"),
            P("fsdp"),
            P("fsdp"),
            P("fsdp"),
            P("fsdp"),
            P("fsdp", None),
        ),
        check_vma=False,
    )
```

```python
import functools

import jax
import jax.numpy as jnp
from jax import lax
from jax.experimental import pallas as pl
from jax.experimental.pallas import tpu as pltpu
from jax.sharding import PartitionSpec as P

HEADS = 48
HEADDIM = 64
STATE = 128
CONV = 4
INNER = 3072
CHANNELS = 3328
PROJ = 6448
PLANES = 2
CORES = 2
FIRST = 1792

f32 = jnp.float32
bf16 = jnp.bfloat16
epsilon = 1e-05
scoped = 40 * 2**20
whole_vmem = 60 * 2**20
no_cost = pl.CostEstimate(flops=0, bytes_accessed=0, transcendentals=0)


class Ring:
    def __init__(self, seq, fsdp):
        self.seq, self.fsdp = seq, fsdp
        self.clock = None
        self.line, self.row = seq // PLANES, fsdp // CORES

    def send(self, block, move):
        route = []
        for s in range(self.seq):
            for f in range(self.fsdp):
                there = move(s // PLANES, s % PLANES, f // CORES, f % CORES)
                if there is None:
                    continue
                z, x, y, c = there
                route.append((s * self.fsdp + f, (z * PLANES + x) * self.fsdp + y * CORES + c))
        arrived = lax.ppermute(block, ("seq", "fsdp"), route)
        self.clock.sent(arrived)
        return arrived

    def core(self, block):
        return self.send(block, lambda z, x, y, c: (z, x, y, 1 - c))

    def plane(self, block):
        return self.send(block, lambda z, x, y, c: (z, 1 - x, y, c))

    def from_row(self, block, distance):
        return self.send(block, lambda z, x, y, c: (z, x, (y - distance) % self.row, c))

    def far(self, block, distance):
        return self.send(block, lambda z, x, y, c: (z ^ distance, x, y, c))

    def relative(self, block, d, e):
        if not d and not e:
            return block
        return self.send(
            block, lambda z, x, y, c: (z, x, (y - d) % self.row, (c + e) % CORES)
        )

    def relative_back(self, block, d, e):
        return self.relative(block, d, e)

    def next_block(self, block, distance):
        def move(z, x, y, c):
            s = z * PLANES + x + distance
            return (s // PLANES, s % PLANES, y, c) if 0 <= s < self.seq else None

        return self.send(block, move)


def rows_of(block, index, count):
    return lax.dynamic_slice_in_dim(block, index * count, count, axis=0)


def swapped(ring, distance):
    seq_index = lax.axis_index("seq")
    if distance == 0:
        return seq_index % PLANES, ring.plane
    bit = (seq_index // PLANES // distance) % 2
    return bit, lambda block: ring.far(block, distance)


def cube(ring):
    distances, distance = [0], 1
    while distance < ring.line:
        distances.append(distance)
        distance *= 2
    return distances


class Total:
    def __init__(self, ring, grad):
        self.ring, self.value, self.other, self.merge = ring, grad, None, None
        self.steps = [(True, d) for d in cube(ring)] + [(False, d) for d in reversed(cube(ring))]

    def settle(self):
        if self.merge is not None:
            value, other = self.ring.clock.now((self.value, self.other))
            self.value, self.merge = self.merge(value, other), None
        else:
            self.value = self.ring.clock.now(self.value)

    def step(self):
        if not self.steps:
            return
        self.settle()
        halves, distance = self.steps.pop(0)
        bit, send = swapped(self.ring, distance)
        if halves:
            half = self.value.shape[0] // 2
            self.other = send(rows_of(self.value, 1 - bit, half).astype(bf16))
            self.merge = lambda value, other: rows_of(value, bit, half) + other.astype(f32)
        else:
            self.value = self.value.astype(bf16)
            self.other = send(self.value)
            self.merge = lambda value, other: jnp.concatenate(
                [jnp.where(bit == 0, value, other), jnp.where(bit == 0, other, value)], axis=0
            )

    def finish(self):
        while self.steps:
            self.step()
        self.settle()
        return self.value.astype(f32)

    def halves(self):
        while self.steps:
            self.step()
        return self.value, self.other


class Clock:
    def __init__(self, value):
        self.token = value
        self.pending = []

    def sent(self, value):
        self.pending.append([1, value])

    def tick(self, *values):
        due = [value for ticks, value in self.pending if ticks == 1]
        out = lax.optimization_barrier((self.token,) + values + tuple(due))
        self.token = out[0]
        self.pending = [[ticks - 1, value] for ticks, value in self.pending if ticks > 1]
        return out[1 : 1 + len(values)]

    def defer(self, count=1, ticks=1):
        for entry in self.pending[len(self.pending) - count :]:
            entry[0] += ticks

    def now(self, value):
        return lax.optimization_barrier((value, self.token))[0]


class Spread:
    def __init__(self, ring, source, origin=0, whole_only=False):
        self.ring, self.source, self.origin, self.whole_only = ring, source, origin, whole_only
        block = self.block = source[origin:]
        self.quarter = -(-block.shape[0] // 64) * 16
        self.cut = -(-self.quarter // 32) * 16
        seq_index = lax.axis_index("seq")
        self.place = seq_index % 2 + 2 * ((seq_index // PLANES) % 2)
        self.arrived = []

    def start(self, index):
        return jnp.minimum((self.place ^ index) * self.quarter, self.block.shape[0] - self.quarter)

    def put(self, pieces):
        sides = (pieces,)
        if not self.whole_only:
            sides += ([self.ring.core(piece) for piece in pieces],)
        self.arrived.append(sides)

    def first(self, at_once=False):
        ring = self.ring
        mine = lax.dynamic_slice_in_dim(self.source, self.origin + self.start(0), self.quarter, axis=0)
        mine = mine if at_once else ring.clock.now(mine)
        self.mine = [ring.from_row(mine, d) for d in range(1, ring.row)]

    def second(self):
        ring = self.ring
        mine = [ring.clock.now(part) for part in self.mine]
        self.beside = [ring.plane(part) for part in mine]
        self.behind = [ring.far(part, 1) for part in mine]
        self.put(mine)

    def third(self):
        ring, cut = self.ring, self.cut
        beside = [ring.clock.now(part) for part in self.beside]
        behind = [ring.clock.now(part) for part in self.behind]
        self.corner = (
            [ring.plane(part[:cut]) for part in behind],
            [ring.far(part[cut:], 1) for part in beside],
        )
        self.put(beside)
        self.put(behind)

    def fourth(self):
        now = self.ring.clock.now
        self.put([now(part) for part in self.corner[0]])
        self.put([now(part) for part in self.corner[1]])

    def whole(self, near):
        found = {(0, 0): self.block, (0, 1): near}
        index = jnp.stack([self.place ^ k for k in range(4)]).astype(jnp.int32)
        for d in range(1, self.ring.row):
            sides = [[side[d - 1] for side in pieces] for pieces in zip(*self.arrived)]
            shards = laid(self.block, self.quarter, self.cut, index, sides)
            found[d, 0] = shards[0]
            found[d, 1] = self.ring.core(shards[0]) if self.whole_only else shards[1]
        return found


def sum_body(count, *refs):
    out_ref = refs[-1]
    total = None
    for left, right in zip(refs[:count], refs[count:-1]):
        term = lax.dot_general(
            left[...], right[...], (((0,), (0,)), ((), ())), preferred_element_type=f32
        )
        total = term if total is None else total + term
    out_ref[...] = total


def weight_grad(rows_all, columns_all, tile):
    keys = list(rows_all)
    tokens, rows = rows_all[keys[0]].shape
    width = columns_all[keys[0]].shape[1]
    return pl.pallas_call(
        functools.partial(sum_body, len(keys)),
        grid=(rows // tile,),
        in_specs=[pl.BlockSpec((tokens, tile), lambda i: (0, i))] * len(keys)
        + [pl.BlockSpec((tokens, width), lambda i: (0, 0))] * len(keys),
        out_specs=pl.BlockSpec((tile, width), lambda i: (i, 0)),
        out_shape=jax.ShapeDtypeStruct((rows, width), f32),
        name="weight_grad",
        cost_estimate=no_cost,
        compiler_params=pltpu.CompilerParams(vmem_limit_bytes=scoped),
    )(*[rows_all[key] for key in keys], *[columns_all[key] for key in keys])


def to_inner_body(tiles, place_ref, grad_ref, *refs):
    out_ref = refs[-1]
    shard = pl.program_id(0) // tiles
    for k, weight in enumerate(refs[:-1]):

        @pl.when(shard == k)
        def _(weight=weight):
            out_ref[...] = dot_last(grad_ref[...], weight[...])


def to_inner(grad, weights, places):
    tokens, width = grad.shape
    rows = weights[0].shape[0]
    tile = 384
    tiles = rows // tile
    return pl.pallas_call(
        functools.partial(to_inner_body, tiles),
        grid_spec=pltpu.PrefetchScalarGridSpec(
            num_scalar_prefetch=1,
            grid=(len(weights) * tiles,),
            in_specs=[pl.BlockSpec((tokens, width), lambda i, place: (0, 0))]
            + [
                pl.BlockSpec(
                    (tile, width), lambda i, place, k=k: (jnp.clip(i - k * tiles, 0, tiles - 1), 0)
                )
                for k in range(len(weights))
            ],
            out_specs=pl.BlockSpec(
                (tokens, tile), lambda i, place: (0, place[i // tiles] * tiles + i % tiles)
            ),
        ),
        out_shape=jax.ShapeDtypeStruct((tokens, rows * len(weights)), f32),
        name="to_inner",
        cost_estimate=no_cost,
        compiler_params=pltpu.CompilerParams(vmem_limit_bytes=scoped),
    )(places, grad, *weights)


def to_model_body(terms, gate_ref, tail_ref, *refs):
    out_ref = refs[-1]
    for k, shard in enumerate(terms):
        total = None
        for tail, column, array, row, count in shard:
            left = (tail_ref if tail else gate_ref)[:, column : column + count]
            term = jnp.dot(left, refs[array][row : row + count], preferred_element_type=f32)
            total = term if total is None else total + term
        out_ref[k] = total


def to_model(grad_gate, grad_tail, gate_weights, tail_weights):
    width = grad_tail.shape[1]
    rows = grad_gate.shape[1] // len(gate_weights[0])
    flat, terms = [], []

    def place(array):
        for k, held in enumerate(flat):
            if held is array:
                return k
        flat.append(array)
        return len(flat) - 1

    for pieces, (tail, start) in zip(gate_weights, tail_weights):
        shard = [(True, 0, place(tail), start, width)]
        if pieces[0][0] is tail:
            shard.append((False, 0, place(tail), 0, grad_gate.shape[1]))
        else:
            shard += [
                (False, at * rows, place(array), block * rows, rows)
                for at, (array, block) in enumerate(pieces)
            ]
        terms.append(shard)
    inside = pl.BlockSpec(memory_space=pltpu.VMEM)
    return pl.pallas_call(
        functools.partial(to_model_body, terms),
        in_specs=[inside] * (2 + len(flat)),
        out_specs=inside,
        out_shape=jax.ShapeDtypeStruct((len(terms), grad_gate.shape[0], flat[0].shape[1]), f32),
        name="to_model",
        cost_estimate=no_cost,
        compiler_params=pltpu.CompilerParams(vmem_limit_bytes=scoped),
    )(grad_gate, grad_tail, *flat)


def output_body(count, token_ref, *refs):
    out_ref = refs[-1]
    total = token_ref[...].astype(f32)
    for columns, weight in zip(refs[:count], refs[count:-1]):
        total = total + jnp.dot(columns[...], weight[...], preferred_element_type=f32)
    out_ref[...] = total.astype(bf16)


def output_rows(tokens, columns, weights):
    inside = pl.BlockSpec(memory_space=pltpu.VMEM)
    return pl.pallas_call(
        functools.partial(output_body, len(columns)),
        in_specs=[inside] * (1 + 2 * len(columns)),
        out_specs=inside,
        out_shape=jax.ShapeDtypeStruct(tokens.shape, bf16),
        name="output_rows",
        cost_estimate=no_cost,
        compiler_params=pltpu.CompilerParams(vmem_limit_bytes=scoped),
    )(tokens, *columns, *weights)


def laid_body(quarter, cut, index_ref, *refs):
    count = len(refs) // 6
    pieces, shards = refs[:-count], refs[-count:]
    for e, shard in enumerate(shards):
        own = pieces[e * 5 : e * 5 + 5]
        for piece, quarter_of, offset in zip(own, (0, 1, 2, 3, 3), (0, 0, 0, 0, cut)):
            start = jnp.minimum(index_ref[quarter_of] * quarter, shard.shape[0] - quarter)
            start = pl.multiple_of(start + offset, 16)
            shard[pl.ds(start, piece.shape[0]), :] = piece[...]


def laid(block, quarter, cut, index, sides):
    flat = [piece for side in sides for piece in side]
    inside = pl.BlockSpec(memory_space=pltpu.VMEM)
    return pl.pallas_call(
        functools.partial(laid_body, quarter, cut),
        grid_spec=pltpu.PrefetchScalarGridSpec(
            num_scalar_prefetch=1,
            grid=(),
            in_specs=[inside] * len(flat),
            out_specs=[inside] * len(sides),
        ),
        out_shape=[jax.ShapeDtypeStruct(block.shape, block.dtype)] * len(sides),
        name="laid",
        cost_estimate=no_cost,
        compiler_params=pltpu.CompilerParams(vmem_limit_bytes=scoped),
    )(index, *flat)


def project_body(count, *refs):
    out_ref = refs[-1]
    total = None
    for columns, weight in zip(refs[:count], refs[count:-1]):
        term = lax.dot_general(
            columns[...], weight[...], (((1,), (1,)), ((), ())), preferred_element_type=f32
        )
        total = term if total is None else total + term
    out_ref[...] = total.astype(out_ref.dtype)


def project(columns, weights, tile, width):
    count = len(columns)
    tokens, depth = columns[0].shape
    return pl.pallas_call(
        functools.partial(project_body, count),
        grid=(pl.cdiv(width, tile),),
        in_specs=[pl.BlockSpec((tokens, depth), lambda i: (0, 0))] * count
        + [pl.BlockSpec((tile, depth), lambda i, k=k: (i + k, 0)) for _, k in weights],
        out_specs=pl.BlockSpec((tokens, tile), lambda i: (0, i)),
        out_shape=jax.ShapeDtypeStruct((tokens, width), bf16),
        name="project",
        cost_estimate=no_cost,
        compiler_params=pltpu.CompilerParams(vmem_limit_bytes=scoped),
    )(*columns, *[array for array, _ in weights])


class Pieces:
    def __init__(self, ring, block, count=1):
        self.ring, self.block = ring, block
        self.rows = block.shape[0] // count
        self.parts = []

    def near(self):
        self.beside = self.ring.core(self.ring.clock.now(self.block))

    def send(self, later=0):
        clock = self.ring.clock
        at = len(self.parts) * self.rows
        piece = clock.now(self.block[at : at + self.rows])
        self.parts.append([self.ring.from_row(piece, d) for d in range(1, self.ring.row)])
        clock.defer(self.ring.row - 1, later)

    def pass_on(self, at):
        far = [self.ring.clock.now(piece) for piece in self.parts[at]]
        self.parts[at] = [(piece, self.ring.core(piece)) for piece in far]

    def pieces(self, own, near):
        count = len(self.parts)
        found = {
            (0, 0): [(own, at) for at in range(count)],
            (0, 1): [(near, at) for at in range(count)],
        }
        for d in range(1, self.ring.row):
            for e in range(CORES):
                found[d, e] = [(part[d - 1][e], 0) for part in self.parts]
        return found

    def whole(self):
        found = {(0, 0): self.block, (0, 1): self.beside}
        for d in range(1, self.ring.row):
            found[d, 0] = self.ring.clock.now(self.parts[0][d - 1])
            found[d, 1] = self.ring.core(found[d, 0])
        return found


def gather_rows(ring, block):
    found = {}
    for d in range(ring.row):
        found[d, 0] = block if d == 0 else ring.from_row(block, d)
        found[d, 1] = ring.core(found[d, 0])
    return found


def places(ring):
    index = lax.axis_index("fsdp")
    y, c = index // CORES, index % CORES
    return {
        (d, e): ((y + d) % ring.row) * CORES + (c + e) % CORES
        for d in range(ring.row)
        for e in range(CORES)
    }


def columns_for(ring, block):
    index = lax.axis_index("fsdp")
    y, c = index // CORES, index % CORES
    width = block.shape[1] // ring.fsdp
    return {
        (d, e): lax.dynamic_slice_in_dim(
            block, (((y - d) % ring.row) * CORES + (c + e) % CORES) * width, width, axis=1
        )
        for d in range(ring.row)
        for e in range(CORES)
    }


def trade_columns(ring, pieces):
    return {key: ring.relative_back(piece, *key) for key, piece in pieces.items()}


class SmallSum:
    def __init__(self, ring, vector):
        self.ring, self.value = ring, vector
        self.steps = ["core", "row"] + cube(ring)

    def step(self):
        if not self.steps:
            return
        kind = self.steps.pop(0)
        vector = self.ring.clock.now(self.value)
        if kind == "core":
            self.value = vector + self.ring.core(vector)
        elif kind == "row":
            self.value = sum([self.ring.from_row(vector, d) for d in range(1, self.ring.row)], vector)
        else:
            self.value = vector + swapped(self.ring, kind)[1](vector)

    def finish(self):
        while self.steps:
            self.step()
        return self.value


def head_rows(ring):
    part = INNER // ring.seq
    run = HEADDIM
    while part % run:
        run //= 2
    return part, run


def spread_factors(ring, through):
    part, run = head_rows(ring)
    factor = jnp.repeat(through, HEADDIM // run).reshape(ring.seq, part // run)
    factor = jnp.pad(factor, ((0, 0), (0, 8 - part // run)))
    return jnp.broadcast_to(factor[:, :, None], (ring.seq, 8, STATE))


def carried_body(reverse, run, blocks_ref, factor_ref, out_ref):
    count, part = out_ref.shape[0], out_ref.shape[1]
    state = jnp.zeros((part, STATE), f32)
    for k in reversed(range(count)) if reverse else range(count):
        out_ref[k] = state.astype(bf16)
        factor = factor_ref[k]
        spread = [jnp.broadcast_to(factor[j : j + 1], (run, STATE)) for j in range(part // run)]
        state = jnp.concatenate(spread, axis=0) * state + blocks_ref[k, :part]


def carried(ring, blocks, factor, reverse):
    part, run = head_rows(ring)
    return pl.pallas_call(
        functools.partial(carried_body, reverse, run),
        out_shape=jax.ShapeDtypeStruct((ring.seq, part, STATE), bf16),
        name="carried",
        cost_estimate=no_cost,
        compiler_params=pltpu.CompilerParams(vmem_limit_bytes=scoped),
    )(blocks, factor)


def returned(ring, states):
    states = lax.all_to_all(states, "seq", 0, 0, tiled=True)
    return states.reshape(HEADS, HEADDIM, STATE)


def place_rows(whole, sides, start, rows):
    mine, other = sides
    first = (lax.axis_index("seq") % PLANES) == 0
    half = mine.shape[0]
    low = jnp.where(first, mine, other).astype(f32)
    high = jnp.where(first, other, mine)[: rows - half].astype(f32)
    whole = lax.dynamic_update_slice_in_dim(whole, low, start, axis=0)
    return lax.dynamic_update_slice_in_dim(whole, high, start + half, axis=0)


def steps_body(dt_ref, bias_ref, rate_ref, cum_ref, weigh_ref, decay_ref, cum_rows, step_rows, through_ref):
    raw = dt_ref[...].astype(f32) + bias_ref[...]
    step = jnp.maximum(raw, 0.0) + jnp.log1p(jnp.exp(-jnp.abs(raw)))
    tokens = step.shape[0]
    row = lax.broadcasted_iota(jnp.int32, step.shape, 0)
    cum = step * -jnp.exp(rate_ref[...])
    distance = 1
    while distance < tokens:
        cum = cum + jnp.where(row >= distance, pltpu.roll(cum, distance, 0), 0.0)
        distance *= 2
    end = cum[tokens - 1 :]
    cum_ref[...] = cum
    weigh_ref[...] = jnp.exp(end - cum) * step
    decay_ref[...] = jnp.exp(cum)
    cum_rows[...] = cum.T[:HEADS]
    step_rows[...] = step.T[:HEADS]
    through_ref[...] = jnp.exp(end)


def steps(projected, bias, rate):
    tokens = projected.shape[0]
    row = pl.BlockSpec((1, STATE), lambda i: (0, 0))
    by_token = pl.BlockSpec((tokens, STATE), lambda i: (0, 0))
    by_head = pl.BlockSpec((HEADS, tokens), lambda i: (0, 0))
    pad = lambda v: jnp.pad(v, (0, STATE - HEADS))[None]
    return pl.pallas_call(
        steps_body,
        grid=(1,),
        in_specs=[pl.BlockSpec((tokens, STATE), lambda i: (0, CHANNELS // STATE)), row, row],
        out_specs=[by_token] * 3 + [by_head] * 2 + [row],
        out_shape=[jax.ShapeDtypeStruct((tokens, STATE), f32)] * 3
        + [jax.ShapeDtypeStruct((HEADS, tokens), f32)] * 2
        + [jax.ShapeDtypeStruct((1, STATE), f32)],
        name="steps",
        cost_estimate=no_cost,
        compiler_params=pltpu.CompilerParams(vmem_limit_bytes=scoped),
    )(projected, pad(bias), pad(rate))


def steps_back_body(
    dt_ref, bias_ref, rate_ref, step_ref, cum_ref, grad_step_ref, grad_cum_ref, factor_ref, crossed_ref,
    grad_ref, bias_grad_ref, rate_grad_ref,
):
    step, cum, factor = step_ref[...], cum_ref[...], factor_ref[...]
    tokens = step.shape[1]
    lane = lax.broadcasted_iota(jnp.int32, step.shape, 1)
    end = cum[:, tokens - 1 :]
    to_end = jnp.exp(end - cum)
    tail = factor * step * to_end
    grad_end = jnp.sum(tail, axis=1, keepdims=True) + jnp.exp(end) * jnp.sum(
        crossed_ref[...], axis=1, keepdims=True
    )
    total = grad_cum_ref[...] - tail + jnp.where(lane == tokens - 1, grad_end, 0.0)
    distance = 1
    while distance < tokens:
        moved = pltpu.roll(total, tokens - distance, 1)
        total = total + jnp.where(lane < tokens - distance, moved, 0.0)
        distance *= 2
    rate = -jnp.exp(rate_ref[...])
    rate_grad_ref[...] = rate * jnp.sum(total * step, axis=1, keepdims=True)
    raw = dt_ref[...].astype(f32).T[:HEADS] + bias_ref[...]
    grad = (grad_step_ref[...] + factor * to_end + total * rate) * jax.nn.sigmoid(raw)
    bias_grad_ref[...] = jnp.sum(grad, axis=1, keepdims=True)
    none = jnp.zeros((STATE - HEADS, tokens), f32)
    grad_ref[...] = jnp.concatenate([grad, none], axis=0).T.astype(bf16)


def steps_back(projected, bias, rate, step_rows, cum_rows, grad_step, grad_cum, factor, crossed):
    tokens = projected.shape[0]
    column = pl.BlockSpec((HEADS, 1), lambda i: (0, 0))
    by_head = pl.BlockSpec((HEADS, tokens), lambda i: (0, 0))
    return pl.pallas_call(
        steps_back_body,
        grid=(1,),
        in_specs=[pl.BlockSpec((tokens, STATE), lambda i: (0, CHANNELS // STATE)), column, column]
        + [by_head] * 5
        + [pl.BlockSpec((HEADS, STATE), lambda i: (0, 0))],
        out_specs=[pl.BlockSpec((tokens, STATE), lambda i: (0, 0)), column, column],
        out_shape=[
            jax.ShapeDtypeStruct((tokens, STATE), bf16),
            jax.ShapeDtypeStruct((HEADS, 1), f32),
            jax.ShapeDtypeStruct((HEADS, 1), f32),
        ],
        name="steps_back",
        cost_estimate=no_cost,
        compiler_params=pltpu.CompilerParams(vmem_limit_bytes=scoped),
    )(
        projected, bias[:, None], rate[:, None], step_rows, cum_rows, grad_step, grad_cum, factor,
        crossed,
    )


def group_columns(wide_ref, group, heads):
    shift = lax.rem(STATE - heads * group, STATE)
    return pltpu.roll(wide_ref[...], shift, 1)[:, :heads]


def keep_columns(wide_ref, at, columns):
    wide = wide_ref[...]
    lane = lax.broadcasted_iota(jnp.int32, wide.shape, 1)
    for k, column in enumerate(columns):
        wide = jnp.where(lane == at + k, column, wide)
    wide_ref[...] = wide


def along(column_pair):
    lane = lax.broadcasted_iota(jnp.int32, (column_pair.shape[0], 2 * HEADDIM), 1)
    return jnp.where(lane < HEADDIM, column_pair[:, :1], column_pair[:, 1:2])


def conv_sum(edge, rows, taps, shift):
    window = jnp.concatenate([edge, rows], axis=0)
    total = shift
    for k in range(CONV):
        moved = window if k == CONV - 1 else pltpu.roll(window, CONV - 1 - k, 0)
        total = total + taps[k : k + 1] * moved[8:]
    return total


def enter_body(part, proj_ref, edge_ref, taps_ref, shift_ref, weigh_ref, factor_ref, low_ref, fresh_ref):
    def conv(at, width):
        columns = slice(at, at + width)
        total = conv_sum(
            edge_ref[:, columns].astype(f32),
            proj_ref[:, columns].astype(f32),
            taps_ref[:, columns],
            shift_ref[:, columns],
        )
        low = (total * jax.nn.sigmoid(total)).astype(bf16)
        low_ref[:, columns] = low
        return low

    proj_b = conv(INNER, 2 * STATE)[:, :STATE]
    fresh_ref[:, part:] = factor_ref[...]
    for at in range(0, INNER, 2 * HEADDIM):
        low = conv(at, 2 * HEADDIM)
        head = at // HEADDIM
        weighted = (low.astype(f32) * along(weigh_ref[:, head : head + 2])).astype(bf16)
        fresh = lax.dot_general(
            weighted, proj_b, (((0,), (0,)), ((), ())), preferred_element_type=f32
        )
        row = at
        while row < at + 2 * HEADDIM:
            device, offset = row // part, row % part
            count = min(part - offset, at + 2 * HEADDIM - row)
            fresh_ref[device, offset : offset + count] = fresh[row - at : row - at + count]
            row += count


def enter(ring, projected, edge, taps, shift, weigh, factor):
    part, _ = head_rows(ring)
    return pl.pallas_call(
        functools.partial(enter_body, part),
        out_shape=[
            jax.ShapeDtypeStruct((projected.shape[0], CHANNELS), bf16),
            jax.ShapeDtypeStruct((ring.seq, part + 8, STATE), f32),
        ],
        name="enter",
        cost_estimate=no_cost,
        compiler_params=pltpu.CompilerParams(vmem_limit_bytes=scoped),
    )(projected, edge, taps, shift[None], weigh, factor)


def pairs_along(columns):
    return jnp.concatenate(
        [along(columns[:, i : i + 2]) for i in range(0, columns.shape[1], 2)], axis=1
    )


def turn_body(
    base_ref, incoming_ref, c_ref, decay_ref, grad_ref, gain_ref, *refs,
):
    count = len(refs) - 10
    gate_refs = refs[:count]
    (
    mixed_ref, grad_y_ref, grad_gate_ref, grad_reach_ref, direct_ref, gain_grad_ref,
    mixer, grads, squares, products,
    ) = refs[count:]
    later, j = pl.program_id(0), pl.program_id(1)
    gate = gate_refs[0][...]
    for k in range(1, count):
        gate = jnp.where(j * count >= k * pl.num_programs(1), gate_refs[k][...], gate)
    gate = gate.astype(f32)
    sig = jax.nn.sigmoid(gate)
    silu = gate * sig
    gain = gain_ref[...]

    @pl.when((later == 0) & (j == 0))
    def _():
        squares[...] = jnp.zeros_like(squares)
        products[...] = jnp.zeros_like(products)

    @pl.when(later == 0)
    def _():
        reached = lax.dot_general(
            c_ref[...], incoming_ref[...], (((1,), (1,)), ((), ())), preferred_element_type=f32
        )
        ssd = base_ref[...] + pairs_along(group_columns(decay_ref, j, gain.shape[1] // HEADDIM)) * reached
        gated = ssd * silu
        mixer[j] = ssd
        grads[j] = grad_ref[...]
        squares[...] += jnp.sum(gated * gated, axis=1, keepdims=True)
        products[...] += jnp.sum(gated * grad_ref[...] * gain, axis=1, keepdims=True)

    @pl.when(later == 1)
    def _():
        scale = lax.rsqrt(squares[...] / INNER + epsilon)
        ssd = mixer[j]
        grad = grads[j]
        normal = ssd * silu * scale
        mixed_ref[...] = (normal * gain).astype(bf16)
        gain_grad_ref[...] = jnp.sum(grad * normal, axis=0, keepdims=True)
        grad_gated = scale * (grad * gain - normal * (scale * products[...] / INNER))
        grad_y = (grad_gated * silu).astype(bf16)
        grad_y_ref[...] = grad_y
        grad_gate_ref[...] = (grad_gated * ssd * (sig + silu * (1.0 - sig))).astype(bf16)
        grad_reach = (grad_y.astype(f32) * pairs_along(group_columns(decay_ref, j, gain.shape[1] // HEADDIM))).astype(bf16)
        grad_reach_ref[...] = grad_reach
        direct_ref[...] = lax.dot_general(
            grad_reach, c_ref[...], (((0,), (0,)), ((), ())), preferred_element_type=f32
        )


def later_or_same(tokens):
    t = lax.broadcasted_iota(jnp.int32, (tokens, tokens), 0)
    return t >= lax.broadcasted_iota(jnp.int32, (tokens, tokens), 1)


def dot_last(a, b):
    return lax.dot_general(a, b, (((1,), (1,)), ((), ())), preferred_element_type=f32)


def dot_first(a, b):
    return lax.dot_general(a, b, (((0,), (0,)), ((), ())), preferred_element_type=f32)


def inside_body(x_ref, b_ref, c_ref, cum_ref, cum_rows_ref, step_rows_ref, skip_ref, out_ref, scores):
    tokens = x_ref.shape[0]

    @pl.when(pl.program_id(0) == 0)
    def _():
        table = dot_last(c_ref[...], b_ref[...])
        scores[...] = jnp.where(later_or_same(tokens), table, 0.0)

    x = x_ref[...]
    j = pl.program_id(0)
    same = later_or_same(tokens)
    cum = group_columns(cum_ref, j, 2)
    parts = []
    for head in range(2):
        row = pl.ds(2 * j + head, 1)
        exponent = cum[:, head : head + 1] - cum_rows_ref[row, :]
        decay = jnp.exp(jnp.where(same, exponent, 0.0))
        mixing = (scores[...] * decay * step_rows_ref[row, :]).astype(bf16)
        parts.append(jnp.dot(mixing, x, preferred_element_type=f32))
    first = lax.broadcasted_iota(jnp.int32, x.shape, 1) < HEADDIM
    out_ref[...] = jnp.where(first, parts[0], parts[1]) + skip_ref[...] * x.astype(f32)


def pair_specs(tokens):
    columns = pl.BlockSpec((tokens, 2 * HEADDIM), lambda j: (0, j))
    by_token = pl.BlockSpec((tokens, STATE), lambda j: (0, 0))
    by_head = pl.BlockSpec((HEADS, tokens), lambda j: (0, 0))
    row = pl.BlockSpec((1, 2 * HEADDIM), lambda j: (0, j))
    proj_b = pl.BlockSpec((tokens, STATE), lambda j: (0, INNER // STATE))
    proj_c = pl.BlockSpec((tokens, STATE), lambda j: (0, INNER // STATE + 1))
    return columns, by_token, by_head, row, proj_b, proj_c


def inside(conv_low, cum_pairs, cum_rows, step_rows, skip_row):
    tokens = conv_low.shape[0]
    columns, by_token, by_head, row, proj_b, proj_c = pair_specs(tokens)
    return pl.pallas_call(
        inside_body,
        grid=(HEADS // 2,),
        in_specs=[columns, proj_b, proj_c, by_token, by_head, by_head, row],
        out_specs=columns,
        out_shape=jax.ShapeDtypeStruct((tokens, INNER), f32),
        scratch_shapes=[pltpu.VMEM((tokens, tokens), f32)],
        name="inside",
        cost_estimate=no_cost,
        compiler_params=pltpu.CompilerParams(vmem_limit_bytes=scoped),
    )(conv_low, conv_low, conv_low, cum_pairs, cum_rows, step_rows, skip_row)


def inside_back_body(
    y_ref, reach_ref, x_ref, b_ref, c_ref, incoming_ref, cum_ref, cum_rows_ref, step_rows_ref, skip_ref,
    x_out, b_out, c_out, step_out, cum_out, skip_out,
    scores, grad_scores, wide_sums,
):
    tokens = x_ref.shape[0]
    j = pl.program_id(0)

    @pl.when(j == 0)
    def _():
        table = dot_last(c_ref[...], b_ref[...])
        scores[...] = jnp.where(later_or_same(tokens), table, 0.0)
        grad_scores[...] = jnp.zeros_like(grad_scores)
        c_out[...] = jnp.zeros_like(c_out)

    x, y = x_ref[...], y_ref[...]
    wide = y.astype(f32)
    incoming = incoming_ref[...]
    reached = wide * dot_last(c_ref[...], incoming)
    c_out[...] += jnp.dot(reach_ref[...], incoming, preferred_element_type=f32)
    skip_out[...] = jnp.sum(wide * x.astype(f32), axis=0, keepdims=True)
    first = lax.broadcasted_iota(jnp.int32, x.shape, 1) < HEADDIM
    wide_cum = group_columns(cum_ref, j, 2)
    middle = tokens // 2
    same = later_or_same(middle)
    parts, sums = [], []
    totals = [0.0, 0.0, 0.0]
    for head in range(2):
        row = pl.ds(2 * j + head, 1)
        steps_row, cum_row = step_rows_ref[row, :], cum_rows_ref[row, :]
        own = jnp.where(first == (head == 0), y, jnp.zeros_like(y))
        mine = jnp.sum(
            reached[:, head * HEADDIM : (head + 1) * HEADDIM], axis=1, keepdims=True
        ) * jnp.exp(wide_cum[:, head : head + 1])
        by_row, by_column, given = [0.0, 0.0], [0.0, 0.0], [0.0, 0.0]
        for k, (late, early) in enumerate(((0, 0), (1, 0), (1, 1))):
            rows = slice(late * middle, (late + 1) * middle)
            columns = slice(early * middle, (early + 1) * middle)
            step = steps_row[:, columns]
            exponent = wide_cum[rows, head : head + 1] - cum_row[:, columns]
            decay = jnp.exp(jnp.where(same, exponent, 0.0) if late == early else exponent)
            both = scores[rows, columns] * decay
            grad_mix = dot_last(own[rows], x[columns])
            totals[k] = totals[k] + grad_mix * (decay * step)
            by_source = grad_mix * both
            by_column[early] = by_column[early] + jnp.sum(by_source, axis=0, keepdims=True)
            by_row[late] = by_row[late] + jnp.sum(by_source * step, axis=1, keepdims=True)
            given[early] = given[early] + dot_first((both * step).astype(bf16), y[rows])
        step_out[row, :] = jnp.concatenate(by_column, axis=1)
        sums.append(jnp.concatenate(by_row, axis=0) + mine)
        parts.append(jnp.concatenate(given, axis=0))
    for total, (late, early) in zip(totals, ((0, 0), (1, 0), (1, 1))):
        grad_scores[late * middle : (late + 1) * middle, early * middle : (early + 1) * middle] += total
    keep_columns(wide_sums, 2 * j, sums)
    x_out[...] = jnp.where(first, parts[0], parts[1]) + skip_ref[...] * wide

    @pl.when(j == pl.num_programs(0) - 1)
    def _():
        grad = jnp.where(later_or_same(tokens), grad_scores[...], 0.0).astype(bf16)
        c_out[...] += jnp.dot(grad, b_ref[...], preferred_element_type=f32)
        b_out[...] = dot_first(grad, c_ref[...])
        cum_out[...] = wide_sums[...].T[:HEADS] - step_out[...] * step_rows_ref[...]


def inside_back(grad_y, grad_reach, conv_low, incoming, cum_pairs, cum_rows, step_rows, skip_row):
    tokens = conv_low.shape[0]
    columns, by_token, by_head, row, proj_b, proj_c = pair_specs(tokens)
    whole = pl.BlockSpec((tokens, STATE), lambda j: (0, 0))
    pairs = HEADS // 2
    return pl.pallas_call(
        inside_back_body,
        grid=(pairs,),
        in_specs=[columns, columns, columns, proj_b, proj_c]
        + [pl.BlockSpec((2 * HEADDIM, STATE), lambda j: (j, 0)), by_token, by_head, by_head, row],
        out_specs=[columns, whole, whole, by_head, by_head, row],
        out_shape=[
            jax.ShapeDtypeStruct((tokens, INNER), f32),
            jax.ShapeDtypeStruct((tokens, STATE), f32),
            jax.ShapeDtypeStruct((tokens, STATE), f32),
            jax.ShapeDtypeStruct((HEADS, tokens), f32),
            jax.ShapeDtypeStruct((HEADS, tokens), f32),
            jax.ShapeDtypeStruct((1, INNER), f32),
        ],
        scratch_shapes=[
            pltpu.VMEM((tokens, tokens), f32),
            pltpu.VMEM((tokens, tokens), f32),
            pltpu.VMEM((tokens, STATE), f32),
        ],
        name="inside_back",
        cost_estimate=no_cost,
        compiler_params=pltpu.CompilerParams(vmem_limit_bytes=scoped),
    )(
        grad_y, grad_reach, conv_low, conv_low, conv_low, incoming, cum_pairs, cum_rows, step_rows,
        skip_row,
    )


def turn(base, incoming, proj_c, decay, gate_parts, grad_mixed, gain):
    tokens, heads = base.shape[0], 8
    width = heads * HEADDIM
    groups = INNER // width
    share = groups // len(gate_parts)
    once = lambda p, j: (0, jnp.where(p == 0, j, groups - 1))
    last = lambda p, j: (0, jnp.where(p == 0, 0, j))
    wide = jax.ShapeDtypeStruct((tokens, INNER), bf16)
    return pl.pallas_call(
        turn_body,
        grid=(2, groups),
        in_specs=[
            pl.BlockSpec((tokens, width), once),
            pl.BlockSpec((width, STATE), lambda p, j: (jnp.where(p == 0, j, groups - 1), 0)),
            pl.BlockSpec((tokens, STATE), lambda p, j: (0, 0)),
            pl.BlockSpec((tokens, STATE), lambda p, j: (0, 0)),
            pl.BlockSpec((tokens, width), once),
            pl.BlockSpec((1, width), lambda p, j: (0, j)),
        ]
        + [
            pl.BlockSpec(
                (tokens, width), lambda p, j, k=k: (0, jnp.clip(j - k * share, 0, share - 1))
            )
            for k in range(len(gate_parts))
        ],
        out_specs=[pl.BlockSpec((tokens, width), last)] * 4
        + [
            pl.BlockSpec((width, STATE), lambda p, j: (jnp.where(p == 0, 0, j), 0)),
            pl.BlockSpec((1, width), last),
        ],
        out_shape=[wide] * 4
        + [jax.ShapeDtypeStruct((INNER, STATE), f32), jax.ShapeDtypeStruct((1, INNER), f32)],
        scratch_shapes=[
            pltpu.VMEM((groups, tokens, width), f32),
            pltpu.VMEM((groups, tokens, width), f32),
            pltpu.VMEM((tokens, 1), f32),
            pltpu.VMEM((tokens, 1), f32),
        ],
        name="turn",
        cost_estimate=no_cost,
        compiler_params=pltpu.CompilerParams(vmem_limit_bytes=whole_vmem),
    )(base, incoming, proj_c, decay, grad_mixed, gain[None], *gate_parts)


def ahead(rows, count, distance):
    return (pltpu.roll(rows, rows.shape[0] - distance, 0) if distance else rows)[:count]


def leave_body(
    steps, proj_ref, edge_ref, taps_ref, shift_ref, low_ref, part_ref, fresh_ref, incoming_ref, b_ref,
    weigh_ref, b_part_ref, c_part_ref,
    grad_ref, grad_more_ref, first_ref, last_ref, taps_grad_ref, shift_grad_ref, factor_ref, crossed_ref,
    b_total, wide_factor,
):
    j = pl.program_id(0)

    def conv_back(grad_out):
        rows = proj_ref[...].astype(f32)
        window = jnp.concatenate([edge_ref[...].astype(f32), rows], axis=0)
        taps = taps_ref[...]
        moved = [
            (pltpu.roll(window, CONV - 1 - k, 0) if k < CONV - 1 else window)[8:]
            for k in range(CONV)
        ]
        total = shift_ref[...]
        for k in range(CONV):
            total = total + taps[k : k + 1] * moved[k]
        sig = jax.nn.sigmoid(total)
        grad = grad_out * (sig * (1.0 + total * (1.0 - sig)))
        shift_grad_ref[...] = jnp.sum(grad, axis=0, keepdims=True)
        taps_grad_ref[...] = jnp.concatenate(
            [jnp.sum(grad * part, axis=0, keepdims=True) for part in moved], axis=0
        )
        none = jnp.zeros((8, grad.shape[1]), f32)
        after_it = jnp.concatenate([grad, none], axis=0)
        before_it = jnp.concatenate([none, grad[:8]], axis=0)
        inner, outer = 0.0, 0.0
        for k in range(CONV):
            tap = taps[k : k + 1]
            inner = inner + tap * ahead(after_it, grad.shape[0], CONV - 1 - k)
            outer = outer + tap * ahead(before_it, 8, CONV - 1 - k)
        cut = FIRST // grad.shape[1]

        @pl.when(j < cut)
        def _():
            grad_ref[...] = inner.astype(bf16)

        @pl.when(j >= cut)
        def _():
            grad_more_ref[...] = inner.astype(bf16)

        last_ref[...] = inner[grad.shape[0] - 8 :]
        first_ref[...] = outer

    @pl.when(j == 0)
    def _():
        b_total[...] = b_part_ref[...]

    @pl.when(j < steps)
    def _():
        fresh = fresh_ref[...]
        x = low_ref[...].astype(f32)
        heads = x.shape[1] // HEADDIM
        weigh = pairs_along(group_columns(weigh_ref, j, heads))
        grad_weighted = lax.dot_general(
            b_ref[...], fresh, (((1,), (1,)), ((), ())), preferred_element_type=f32
        )
        weighted = (x * weigh).astype(bf16)
        b_total[...] += jnp.dot(weighted, fresh, preferred_element_type=f32)
        product = grad_weighted * x
        keep_columns(
            wide_factor,
            heads * j,
            [
                jnp.sum(product[:, i * HEADDIM : (i + 1) * HEADDIM], axis=1, keepdims=True)
                for i in range(heads)
            ],
        )
        both = fresh.astype(f32) * incoming_ref[...].astype(f32)
        for i in range(heads):
            row = pl.ds(heads * j + i, 1)
            crossed_ref[row, :] = jnp.sum(
                both[i * HEADDIM : (i + 1) * HEADDIM], axis=0, keepdims=True
            )
        conv_back(part_ref[...] + grad_weighted * weigh)

    @pl.when(j == steps)
    def _():
        factor_ref[...] = wide_factor[...].T[:HEADS]
        conv_back(jnp.concatenate([b_total[...], c_part_ref[...]], axis=1))


def leave(projected, edge, taps, shift, conv_low, part, grad_fresh, incoming, weigh, b_part, c_part):
    tokens, heads = part.shape[0], 4
    width = heads * HEADDIM
    steps = INNER // width
    cut = FIRST // width
    inside = lambda j: jnp.minimum(j, steps - 1)
    block = lambda rows: pl.BlockSpec((rows, width), lambda j: (0, j))
    whole = lambda rows: pl.BlockSpec((rows, STATE), lambda j: (0, 0))
    state = pl.BlockSpec((width, STATE), lambda j: (inside(j), 0))
    return pl.pallas_call(
        functools.partial(leave_body, steps),
        grid=(steps + 1,),
        in_specs=[
            block(tokens),
            block(8),
            block(CONV),
            block(1),
            block(tokens),
            pl.BlockSpec((tokens, width), lambda j: (0, inside(j))),
            state,
            state,
            pl.BlockSpec((tokens, STATE), lambda j: (0, INNER // STATE)),
            whole(tokens),
            whole(tokens),
            whole(tokens),
        ],
        out_specs=[
            pl.BlockSpec((tokens, width), lambda j: (0, jnp.minimum(j, cut - 1))),
            pl.BlockSpec((tokens, width), lambda j: (0, jnp.maximum(j - cut, 0))),
            block(8),
            block(8),
            block(CONV),
            block(1),
            pl.BlockSpec((HEADS, tokens), lambda j: (0, 0)),
            whole(HEADS),
        ],
        out_shape=[
            jax.ShapeDtypeStruct((tokens, FIRST), bf16),
            jax.ShapeDtypeStruct((tokens, CHANNELS - FIRST), bf16),
            jax.ShapeDtypeStruct((8, CHANNELS), f32),
            jax.ShapeDtypeStruct((8, CHANNELS), f32),
            jax.ShapeDtypeStruct((CONV, CHANNELS), f32),
            jax.ShapeDtypeStruct((1, CHANNELS), f32),
            jax.ShapeDtypeStruct((HEADS, tokens), f32),
            jax.ShapeDtypeStruct((HEADS, STATE), f32),
        ],
        scratch_shapes=[pltpu.VMEM((tokens, STATE), f32), pltpu.VMEM((tokens, STATE), f32)],
        name="leave",
        cost_estimate=no_cost,
        compiler_params=pltpu.CompilerParams(vmem_limit_bytes=whole_vmem),
    )(
        projected, edge, taps, shift[None], conv_low, part, grad_fresh, incoming, conv_low,
        weigh, b_part, c_part,
    )


def rms_scale(values, gain):
    return values * lax.rsqrt(jnp.mean(values * values, axis=-1, keepdims=True) + epsilon) * gain


def pack(arrays):
    flat = jnp.concatenate([a.reshape(-1) for a in arrays])
    pad = -flat.shape[0] % 1024
    return jnp.pad(flat, (0, pad)).reshape(-1, 128)


def local(
    hidden,
    lengths,
    norm_gain,
    in_weight,
    conv_weight,
    conv_bias,
    dt_bias,
    a_log,
    skip_d,
    gate_gain,
    out_weight,
    out_grad,
):
    ring = Ring(lax.axis_size("seq"), lax.axis_size("fsdp"))
    ring.clock = clock = Clock(hidden[0, :8, :128])
    _, row_count, model_width = hidden.shape
    fsdp_index = lax.axis_index("fsdp")
    where = places(ring)
    tokens = hidden[0].astype(f32)

    small = [norm_gain, conv_weight, conv_bias, dt_bias, a_log, skip_d, gate_gain]
    in_rows = in_weight.T
    shared = Spread(ring, in_rows, INNER)
    shared.first(at_once=True)
    near_rows = ring.core(in_rows)
    packed = pack(small)
    spread = jnp.zeros((ring.fsdp,) + packed.shape, bf16)
    for (d, e), place in where.items():
        block = ring.relative(packed, d, e)
        spread = lax.dynamic_update_slice_in_dim(spread, block[None], place, axis=0)
    spread = spread.reshape(ring.fsdp, -1)
    whole_small, at = [], 0
    for part in small:
        piece = spread[:, at : at + part.size]
        at += part.size
        if part.ndim == 2:
            piece = piece.reshape((ring.fsdp,) + part.shape).transpose(1, 0, 2)
            whole_small.append(piece.reshape(part.shape[0], -1).astype(f32))
        else:
            whole_small.append(piece.reshape(-1).astype(f32))
    gain_norm, conv_taps, conv_shift, step_bias, rate_log, skip_gain, gain_gate = whole_small

    gate_pieces = Pieces(ring, in_rows[:INNER], 3)
    out_spread = Spread(ring, out_weight, 0, whole_only=True)
    (spread,) = clock.tick(spread)
    shared.second()
    near_out = ring.core(clock.now(out_weight))
    out_spread.first()
    clock.tick()
    shared.third()
    gate_pieces.send(later=1)
    clock.tick()
    shared.fourth()
    gate_pieces.send(later=3)
    out_spread.second()
    clock.tick()
    tile = 768
    weight_conv = {key: (array, 0) for key, array in shared.whole(near_rows).items()}
    weight_conv[0, 0] = (in_rows, INNER // tile)
    weight_conv[0, 1] = (near_rows, INNER // tile)

    position = lax.axis_index("seq") * row_count + lax.broadcasted_iota(
        jnp.int32, (row_count, 1), 0
    )
    grad_out = jnp.where(position < lengths[0], out_grad[0], jnp.zeros_like(out_grad[0]))

    normed, pull_norm = jax.vjp(rms_scale, tokens, gain_norm)
    normed = normed.astype(bf16)
    depth = in_weight.shape[0]

    normed_columns = [
        lax.dynamic_slice_in_dim(normed, place * depth, depth, axis=1) for place in where.values()
    ]
    normed_for = columns_for(ring, normed)
    projected = project(normed_columns, list(weight_conv.values()), tile, PROJ - INNER)
    (projected,) = clock.tick(projected)
    edge_rows = ring.next_block(projected[row_count - 8 :, :CHANNELS], 1)
    cum, weigh, decay, cum_rows, step_rows, through = steps(projected, step_bias, rate_log)
    cum, weigh, edge_rows = clock.tick(cum, weigh, edge_rows)
    gate_pieces.send(later=1)
    conv_low, fresh_state = enter(
        ring,
        projected,
        edge_rows,
        conv_taps,
        conv_shift,
        weigh,
        spread_factors(ring, through[0, :HEADS]),
    )
    proj_b = conv_low[:, INNER : INNER + STATE]
    proj_c = conv_low[:, INNER + STATE :]
    (fresh_state,) = clock.tick(fresh_state)
    blocks = lax.all_to_all(fresh_state, "seq", 0, 0, tiled=True)
    out_spread.third()
    gate_pieces.pass_on(0)
    gate_pieces.pass_on(1)
    skip_row = jnp.repeat(skip_gain, HEADDIM)[None]
    base = inside(conv_low, cum, cum_rows, step_rows, skip_row)
    blocks, base = clock.tick(blocks, base)
    factor = blocks[:, INNER // ring.seq :]
    (states,) = clock.tick(carried(ring, blocks, factor, False))
    incoming = returned(ring, states).reshape(INNER, STATE)
    gate_pieces.pass_on(2)
    out_spread.fourth()
    weight_gate = gate_pieces.pieces(in_rows, near_rows)
    weight_out = out_spread.whole(near_out)
    grad_pieces = Pieces(ring, grad_out)
    grad_pieces.send()
    gate_rows = gate_pieces.rows
    gate_parts = [
        project(normed_columns, [weight_gate[key][at] for key in where], gate_rows, gate_rows)
        for at in range(3)
    ]
    wide = out_weight.shape[0]
    place_row = jnp.stack(list(where.values())).astype(jnp.int32)
    grad_mixed = to_inner(grad_out, list(weight_out.values()), place_row)
    incoming, grad_mixed, *gate_parts = clock.tick(incoming, grad_mixed, *gate_parts)
    normed_all = trade_columns(ring, {key: clock.now(part) for key, part in normed_for.items()})
    grad_pieces.near()
    mixed, grad_y, grad_gate, grad_reach, direct, grad_g_gate = turn(
        base, incoming, proj_c, decay, gate_parts, grad_mixed, gain_gate
    )
    direct, mixed, grad_y, grad_reach, grad_gate = clock.tick(
        direct, mixed, grad_y, grad_reach, grad_gate
    )
    blocks = lax.all_to_all(direct.reshape(ring.seq, -1, STATE), "seq", 0, 0, tiled=True)
    mixed_all = trade_columns(ring, columns_for(ring, mixed))
    clock.defer(len(mixed_all) - 1, 2)
    grad_out_all = grad_pieces.whole()
    x_part, b_part, c_part, grad_step, grad_cum, grad_skip = inside_back(
        grad_y, grad_reach, conv_low, incoming, cum, cum_rows, step_rows, skip_row
    )
    gate_grads = Pieces(ring, grad_gate)
    gate_grads.send(later=2)
    blocks, x_part, b_part, c_part = clock.tick(blocks, x_part, b_part, c_part)
    states = carried(ring, blocks, factor, True)
    (states,) = clock.tick(states)
    chain_grad = returned(ring, states)
    mixed_all = {key: clock.now(block) for key, block in mixed_all.items()}
    total_w_out = Total(ring, weight_grad(mixed_all, grad_out_all, 384))
    total_w_out.step()
    clock.defer()
    gate_grads.near()
    total_w_gate = Total(ring, weight_grad(gate_grads.whole(), normed_all, 768))
    (total_w_gate.value,) = clock.tick(total_w_gate.value)
    total_w_gate.step()
    clock.defer()
    mixed = clock.now(mixed)
    mixed_columns = [
        lax.dynamic_slice_in_dim(mixed, place * wide, wide, axis=1) for place in where.values()
    ]
    output = output_rows(hidden[0], mixed_columns, list(weight_out.values()))
    chain_grad, output = clock.tick(chain_grad, output)
    total_w_out.step()
    grad_conv, grad_more, first_rows, last_rows, grad_taps, grad_shift, grad_factor, crossed = leave(
        projected,
        edge_rows,
        conv_taps,
        conv_shift,
        conv_low,
        x_part,
        chain_grad.reshape(INNER, STATE),
        incoming,
        weigh,
        b_part,
        c_part,
    )
    grad_conv, grad_more, last_rows, first_rows = clock.tick(
        grad_conv, grad_more, last_rows, first_rows
    )
    total_w_out.step()
    clock.defer()
    last_rows = (last_rows + ring.next_block(first_rows, -1)).astype(bf16)
    grad_conv = lax.dynamic_update_slice_in_dim(
        grad_conv, last_rows[:, :FIRST], row_count - 8, axis=0
    )
    (grad_conv,) = clock.tick(grad_conv)
    grad_more = lax.dynamic_update_slice_in_dim(
        grad_more, last_rows[:, FIRST:], row_count - 8, axis=0
    )
    grad_dt_raw, grad_step_bias, grad_rate = steps_back(
        projected,
        step_bias,
        rate_log,
        step_rows,
        cum_rows,
        grad_step,
        grad_cum,
        clock.now(grad_factor),
        crossed,
    )
    grad_tail = jnp.concatenate([grad_conv, grad_more, grad_dt_raw[:, :HEADS]], axis=1)

    first = Pieces(ring, grad_conv)
    last = Pieces(ring, jnp.concatenate([grad_more, grad_dt_raw], axis=1))
    first.send()
    first.near()
    total_w_gate.step()
    clock.tick()
    last.send(later=1)
    last.near()
    total_first = Total(ring, weight_grad(first.whole(), normed_all, 896))
    (total_first.value,) = clock.tick(total_first.value)
    total_first.step()
    total_w_out.step()
    total_w_gate.step()
    grad_shards = to_model(
        grad_gate, clock.now(grad_tail), list(weight_gate.values()), [
            (array, block * tile) for array, block in weight_conv.values()
        ]
    )
    (grad_shards,) = clock.tick(grad_shards)
    total_last = Total(ring, weight_grad(last.whole(), normed_all, 1664))
    (total_last.value,) = clock.tick(total_last.value)
    total_last.step()
    total_first.step()
    total_w_out.step()
    total_w_gate.step()
    grad_normed = jnp.zeros((row_count, model_width), f32)
    for k, place in enumerate(where.values()):
        grad_normed = lax.dynamic_update_slice_in_dim(
            grad_normed, grad_shards[k], place * depth, axis=1
        )
    grad_skip = jnp.sum(clock.now(grad_skip).reshape(HEADS, HEADDIM), axis=1)
    grad_tokens, grad_g_norm = pull_norm(grad_normed)
    hidden_grad = (grad_tokens + grad_out.astype(f32)).astype(bf16)
    hidden_grad, grad_g_norm = clock.tick(hidden_grad, grad_g_norm)
    grad_shift, grad_step_bias, grad_rate, grad_g_gate = (
        clock.now(part) for part in (grad_shift, grad_step_bias, grad_rate, grad_g_gate)
    )
    parts = [grad_g_norm, grad_taps, grad_shift[0], grad_step_bias[:, 0], grad_rate[:, 0]]
    parts += [grad_skip, grad_g_gate[0]]
    small_total = SmallSum(ring, pack(parts))
    total_w_out.step()
    clock.defer()
    total_first.step()
    total_last.step()
    total_w_gate.step()
    clock.tick()
    small_total.step()
    total_w_gate.halves()
    clock.defer()
    total_first.step()
    total_last.step()
    clock.tick()
    small_total.step()
    total_first.step()
    total_last.step()
    clock.tick()
    small_total.step()
    small_total.step()
    total_first.halves()
    clock.defer()
    total_last.step()
    clock.tick()
    small_total.step()
    total_last.halves()
    summed = small_total.finish().reshape(-1)
    shares, at = [], 0
    for part in parts:
        piece = summed[at : at + part.size].reshape(part.shape)
        at += part.size
        width = part.shape[-1] // ring.fsdp
        shares.append(
            lax.dynamic_slice_in_dim(piece, fsdp_index * width, width, axis=part.ndim - 1)
        )
    total_w_in = jnp.zeros((PROJ, depth), f32)
    total_w_in = place_rows(total_w_in, total_w_gate.halves(), 0, INNER)
    total_w_in = place_rows(total_w_in, total_first.halves(), INNER, FIRST)
    total_w_in = place_rows(
        total_w_in, total_last.halves(), INNER + FIRST, PROJ - INNER - FIRST
    )
    total_w_in = total_w_in.T
    total_w_out = total_w_out.finish()
    return (
        output[None],
        hidden_grad[None],
        shares[0],
        total_w_in,
        shares[1],
        shares[2],
        shares[3],
        shares[4],
        shares[5],
        shares[6],
        total_w_out,
    )


def solution(mesh):
    placed = (
        P("fsdp", "seq", None),
        P("fsdp"),
        P("fsdp"),
        P("fsdp", None),
        P(None, "fsdp"),
        P("fsdp"),
        P("fsdp"),
        P("fsdp"),
        P("fsdp"),
        P("fsdp"),
        P("fsdp", None),
        P("fsdp", "seq", None),
    )
    return jax.shard_map(
        local,
        mesh=mesh,
        in_specs=placed,
        out_specs=(
            P("fsdp", "seq", None),
            P("fsdp", "seq", None),
            P("fsdp"),
            P("fsdp", None),
            P(None, "fsdp"),
            P("fsdp"),
            P("fsdp"),
            P("fsdp"),
            P("fsdp"),
            P("fsdp"),
            P("fsdp", None),
        ),
        check_vma=False,
    )
```

```python
import functools

import jax
import jax.numpy as jnp
from jax import lax
from jax.experimental import pallas as pl
from jax.experimental.pallas import tpu as pltpu
from jax.sharding import PartitionSpec as P

HEADS = 48
HEADDIM = 64
STATE = 128
CONV = 4
INNER = 3072
CHANNELS = 3328
PROJ = 6448
PLANES = 2
CORES = 2
FIRST = 1792

f32 = jnp.float32
bf16 = jnp.bfloat16
epsilon = 1e-05
scoped = 40 * 2**20
whole_vmem = 60 * 2**20
no_cost = pl.CostEstimate(flops=0, bytes_accessed=0, transcendentals=0)


class Ring:
    def __init__(self, seq, fsdp):
        self.seq, self.fsdp = seq, fsdp
        self.clock = None
        self.line, self.row = seq // PLANES, fsdp // CORES

    def send(self, block, move):
        route = []
        for s in range(self.seq):
            for f in range(self.fsdp):
                there = move(s // PLANES, s % PLANES, f // CORES, f % CORES)
                if there is None:
                    continue
                z, x, y, c = there
                route.append((s * self.fsdp + f, (z * PLANES + x) * self.fsdp + y * CORES + c))
        arrived = lax.ppermute(block, ("seq", "fsdp"), route)
        self.clock.sent(arrived)
        return arrived

    def core(self, block):
        return self.send(block, lambda z, x, y, c: (z, x, y, 1 - c))

    def plane(self, block):
        return self.send(block, lambda z, x, y, c: (z, 1 - x, y, c))

    def from_row(self, block, distance):
        return self.send(block, lambda z, x, y, c: (z, x, (y - distance) % self.row, c))

    def far(self, block, distance):
        return self.send(block, lambda z, x, y, c: (z ^ distance, x, y, c))

    def relative(self, block, d, e):
        if not d and not e:
            return block
        return self.send(
            block, lambda z, x, y, c: (z, x, (y - d) % self.row, (c + e) % CORES)
        )

    def relative_back(self, block, d, e):
        return self.relative(block, d, e)

    def next_block(self, block, distance):
        def move(z, x, y, c):
            s = z * PLANES + x + distance
            return (s // PLANES, s % PLANES, y, c) if 0 <= s < self.seq else None

        return self.send(block, move)


def rows_of(block, index, count):
    return lax.dynamic_slice_in_dim(block, index * count, count, axis=0)


def swapped(ring, distance):
    seq_index = lax.axis_index("seq")
    if distance == 0:
        return seq_index % PLANES, ring.plane
    bit = (seq_index // PLANES // distance) % 2
    return bit, lambda block: ring.far(block, distance)


def cube(ring):
    distances, distance = [0], 1
    while distance < ring.line:
        distances.append(distance)
        distance *= 2
    return distances


class Total:
    def __init__(self, ring, grad):
        self.ring, self.value, self.other, self.merge = ring, grad, None, None
        self.steps = [(True, d) for d in cube(ring)] + [(False, d) for d in reversed(cube(ring))]

    def settle(self):
        if self.merge is not None:
            value, other = self.ring.clock.now((self.value, self.other))
            self.value, self.merge = self.merge(value, other), None
        else:
            self.value = self.ring.clock.now(self.value)

    def step(self):
        if not self.steps:
            return
        self.settle()
        halves, distance = self.steps.pop(0)
        bit, send = swapped(self.ring, distance)
        if halves:
            half = self.value.shape[0] // 2
            self.other = send(rows_of(self.value, 1 - bit, half).astype(bf16))
            self.merge = lambda value, other: rows_of(value, bit, half) + other.astype(f32)
        else:
            self.value = self.value.astype(bf16)
            self.other = send(self.value)
            self.merge = lambda value, other: jnp.concatenate(
                [jnp.where(bit == 0, value, other), jnp.where(bit == 0, other, value)], axis=0
            )

    def finish(self):
        while self.steps:
            self.step()
        self.settle()
        return self.value.astype(f32)

    def halves(self):
        while self.steps:
            self.step()
        return self.value, self.other


class Clock:
    def __init__(self, value):
        self.token = value
        self.pending = []

    def sent(self, value):
        self.pending.append([1, value])

    def tick(self, *values):
        due = [value for ticks, value in self.pending if ticks == 1]
        out = lax.optimization_barrier((self.token,) + values + tuple(due))
        self.token = out[0]
        self.pending = [[ticks - 1, value] for ticks, value in self.pending if ticks > 1]
        return out[1 : 1 + len(values)]

    def defer(self, count=1, ticks=1):
        for entry in self.pending[len(self.pending) - count :]:
            entry[0] += ticks

    def now(self, value):
        return lax.optimization_barrier((value, self.token))[0]


class Spread:
    def __init__(self, ring, source, origin=0, whole_only=False):
        self.ring, self.source, self.origin, self.whole_only = ring, source, origin, whole_only
        block = self.block = source[origin:]
        self.quarter = -(-block.shape[0] // 64) * 16
        self.cut = -(-self.quarter // 32) * 16
        seq_index = lax.axis_index("seq")
        self.place = seq_index % 2 + 2 * ((seq_index // PLANES) % 2)
        self.arrived = []

    def start(self, index):
        return jnp.minimum((self.place ^ index) * self.quarter, self.block.shape[0] - self.quarter)

    def put(self, pieces):
        sides = (pieces,)
        if not self.whole_only:
            sides += ([self.ring.core(piece) for piece in pieces],)
        self.arrived.append(sides)

    def first(self, at_once=False):
        ring = self.ring
        mine = lax.dynamic_slice_in_dim(self.source, self.origin + self.start(0), self.quarter, axis=0)
        mine = mine if at_once else ring.clock.now(mine)
        self.mine = [ring.from_row(mine, d) for d in range(1, ring.row)]

    def second(self):
        ring = self.ring
        mine = [ring.clock.now(part) for part in self.mine]
        self.beside = [ring.plane(part) for part in mine]
        self.behind = [ring.far(part, 1) for part in mine]
        self.put(mine)

    def third(self):
        ring, cut = self.ring, self.cut
        beside = [ring.clock.now(part) for part in self.beside]
        behind = [ring.clock.now(part) for part in self.behind]
        self.corner = (
            [ring.plane(part[:cut]) for part in behind],
            [ring.far(part[cut:], 1) for part in beside],
        )
        self.put(beside)
        self.put(behind)

    def fourth(self):
        now = self.ring.clock.now
        self.put([now(part) for part in self.corner[0]])
        self.put([now(part) for part in self.corner[1]])

    def whole(self, near):
        found = {(0, 0): self.block, (0, 1): near}
        index = jnp.stack([self.place ^ k for k in range(4)]).astype(jnp.int32)
        for d in range(1, self.ring.row):
            sides = [[side[d - 1] for side in pieces] for pieces in zip(*self.arrived)]
            shards = laid(self.block, self.quarter, self.cut, index, sides)
            found[d, 0] = shards[0]
            found[d, 1] = self.ring.core(shards[0]) if self.whole_only else shards[1]
        return found


def sum_body(count, *refs):
    out_ref = refs[-1]
    total = None
    for left, right in zip(refs[:count], refs[count:-1]):
        term = lax.dot_general(
            left[...], right[...], (((0,), (0,)), ((), ())), preferred_element_type=f32
        )
        total = term if total is None else total + term
    out_ref[...] = total


def weight_grad(rows_all, columns_all, tile):
    keys = list(rows_all)
    tokens, rows = rows_all[keys[0]].shape
    width = columns_all[keys[0]].shape[1]
    return pl.pallas_call(
        functools.partial(sum_body, len(keys)),
        grid=(rows // tile,),
        in_specs=[pl.BlockSpec((tokens, tile), lambda i: (0, i))] * len(keys)
        + [pl.BlockSpec((tokens, width), lambda i: (0, 0))] * len(keys),
        out_specs=pl.BlockSpec((tile, width), lambda i: (i, 0)),
        out_shape=jax.ShapeDtypeStruct((rows, width), f32),
        name="weight_grad",
        cost_estimate=no_cost,
        compiler_params=pltpu.CompilerParams(vmem_limit_bytes=scoped),
    )(*[rows_all[key] for key in keys], *[columns_all[key] for key in keys])


def to_inner_body(tiles, place_ref, grad_ref, *refs):
    out_ref = refs[-1]
    shard = pl.program_id(0) // tiles
    for k, weight in enumerate(refs[:-1]):

        @pl.when(shard == k)
        def _(weight=weight):
            out_ref[...] = dot_last(grad_ref[...], weight[...])


def to_inner(grad, weights, places):
    tokens, width = grad.shape
    rows = weights[0].shape[0]
    tile = 384
    tiles = rows // tile
    return pl.pallas_call(
        functools.partial(to_inner_body, tiles),
        grid_spec=pltpu.PrefetchScalarGridSpec(
            num_scalar_prefetch=1,
            grid=(len(weights) * tiles,),
            in_specs=[pl.BlockSpec((tokens, width), lambda i, place: (0, 0))]
            + [
                pl.BlockSpec(
                    (tile, width), lambda i, place, k=k: (jnp.clip(i - k * tiles, 0, tiles - 1), 0)
                )
                for k in range(len(weights))
            ],
            out_specs=pl.BlockSpec(
                (tokens, tile), lambda i, place: (0, place[i // tiles] * tiles + i % tiles)
            ),
        ),
        out_shape=jax.ShapeDtypeStruct((tokens, rows * len(weights)), f32),
        name="to_inner",
        cost_estimate=no_cost,
        compiler_params=pltpu.CompilerParams(vmem_limit_bytes=scoped),
    )(places, grad, *weights)


def to_model_body(terms, gate_ref, tail_ref, *refs):
    out_ref = refs[-1]
    for k, shard in enumerate(terms):
        total = None
        for tail, column, array, row, count in shard:
            left = (tail_ref if tail else gate_ref)[:, column : column + count]
            term = jnp.dot(left, refs[array][row : row + count], preferred_element_type=f32)
            total = term if total is None else total + term
        out_ref[k] = total


def to_model(grad_gate, grad_tail, gate_weights, tail_weights):
    width = grad_tail.shape[1]
    rows = grad_gate.shape[1] // len(gate_weights[0])
    flat, terms = [], []

    def place(array):
        for k, held in enumerate(flat):
            if held is array:
                return k
        flat.append(array)
        return len(flat) - 1

    for pieces, (tail, start) in zip(gate_weights, tail_weights):
        shard = [(True, 0, place(tail), start, width)]
        if pieces[0][0] is tail:
            shard.append((False, 0, place(tail), 0, grad_gate.shape[1]))
        else:
            shard += [
                (False, at * rows, place(array), block * rows, rows)
                for at, (array, block) in enumerate(pieces)
            ]
        terms.append(shard)
    inside = pl.BlockSpec(memory_space=pltpu.VMEM)
    return pl.pallas_call(
        functools.partial(to_model_body, terms),
        in_specs=[inside] * (2 + len(flat)),
        out_specs=inside,
        out_shape=jax.ShapeDtypeStruct((len(terms), grad_gate.shape[0], flat[0].shape[1]), f32),
        name="to_model",
        cost_estimate=no_cost,
        compiler_params=pltpu.CompilerParams(vmem_limit_bytes=scoped),
    )(grad_gate, grad_tail, *flat)


def output_body(count, token_ref, *refs):
    out_ref = refs[-1]
    total = token_ref[...].astype(f32)
    for columns, weight in zip(refs[:count], refs[count:-1]):
        total = total + jnp.dot(columns[...], weight[...], preferred_element_type=f32)
    out_ref[...] = total.astype(bf16)


def output_rows(tokens, columns, weights):
    inside = pl.BlockSpec(memory_space=pltpu.VMEM)
    return pl.pallas_call(
        functools.partial(output_body, len(columns)),
        in_specs=[inside] * (1 + 2 * len(columns)),
        out_specs=inside,
        out_shape=jax.ShapeDtypeStruct(tokens.shape, bf16),
        name="output_rows",
        cost_estimate=no_cost,
        compiler_params=pltpu.CompilerParams(vmem_limit_bytes=scoped),
    )(tokens, *columns, *weights)


def laid_body(quarter, cut, index_ref, *refs):
    count = len(refs) // 6
    pieces, shards = refs[:-count], refs[-count:]
    for e, shard in enumerate(shards):
        own = pieces[e * 5 : e * 5 + 5]
        for piece, quarter_of, offset in zip(own, (0, 1, 2, 3, 3), (0, 0, 0, 0, cut)):
            start = jnp.minimum(index_ref[quarter_of] * quarter, shard.shape[0] - quarter)
            start = pl.multiple_of(start + offset, 16)
            shard[pl.ds(start, piece.shape[0]), :] = piece[...]


def laid(block, quarter, cut, index, sides):
    flat = [piece for side in sides for piece in side]
    inside = pl.BlockSpec(memory_space=pltpu.VMEM)
    return pl.pallas_call(
        functools.partial(laid_body, quarter, cut),
        grid_spec=pltpu.PrefetchScalarGridSpec(
            num_scalar_prefetch=1,
            grid=(),
            in_specs=[inside] * len(flat),
            out_specs=[inside] * len(sides),
        ),
        out_shape=[jax.ShapeDtypeStruct(block.shape, block.dtype)] * len(sides),
        name="laid",
        cost_estimate=no_cost,
        compiler_params=pltpu.CompilerParams(vmem_limit_bytes=scoped),
    )(index, *flat)


def project_body(count, *refs):
    out_ref = refs[-1]
    total = None
    for columns, weight in zip(refs[:count], refs[count:-1]):
        term = lax.dot_general(
            columns[...], weight[...], (((1,), (1,)), ((), ())), preferred_element_type=f32
        )
        total = term if total is None else total + term
    out_ref[...] = total.astype(out_ref.dtype)


def project(columns, weights, tile, width):
    count = len(columns)
    tokens, depth = columns[0].shape
    return pl.pallas_call(
        functools.partial(project_body, count),
        grid=(pl.cdiv(width, tile),),
        in_specs=[pl.BlockSpec((tokens, depth), lambda i: (0, 0))] * count
        + [pl.BlockSpec((tile, depth), lambda i, k=k: (i + k, 0)) for _, k in weights],
        out_specs=pl.BlockSpec((tokens, tile), lambda i: (0, i)),
        out_shape=jax.ShapeDtypeStruct((tokens, width), bf16),
        name="project",
        cost_estimate=no_cost,
        compiler_params=pltpu.CompilerParams(vmem_limit_bytes=scoped),
    )(*columns, *[array for array, _ in weights])


class Pieces:
    def __init__(self, ring, block, count=1):
        self.ring, self.block = ring, block
        self.rows = block.shape[0] // count
        self.parts = []

    def near(self):
        self.beside = self.ring.core(self.ring.clock.now(self.block))

    def send(self, later=0):
        clock = self.ring.clock
        at = len(self.parts) * self.rows
        piece = clock.now(self.block[at : at + self.rows])
        self.parts.append([self.ring.from_row(piece, d) for d in range(1, self.ring.row)])
        clock.defer(self.ring.row - 1, later)

    def pass_on(self, at):
        far = [self.ring.clock.now(piece) for piece in self.parts[at]]
        self.parts[at] = [(piece, self.ring.core(piece)) for piece in far]

    def pieces(self, own, near):
        count = len(self.parts)
        found = {
            (0, 0): [(own, at) for at in range(count)],
            (0, 1): [(near, at) for at in range(count)],
        }
        for d in range(1, self.ring.row):
            for e in range(CORES):
                found[d, e] = [(part[d - 1][e], 0) for part in self.parts]
        return found

    def whole(self):
        found = {(0, 0): self.block, (0, 1): self.beside}
        for d in range(1, self.ring.row):
            found[d, 0] = self.ring.clock.now(self.parts[0][d - 1])
            found[d, 1] = self.ring.core(found[d, 0])
        return found


def gather_rows(ring, block):
    found = {}
    for d in range(ring.row):
        found[d, 0] = block if d == 0 else ring.from_row(block, d)
        found[d, 1] = ring.core(found[d, 0])
    return found


def places(ring):
    index = lax.axis_index("fsdp")
    y, c = index // CORES, index % CORES
    return {
        (d, e): ((y + d) % ring.row) * CORES + (c + e) % CORES
        for d in range(ring.row)
        for e in range(CORES)
    }


def columns_for(ring, block):
    index = lax.axis_index("fsdp")
    y, c = index // CORES, index % CORES
    width = block.shape[1] // ring.fsdp
    return {
        (d, e): lax.dynamic_slice_in_dim(
            block, (((y - d) % ring.row) * CORES + (c + e) % CORES) * width, width, axis=1
        )
        for d in range(ring.row)
        for e in range(CORES)
    }


def trade_columns(ring, pieces):
    return {key: ring.relative_back(piece, *key) for key, piece in pieces.items()}


class SmallSum:
    def __init__(self, ring, vector):
        self.ring, self.value = ring, vector
        self.steps = ["core", "row"] + cube(ring)

    def step(self):
        if not self.steps:
            return
        kind = self.steps.pop(0)
        vector = self.ring.clock.now(self.value)
        if kind == "core":
            self.value = vector + self.ring.core(vector)
        elif kind == "row":
            self.value = sum([self.ring.from_row(vector, d) for d in range(1, self.ring.row)], vector)
        else:
            self.value = vector + swapped(self.ring, kind)[1](vector)

    def finish(self):
        while self.steps:
            self.step()
        return self.value


def head_rows(ring):
    part = INNER // ring.seq
    run = HEADDIM
    while part % run:
        run //= 2
    return part, run


def spread_factors(ring, through):
    part, run = head_rows(ring)
    factor = jnp.repeat(through, HEADDIM // run).reshape(ring.seq, part // run)
    factor = jnp.pad(factor, ((0, 0), (0, 8 - part // run)))
    return jnp.broadcast_to(factor[:, :, None], (ring.seq, 8, STATE))


def carried_body(reverse, run, blocks_ref, factor_ref, out_ref):
    count, part = out_ref.shape[0], out_ref.shape[1]
    state = jnp.zeros((part, STATE), f32)
    for k in reversed(range(count)) if reverse else range(count):
        out_ref[k] = state.astype(bf16)
        factor = factor_ref[k]
        spread = [jnp.broadcast_to(factor[j : j + 1], (run, STATE)) for j in range(part // run)]
        state = jnp.concatenate(spread, axis=0) * state + blocks_ref[k, :part]


def carried(ring, blocks, factor, reverse):
    part, run = head_rows(ring)
    return pl.pallas_call(
        functools.partial(carried_body, reverse, run),
        out_shape=jax.ShapeDtypeStruct((ring.seq, part, STATE), bf16),
        name="carried",
        cost_estimate=no_cost,
        compiler_params=pltpu.CompilerParams(vmem_limit_bytes=scoped),
    )(blocks, factor)


def returned(ring, states):
    states = lax.all_to_all(states, "seq", 0, 0, tiled=True)
    return states.reshape(HEADS, HEADDIM, STATE)


def place_rows(whole, sides, start, rows):
    mine, other = sides
    first = (lax.axis_index("seq") % PLANES) == 0
    half = mine.shape[0]
    low = jnp.where(first, mine, other).astype(f32)
    high = jnp.where(first, other, mine)[: rows - half].astype(f32)
    whole = lax.dynamic_update_slice_in_dim(whole, low, start, axis=0)
    return lax.dynamic_update_slice_in_dim(whole, high, start + half, axis=0)


def steps_body(dt_ref, bias_ref, rate_ref, cum_ref, weigh_ref, decay_ref, cum_rows, step_rows, through_ref):
    raw = dt_ref[...].astype(f32) + bias_ref[...]
    step = jnp.maximum(raw, 0.0) + jnp.log1p(jnp.exp(-jnp.abs(raw)))
    tokens = step.shape[0]
    row = lax.broadcasted_iota(jnp.int32, step.shape, 0)
    cum = step * -jnp.exp(rate_ref[...])
    distance = 1
    while distance < tokens:
        cum = cum + jnp.where(row >= distance, pltpu.roll(cum, distance, 0), 0.0)
        distance *= 2
    end = cum[tokens - 1 :]
    cum_ref[...] = cum
    weigh_ref[...] = jnp.exp(end - cum) * step
    decay_ref[...] = jnp.exp(cum)
    cum_rows[...] = cum.T[:HEADS]
    step_rows[...] = step.T[:HEADS]
    through_ref[...] = jnp.exp(end)


def steps(projected, bias, rate):
    tokens = projected.shape[0]
    row = pl.BlockSpec((1, STATE), lambda i: (0, 0))
    by_token = pl.BlockSpec((tokens, STATE), lambda i: (0, 0))
    by_head = pl.BlockSpec((HEADS, tokens), lambda i: (0, 0))
    pad = lambda v: jnp.pad(v, (0, STATE - HEADS))[None]
    return pl.pallas_call(
        steps_body,
        grid=(1,),
        in_specs=[pl.BlockSpec((tokens, STATE), lambda i: (0, CHANNELS // STATE)), row, row],
        out_specs=[by_token] * 3 + [by_head] * 2 + [row],
        out_shape=[jax.ShapeDtypeStruct((tokens, STATE), f32)] * 3
        + [jax.ShapeDtypeStruct((HEADS, tokens), f32)] * 2
        + [jax.ShapeDtypeStruct((1, STATE), f32)],
        name="steps",
        cost_estimate=no_cost,
        compiler_params=pltpu.CompilerParams(vmem_limit_bytes=scoped),
    )(projected, pad(bias), pad(rate))


def steps_back_body(
    dt_ref, bias_ref, rate_ref, step_ref, cum_ref, grad_step_ref, grad_cum_ref, factor_ref, crossed_ref,
    grad_ref, bias_grad_ref, rate_grad_ref,
):
    step, cum, factor = step_ref[...], cum_ref[...], factor_ref[...]
    tokens = step.shape[1]
    lane = lax.broadcasted_iota(jnp.int32, step.shape, 1)
    end = cum[:, tokens - 1 :]
    to_end = jnp.exp(end - cum)
    tail = factor * step * to_end
    grad_end = jnp.sum(tail, axis=1, keepdims=True) + jnp.exp(end) * jnp.sum(
        crossed_ref[...], axis=1, keepdims=True
    )
    total = grad_cum_ref[...] - tail + jnp.where(lane == tokens - 1, grad_end, 0.0)
    distance = 1
    while distance < tokens:
        moved = pltpu.roll(total, tokens - distance, 1)
        total = total + jnp.where(lane < tokens - distance, moved, 0.0)
        distance *= 2
    rate = -jnp.exp(rate_ref[...])
    rate_grad_ref[...] = rate * jnp.sum(total * step, axis=1, keepdims=True)
    raw = dt_ref[...].astype(f32).T[:HEADS] + bias_ref[...]
    grad = (grad_step_ref[...] + factor * to_end + total * rate) * jax.nn.sigmoid(raw)
    bias_grad_ref[...] = jnp.sum(grad, axis=1, keepdims=True)
    none = jnp.zeros((STATE - HEADS, tokens), f32)
    grad_ref[...] = jnp.concatenate([grad, none], axis=0).T.astype(bf16)


def steps_back(projected, bias, rate, step_rows, cum_rows, grad_step, grad_cum, factor, crossed):
    tokens = projected.shape[0]
    column = pl.BlockSpec((HEADS, 1), lambda i: (0, 0))
    by_head = pl.BlockSpec((HEADS, tokens), lambda i: (0, 0))
    return pl.pallas_call(
        steps_back_body,
        grid=(1,),
        in_specs=[pl.BlockSpec((tokens, STATE), lambda i: (0, CHANNELS // STATE)), column, column]
        + [by_head] * 5
        + [pl.BlockSpec((HEADS, STATE), lambda i: (0, 0))],
        out_specs=[pl.BlockSpec((tokens, STATE), lambda i: (0, 0)), column, column],
        out_shape=[
            jax.ShapeDtypeStruct((tokens, STATE), bf16),
            jax.ShapeDtypeStruct((HEADS, 1), f32),
            jax.ShapeDtypeStruct((HEADS, 1), f32),
        ],
        name="steps_back",
        cost_estimate=no_cost,
        compiler_params=pltpu.CompilerParams(vmem_limit_bytes=scoped),
    )(
        projected, bias[:, None], rate[:, None], step_rows, cum_rows, grad_step, grad_cum, factor,
        crossed,
    )


def group_columns(wide_ref, group, heads):
    shift = lax.rem(STATE - heads * group, STATE)
    return pltpu.roll(wide_ref[...], shift, 1)[:, :heads]


def keep_columns(wide_ref, at, columns):
    wide = wide_ref[...]
    lane = lax.broadcasted_iota(jnp.int32, wide.shape, 1)
    for k, column in enumerate(columns):
        wide = jnp.where(lane == at + k, column, wide)
    wide_ref[...] = wide


def along(column_pair):
    lane = lax.broadcasted_iota(jnp.int32, (column_pair.shape[0], 2 * HEADDIM), 1)
    return jnp.where(lane < HEADDIM, column_pair[:, :1], column_pair[:, 1:2])


def conv_sum(edge, rows, taps, shift):
    window = jnp.concatenate([edge, rows], axis=0)
    total = shift
    for k in range(CONV):
        moved = window if k == CONV - 1 else pltpu.roll(window, CONV - 1 - k, 0)
        total = total + taps[k : k + 1] * moved[8:]
    return total


def enter_body(part, proj_ref, edge_ref, taps_ref, shift_ref, weigh_ref, factor_ref, low_ref, fresh_ref):
    def conv(at, width):
        columns = slice(at, at + width)
        total = conv_sum(
            edge_ref[:, columns].astype(f32),
            proj_ref[:, columns].astype(f32),
            taps_ref[:, columns],
            shift_ref[:, columns],
        )
        low = (total * jax.nn.sigmoid(total)).astype(bf16)
        low_ref[:, columns] = low
        return low

    proj_b = conv(INNER, 2 * STATE)[:, :STATE]
    fresh_ref[:, part:] = factor_ref[...]
    for at in range(0, INNER, 2 * HEADDIM):
        low = conv(at, 2 * HEADDIM)
        head = at // HEADDIM
        weighted = (low.astype(f32) * along(weigh_ref[:, head : head + 2])).astype(bf16)
        fresh = lax.dot_general(
            weighted, proj_b, (((0,), (0,)), ((), ())), preferred_element_type=f32
        )
        row = at
        while row < at + 2 * HEADDIM:
            device, offset = row // part, row % part
            count = min(part - offset, at + 2 * HEADDIM - row)
            fresh_ref[device, offset : offset + count] = fresh[row - at : row - at + count]
            row += count


def enter(ring, projected, edge, taps, shift, weigh, factor):
    part, _ = head_rows(ring)
    return pl.pallas_call(
        functools.partial(enter_body, part),
        out_shape=[
            jax.ShapeDtypeStruct((projected.shape[0], CHANNELS), bf16),
            jax.ShapeDtypeStruct((ring.seq, part + 8, STATE), f32),
        ],
        name="enter",
        cost_estimate=no_cost,
        compiler_params=pltpu.CompilerParams(vmem_limit_bytes=scoped),
    )(projected, edge, taps, shift[None], weigh, factor)


def pairs_along(columns):
    return jnp.concatenate(
        [along(columns[:, i : i + 2]) for i in range(0, columns.shape[1], 2)], axis=1
    )


def turn_body(
    base_ref, incoming_ref, c_ref, decay_ref, grad_ref, gain_ref, *refs,
):
    count = len(refs) - 10
    gate_refs = refs[:count]
    (
    mixed_ref, grad_y_ref, grad_gate_ref, grad_reach_ref, direct_ref, gain_grad_ref,
    mixer, grads, squares, products,
    ) = refs[count:]
    later, j = pl.program_id(0), pl.program_id(1)
    gate = gate_refs[0][...]
    for k in range(1, count):
        gate = jnp.where(j * count >= k * pl.num_programs(1), gate_refs[k][...], gate)
    gate = gate.astype(f32)
    sig = jax.nn.sigmoid(gate)
    silu = gate * sig
    gain = gain_ref[...]

    @pl.when((later == 0) & (j == 0))
    def _():
        squares[...] = jnp.zeros_like(squares)
        products[...] = jnp.zeros_like(products)

    @pl.when(later == 0)
    def _():
        reached = lax.dot_general(
            c_ref[...], incoming_ref[...], (((1,), (1,)), ((), ())), preferred_element_type=f32
        )
        ssd = base_ref[...] + pairs_along(group_columns(decay_ref, j, gain.shape[1] // HEADDIM)) * reached
        gated = ssd * silu
        mixer[j] = ssd
        grads[j] = grad_ref[...]
        squares[...] += jnp.sum(gated * gated, axis=1, keepdims=True)
        products[...] += jnp.sum(gated * grad_ref[...] * gain, axis=1, keepdims=True)

    @pl.when(later == 1)
    def _():
        scale = lax.rsqrt(squares[...] / INNER + epsilon)
        ssd = mixer[j]
        grad = grads[j]
        normal = ssd * silu * scale
        mixed_ref[...] = (normal * gain).astype(bf16)
        gain_grad_ref[...] = jnp.sum(grad * normal, axis=0, keepdims=True)
        grad_gated = scale * (grad * gain - normal * (scale * products[...] / INNER))
        grad_y = (grad_gated * silu).astype(bf16)
        grad_y_ref[...] = grad_y
        grad_gate_ref[...] = (grad_gated * ssd * (sig + silu * (1.0 - sig))).astype(bf16)
        grad_reach = (grad_y.astype(f32) * pairs_along(group_columns(decay_ref, j, gain.shape[1] // HEADDIM))).astype(bf16)
        grad_reach_ref[...] = grad_reach
        direct_ref[...] = lax.dot_general(
            grad_reach, c_ref[...], (((0,), (0,)), ((), ())), preferred_element_type=f32
        )


def later_or_same(tokens):
    t = lax.broadcasted_iota(jnp.int32, (tokens, tokens), 0)
    return t >= lax.broadcasted_iota(jnp.int32, (tokens, tokens), 1)


def dot_last(a, b):
    return lax.dot_general(a, b, (((1,), (1,)), ((), ())), preferred_element_type=f32)


def dot_first(a, b):
    return lax.dot_general(a, b, (((0,), (0,)), ((), ())), preferred_element_type=f32)


def inside_body(x_ref, b_ref, c_ref, cum_ref, cum_rows_ref, step_rows_ref, skip_ref, out_ref, scores):
    tokens = x_ref.shape[0]

    @pl.when(pl.program_id(0) == 0)
    def _():
        table = dot_last(c_ref[...], b_ref[...])
        scores[...] = jnp.where(later_or_same(tokens), table, 0.0)

    x = x_ref[...]
    j = pl.program_id(0)
    same = later_or_same(tokens)
    cum = group_columns(cum_ref, j, 2)
    parts = []
    for head in range(2):
        row = pl.ds(2 * j + head, 1)
        exponent = cum[:, head : head + 1] - cum_rows_ref[row, :]
        decay = jnp.exp(jnp.where(same, exponent, 0.0))
        mixing = (scores[...] * decay * step_rows_ref[row, :]).astype(bf16)
        parts.append(jnp.dot(mixing, x, preferred_element_type=f32))
    first = lax.broadcasted_iota(jnp.int32, x.shape, 1) < HEADDIM
    out_ref[...] = jnp.where(first, parts[0], parts[1]) + skip_ref[...] * x.astype(f32)


def pair_specs(tokens):
    columns = pl.BlockSpec((tokens, 2 * HEADDIM), lambda j: (0, j))
    by_token = pl.BlockSpec((tokens, STATE), lambda j: (0, 0))
    by_head = pl.BlockSpec((HEADS, tokens), lambda j: (0, 0))
    row = pl.BlockSpec((1, 2 * HEADDIM), lambda j: (0, j))
    proj_b = pl.BlockSpec((tokens, STATE), lambda j: (0, INNER // STATE))
    proj_c = pl.BlockSpec((tokens, STATE), lambda j: (0, INNER // STATE + 1))
    return columns, by_token, by_head, row, proj_b, proj_c


def inside(conv_low, cum_pairs, cum_rows, step_rows, skip_row):
    tokens = conv_low.shape[0]
    columns, by_token, by_head, row, proj_b, proj_c = pair_specs(tokens)
    return pl.pallas_call(
        inside_body,
        grid=(HEADS // 2,),
        in_specs=[columns, proj_b, proj_c, by_token, by_head, by_head, row],
        out_specs=columns,
        out_shape=jax.ShapeDtypeStruct((tokens, INNER), f32),
        scratch_shapes=[pltpu.VMEM((tokens, tokens), f32)],
        name="inside",
        cost_estimate=no_cost,
        compiler_params=pltpu.CompilerParams(vmem_limit_bytes=scoped),
    )(conv_low, conv_low, conv_low, cum_pairs, cum_rows, step_rows, skip_row)


def inside_back_body(
    y_ref, reach_ref, x_ref, b_ref, c_ref, incoming_ref, cum_ref, cum_rows_ref, step_rows_ref, skip_ref,
    x_out, b_out, c_out, step_out, cum_out, skip_out,
    scores, grad_scores, wide_sums,
):
    tokens = x_ref.shape[0]
    j = pl.program_id(0)

    @pl.when(j == 0)
    def _():
        table = dot_last(c_ref[...], b_ref[...])
        scores[...] = jnp.where(later_or_same(tokens), table, 0.0)
        grad_scores[...] = jnp.zeros_like(grad_scores)
        c_out[...] = jnp.zeros_like(c_out)

    x, y = x_ref[...], y_ref[...]
    wide = y.astype(f32)
    incoming = incoming_ref[...]
    reached = wide * dot_last(c_ref[...], incoming)
    c_out[...] += jnp.dot(reach_ref[...], incoming, preferred_element_type=f32)
    skip_out[...] = jnp.sum(wide * x.astype(f32), axis=0, keepdims=True)
    first = lax.broadcasted_iota(jnp.int32, x.shape, 1) < HEADDIM
    wide_cum = group_columns(cum_ref, j, 2)
    middle = tokens // 2
    same = later_or_same(middle)
    parts, sums = [], []
    totals = [0.0, 0.0, 0.0]
    for head in range(2):
        row = pl.ds(2 * j + head, 1)
        steps_row, cum_row = step_rows_ref[row, :], cum_rows_ref[row, :]
        own = jnp.where(first == (head == 0), y, jnp.zeros_like(y))
        mine = jnp.sum(
            reached[:, head * HEADDIM : (head + 1) * HEADDIM], axis=1, keepdims=True
        ) * jnp.exp(wide_cum[:, head : head + 1])
        by_row, by_column, given = [0.0, 0.0], [0.0, 0.0], [0.0, 0.0]
        for k, (late, early) in enumerate(((0, 0), (1, 0), (1, 1))):
            rows = slice(late * middle, (late + 1) * middle)
            columns = slice(early * middle, (early + 1) * middle)
            step = steps_row[:, columns]
            exponent = wide_cum[rows, head : head + 1] - cum_row[:, columns]
            decay = jnp.exp(jnp.where(same, exponent, 0.0) if late == early else exponent)
            both = scores[rows, columns] * decay
            grad_mix = dot_last(own[rows], x[columns])
            totals[k] = totals[k] + grad_mix * (decay * step)
            by_source = grad_mix * both
            by_column[early] = by_column[early] + jnp.sum(by_source, axis=0, keepdims=True)
            by_row[late] = by_row[late] + jnp.sum(by_source * step, axis=1, keepdims=True)
            given[early] = given[early] + dot_first((both * step).astype(bf16), y[rows])
        step_out[row, :] = jnp.concatenate(by_column, axis=1)
        sums.append(jnp.concatenate(by_row, axis=0) + mine)
        parts.append(jnp.concatenate(given, axis=0))
    for total, (late, early) in zip(totals, ((0, 0), (1, 0), (1, 1))):
        grad_scores[late * middle : (late + 1) * middle, early * middle : (early + 1) * middle] += total
    keep_columns(wide_sums, 2 * j, sums)
    x_out[...] = jnp.where(first, parts[0], parts[1]) + skip_ref[...] * wide

    @pl.when(j == pl.num_programs(0) - 1)
    def _():
        grad = jnp.where(later_or_same(tokens), grad_scores[...], 0.0).astype(bf16)
        c_out[...] += jnp.dot(grad, b_ref[...], preferred_element_type=f32)
        b_out[...] = dot_first(grad, c_ref[...])
        cum_out[...] = wide_sums[...].T[:HEADS] - step_out[...] * step_rows_ref[...]


def inside_back(grad_y, grad_reach, conv_low, incoming, cum_pairs, cum_rows, step_rows, skip_row):
    tokens = conv_low.shape[0]
    columns, by_token, by_head, row, proj_b, proj_c = pair_specs(tokens)
    whole = pl.BlockSpec((tokens, STATE), lambda j: (0, 0))
    pairs = HEADS // 2
    return pl.pallas_call(
        inside_back_body,
        grid=(pairs,),
        in_specs=[columns, columns, columns, proj_b, proj_c]
        + [pl.BlockSpec((2 * HEADDIM, STATE), lambda j: (j, 0)), by_token, by_head, by_head, row],
        out_specs=[columns, whole, whole, by_head, by_head, row],
        out_shape=[
            jax.ShapeDtypeStruct((tokens, INNER), f32),
            jax.ShapeDtypeStruct((tokens, STATE), f32),
            jax.ShapeDtypeStruct((tokens, STATE), f32),
            jax.ShapeDtypeStruct((HEADS, tokens), f32),
            jax.ShapeDtypeStruct((HEADS, tokens), f32),
            jax.ShapeDtypeStruct((1, INNER), f32),
        ],
        scratch_shapes=[
            pltpu.VMEM((tokens, tokens), f32),
            pltpu.VMEM((tokens, tokens), f32),
            pltpu.VMEM((tokens, STATE), f32),
        ],
        name="inside_back",
        cost_estimate=no_cost,
        compiler_params=pltpu.CompilerParams(vmem_limit_bytes=scoped),
    )(
        grad_y, grad_reach, conv_low, conv_low, conv_low, incoming, cum_pairs, cum_rows, step_rows,
        skip_row,
    )


def turn(base, incoming, proj_c, decay, gate_parts, grad_mixed, gain):
    tokens, heads = base.shape[0], 8
    width = heads * HEADDIM
    groups = INNER // width
    share = groups // len(gate_parts)
    once = lambda p, j: (0, jnp.where(p == 0, j, groups - 1))
    last = lambda p, j: (0, jnp.where(p == 0, 0, j))
    wide = jax.ShapeDtypeStruct((tokens, INNER), bf16)
    return pl.pallas_call(
        turn_body,
        grid=(2, groups),
        in_specs=[
            pl.BlockSpec((tokens, width), once),
            pl.BlockSpec((width, STATE), lambda p, j: (jnp.where(p == 0, j, groups - 1), 0)),
            pl.BlockSpec((tokens, STATE), lambda p, j: (0, 0)),
            pl.BlockSpec((tokens, STATE), lambda p, j: (0, 0)),
            pl.BlockSpec((tokens, width), once),
            pl.BlockSpec((1, width), lambda p, j: (0, j)),
        ]
        + [
            pl.BlockSpec(
                (tokens, width), lambda p, j, k=k: (0, jnp.clip(j - k * share, 0, share - 1))
            )
            for k in range(len(gate_parts))
        ],
        out_specs=[pl.BlockSpec((tokens, width), last)] * 4
        + [
            pl.BlockSpec((width, STATE), lambda p, j: (jnp.where(p == 0, 0, j), 0)),
            pl.BlockSpec((1, width), last),
        ],
        out_shape=[wide] * 4
        + [jax.ShapeDtypeStruct((INNER, STATE), f32), jax.ShapeDtypeStruct((1, INNER), f32)],
        scratch_shapes=[
            pltpu.VMEM((groups, tokens, width), f32),
            pltpu.VMEM((groups, tokens, width), f32),
            pltpu.VMEM((tokens, 1), f32),
            pltpu.VMEM((tokens, 1), f32),
        ],
        name="turn",
        cost_estimate=no_cost,
        compiler_params=pltpu.CompilerParams(vmem_limit_bytes=whole_vmem),
    )(base, incoming, proj_c, decay, grad_mixed, gain[None], *gate_parts)


def ahead(rows, count, distance):
    return (pltpu.roll(rows, rows.shape[0] - distance, 0) if distance else rows)[:count]


def leave_body(
    steps, proj_ref, edge_ref, taps_ref, shift_ref, low_ref, part_ref, fresh_ref, incoming_ref, b_ref,
    weigh_ref, b_part_ref, c_part_ref,
    grad_ref, grad_more_ref, first_ref, last_ref, taps_grad_ref, shift_grad_ref, factor_ref, crossed_ref,
    b_total, wide_factor,
):
    j = pl.program_id(0)

    def conv_back(grad_out):
        rows = proj_ref[...].astype(f32)
        window = jnp.concatenate([edge_ref[...].astype(f32), rows], axis=0)
        taps = taps_ref[...]
        moved = [
            (pltpu.roll(window, CONV - 1 - k, 0) if k < CONV - 1 else window)[8:]
            for k in range(CONV)
        ]
        total = shift_ref[...]
        for k in range(CONV):
            total = total + taps[k : k + 1] * moved[k]
        sig = jax.nn.sigmoid(total)
        grad = grad_out * (sig * (1.0 + total * (1.0 - sig)))
        shift_grad_ref[...] = jnp.sum(grad, axis=0, keepdims=True)
        taps_grad_ref[...] = jnp.concatenate(
            [jnp.sum(grad * part, axis=0, keepdims=True) for part in moved], axis=0
        )
        none = jnp.zeros((8, grad.shape[1]), f32)
        after_it = jnp.concatenate([grad, none], axis=0)
        before_it = jnp.concatenate([none, grad[:8]], axis=0)
        inner, outer = 0.0, 0.0
        for k in range(CONV):
            tap = taps[k : k + 1]
            inner = inner + tap * ahead(after_it, grad.shape[0], CONV - 1 - k)
            outer = outer + tap * ahead(before_it, 8, CONV - 1 - k)
        cut = FIRST // grad.shape[1]

        @pl.when(j < cut)
        def _():
            grad_ref[...] = inner.astype(bf16)

        @pl.when(j >= cut)
        def _():
            grad_more_ref[...] = inner.astype(bf16)

        last_ref[...] = inner[grad.shape[0] - 8 :]
        first_ref[...] = outer

    @pl.when(j == 0)
    def _():
        b_total[...] = b_part_ref[...]

    @pl.when(j < steps)
    def _():
        fresh = fresh_ref[...]
        x = low_ref[...].astype(f32)
        heads = x.shape[1] // HEADDIM
        weigh = pairs_along(group_columns(weigh_ref, j, heads))
        grad_weighted = lax.dot_general(
            b_ref[...], fresh, (((1,), (1,)), ((), ())), preferred_element_type=f32
        )
        weighted = (x * weigh).astype(bf16)
        b_total[...] += jnp.dot(weighted, fresh, preferred_element_type=f32)
        product = grad_weighted * x
        keep_columns(
            wide_factor,
            heads * j,
            [
                jnp.sum(product[:, i * HEADDIM : (i + 1) * HEADDIM], axis=1, keepdims=True)
                for i in range(heads)
            ],
        )
        both = fresh.astype(f32) * incoming_ref[...].astype(f32)
        for i in range(heads):
            row = pl.ds(heads * j + i, 1)
            crossed_ref[row, :] = jnp.sum(
                both[i * HEADDIM : (i + 1) * HEADDIM], axis=0, keepdims=True
            )
        conv_back(part_ref[...] + grad_weighted * weigh)

    @pl.when(j == steps)
    def _():
        factor_ref[...] = wide_factor[...].T[:HEADS]
        conv_back(jnp.concatenate([b_total[...], c_part_ref[...]], axis=1))


def leave(projected, edge, taps, shift, conv_low, part, grad_fresh, incoming, weigh, b_part, c_part):
    tokens, heads = part.shape[0], 4
    width = heads * HEADDIM
    steps = INNER // width
    cut = FIRST // width
    inside = lambda j: jnp.minimum(j, steps - 1)
    block = lambda rows: pl.BlockSpec((rows, width), lambda j: (0, j))
    whole = lambda rows: pl.BlockSpec((rows, STATE), lambda j: (0, 0))
    state = pl.BlockSpec((width, STATE), lambda j: (inside(j), 0))
    return pl.pallas_call(
        functools.partial(leave_body, steps),
        grid=(steps + 1,),
        in_specs=[
            block(tokens),
            block(8),
            block(CONV),
            block(1),
            block(tokens),
            pl.BlockSpec((tokens, width), lambda j: (0, inside(j))),
            state,
            state,
            pl.BlockSpec((tokens, STATE), lambda j: (0, INNER // STATE)),
            whole(tokens),
            whole(tokens),
            whole(tokens),
        ],
        out_specs=[
            pl.BlockSpec((tokens, width), lambda j: (0, jnp.minimum(j, cut - 1))),
            pl.BlockSpec((tokens, width), lambda j: (0, jnp.maximum(j - cut, 0))),
            block(8),
            block(8),
            block(CONV),
            block(1),
            pl.BlockSpec((HEADS, tokens), lambda j: (0, 0)),
            whole(HEADS),
        ],
        out_shape=[
            jax.ShapeDtypeStruct((tokens, FIRST), bf16),
            jax.ShapeDtypeStruct((tokens, CHANNELS - FIRST), bf16),
            jax.ShapeDtypeStruct((8, CHANNELS), f32),
            jax.ShapeDtypeStruct((8, CHANNELS), f32),
            jax.ShapeDtypeStruct((CONV, CHANNELS), f32),
            jax.ShapeDtypeStruct((1, CHANNELS), f32),
            jax.ShapeDtypeStruct((HEADS, tokens), f32),
            jax.ShapeDtypeStruct((HEADS, STATE), f32),
        ],
        scratch_shapes=[pltpu.VMEM((tokens, STATE), f32), pltpu.VMEM((tokens, STATE), f32)],
        name="leave",
        cost_estimate=no_cost,
        compiler_params=pltpu.CompilerParams(vmem_limit_bytes=whole_vmem),
    )(
        projected, edge, taps, shift[None], conv_low, part, grad_fresh, incoming, conv_low,
        weigh, b_part, c_part,
    )


def rms_scale(values, gain):
    return values * lax.rsqrt(jnp.mean(values * values, axis=-1, keepdims=True) + epsilon) * gain


def pack(arrays):
    flat = jnp.concatenate([a.reshape(-1) for a in arrays])
    pad = -flat.shape[0] % 1024
    return jnp.pad(flat, (0, pad)).reshape(-1, 128)


def local(
    hidden,
    lengths,
    norm_gain,
    in_weight,
    conv_weight,
    conv_bias,
    dt_bias,
    a_log,
    skip_d,
    gate_gain,
    out_weight,
    out_grad,
):
    ring = Ring(lax.axis_size("seq"), lax.axis_size("fsdp"))
    ring.clock = clock = Clock(hidden[0, :8, :128])
    _, row_count, model_width = hidden.shape
    fsdp_index = lax.axis_index("fsdp")
    where = places(ring)
    tokens = hidden[0].astype(f32)

    small = [norm_gain, conv_weight, conv_bias, dt_bias, a_log, skip_d, gate_gain]
    in_rows = in_weight.T
    shared = Spread(ring, in_rows, INNER)
    shared.first(at_once=True)
    near_rows = ring.core(in_rows)
    packed = pack(small)
    spread = jnp.zeros((ring.fsdp,) + packed.shape, bf16)
    for (d, e), place in where.items():
        block = ring.relative(packed, d, e)
        spread = lax.dynamic_update_slice_in_dim(spread, block[None], place, axis=0)
    clock.defer(ring.fsdp - 1)
    spread = spread.reshape(ring.fsdp, -1)
    whole_small, at = [], 0
    for part in small:
        piece = spread[:, at : at + part.size]
        at += part.size
        if part.ndim == 2:
            piece = piece.reshape((ring.fsdp,) + part.shape).transpose(1, 0, 2)
            whole_small.append(piece.reshape(part.shape[0], -1).astype(f32))
        else:
            whole_small.append(piece.reshape(-1).astype(f32))
    gain_norm, conv_taps, conv_shift, step_bias, rate_log, skip_gain, gain_gate = whole_small

    gate_pieces = Pieces(ring, in_rows[:INNER], 3)
    out_spread = Spread(ring, out_weight, 0, whole_only=True)
    clock.tick()
    shared.second()
    out_spread.first()
    clock.tick()
    shared.third()
    gate_pieces.send(later=1)
    clock.tick()
    shared.fourth()
    gate_pieces.send(later=3)
    out_spread.second()
    clock.tick()
    tile = 768
    weight_conv = {key: (array, 0) for key, array in shared.whole(near_rows).items()}
    weight_conv[0, 0] = (in_rows, INNER // tile)
    weight_conv[0, 1] = (near_rows, INNER // tile)

    position = lax.axis_index("seq") * row_count + lax.broadcasted_iota(
        jnp.int32, (row_count, 1), 0
    )
    grad_out = jnp.where(position < lengths[0], out_grad[0], jnp.zeros_like(out_grad[0]))

    normed, pull_norm = jax.vjp(rms_scale, tokens, gain_norm)
    normed = normed.astype(bf16)
    depth = in_weight.shape[0]

    normed_columns = [
        lax.dynamic_slice_in_dim(normed, place * depth, depth, axis=1) for place in where.values()
    ]
    normed_for = columns_for(ring, normed)
    projected = project(normed_columns, list(weight_conv.values()), tile, PROJ - INNER)
    (projected,) = clock.tick(projected)
    edge_rows = ring.next_block(projected[row_count - 8 :, :CHANNELS], 1)
    near_out = ring.core(clock.now(out_weight))
    clock.defer()
    cum, weigh, decay, cum_rows, step_rows, through = steps(projected, step_bias, rate_log)
    cum, weigh, edge_rows = clock.tick(cum, weigh, edge_rows)
    gate_pieces.send(later=1)
    conv_low, fresh_state = enter(
        ring,
        projected,
        edge_rows,
        conv_taps,
        conv_shift,
        weigh,
        spread_factors(ring, through[0, :HEADS]),
    )
    proj_b = conv_low[:, INNER : INNER + STATE]
    proj_c = conv_low[:, INNER + STATE :]
    (fresh_state,) = clock.tick(fresh_state)
    blocks = lax.all_to_all(fresh_state, "seq", 0, 0, tiled=True)
    out_spread.third()
    gate_pieces.pass_on(0)
    gate_pieces.pass_on(1)
    skip_row = jnp.repeat(skip_gain, HEADDIM)[None]
    base = inside(conv_low, cum, cum_rows, step_rows, skip_row)
    blocks, base = clock.tick(blocks, base)
    factor = blocks[:, INNER // ring.seq :]
    (states,) = clock.tick(carried(ring, blocks, factor, False))
    incoming = returned(ring, states).reshape(INNER, STATE)
    gate_pieces.pass_on(2)
    out_spread.fourth()
    weight_gate = gate_pieces.pieces(in_rows, near_rows)
    weight_out = out_spread.whole(near_out)
    grad_pieces = Pieces(ring, grad_out)
    grad_pieces.send()
    gate_rows = gate_pieces.rows
    gate_parts = [
        project(normed_columns, [weight_gate[key][at] for key in where], gate_rows, gate_rows)
        for at in range(3)
    ]
    wide = out_weight.shape[0]
    place_row = jnp.stack(list(where.values())).astype(jnp.int32)
    grad_mixed = to_inner(grad_out, list(weight_out.values()), place_row)
    incoming, grad_mixed, *gate_parts = clock.tick(incoming, grad_mixed, *gate_parts)
    normed_all = trade_columns(ring, {key: clock.now(part) for key, part in normed_for.items()})
    grad_pieces.near()
    mixed, grad_y, grad_gate, grad_reach, direct, grad_g_gate = turn(
        base, incoming, proj_c, decay, gate_parts, grad_mixed, gain_gate
    )
    direct, mixed, grad_y, grad_reach, grad_gate = clock.tick(
        direct, mixed, grad_y, grad_reach, grad_gate
    )
    blocks = lax.all_to_all(direct.reshape(ring.seq, -1, STATE), "seq", 0, 0, tiled=True)
    mixed_all = trade_columns(ring, columns_for(ring, mixed))
    clock.defer(len(mixed_all) - 1, 2)
    grad_out_all = grad_pieces.whole()
    x_part, b_part, c_part, grad_step, grad_cum, grad_skip = inside_back(
        grad_y, grad_reach, conv_low, incoming, cum, cum_rows, step_rows, skip_row
    )
    gate_grads = Pieces(ring, grad_gate)
    gate_grads.send(later=2)
    blocks, x_part, b_part, c_part = clock.tick(blocks, x_part, b_part, c_part)
    states = carried(ring, blocks, factor, True)
    (states,) = clock.tick(states)
    chain_grad = returned(ring, states)
    mixed_all = {key: clock.now(block) for key, block in mixed_all.items()}
    total_w_out = Total(ring, weight_grad(mixed_all, grad_out_all, 384))
    total_w_out.step()
    clock.defer()
    gate_grads.near()
    total_w_gate = Total(ring, weight_grad(gate_grads.whole(), normed_all, 768))
    (total_w_gate.value,) = clock.tick(total_w_gate.value)
    total_w_gate.step()
    clock.defer()
    mixed = clock.now(mixed)
    mixed_columns = [
        lax.dynamic_slice_in_dim(mixed, place * wide, wide, axis=1) for place in where.values()
    ]
    output = output_rows(hidden[0], mixed_columns, list(weight_out.values()))
    chain_grad, output = clock.tick(chain_grad, output)
    total_w_out.step()
    grad_conv, grad_more, first_rows, last_rows, grad_taps, grad_shift, grad_factor, crossed = leave(
        projected,
        edge_rows,
        conv_taps,
        conv_shift,
        conv_low,
        x_part,
        chain_grad.reshape(INNER, STATE),
        incoming,
        weigh,
        b_part,
        c_part,
    )
    grad_conv, grad_more, last_rows, first_rows = clock.tick(
        grad_conv, grad_more, last_rows, first_rows
    )
    total_w_out.step()
    clock.defer()
    last_rows = (last_rows + ring.next_block(first_rows, -1)).astype(bf16)
    grad_conv = lax.dynamic_update_slice_in_dim(
        grad_conv, last_rows[:, :FIRST], row_count - 8, axis=0
    )
    (grad_conv,) = clock.tick(grad_conv)
    grad_more = lax.dynamic_update_slice_in_dim(
        grad_more, last_rows[:, FIRST:], row_count - 8, axis=0
    )
    grad_dt_raw, grad_step_bias, grad_rate = steps_back(
        projected,
        step_bias,
        rate_log,
        step_rows,
        cum_rows,
        grad_step,
        grad_cum,
        clock.now(grad_factor),
        crossed,
    )
    grad_tail = jnp.concatenate([grad_conv, grad_more, grad_dt_raw[:, :HEADS]], axis=1)

    first = Pieces(ring, grad_conv)
    last = Pieces(ring, jnp.concatenate([grad_more, grad_dt_raw], axis=1))
    first.send()
    first.near()
    total_w_gate.step()
    clock.tick()
    last.send(later=1)
    last.near()
    total_first = Total(ring, weight_grad(first.whole(), normed_all, 896))
    (total_first.value,) = clock.tick(total_first.value)
    total_first.step()
    total_w_out.step()
    total_w_gate.step()
    clock.defer(2)
    grad_shards = to_model(
        grad_gate, clock.now(grad_tail), list(weight_gate.values()), [
            (array, block * tile) for array, block in weight_conv.values()
        ]
    )
    (grad_shards,) = clock.tick(grad_shards)
    total_last = Total(ring, weight_grad(last.whole(), normed_all, 1664))
    (total_last.value,) = clock.tick(total_last.value)
    total_last.step()
    total_first.step()
    total_w_out.step()
    total_w_gate.step()
    grad_normed = jnp.zeros((row_count, model_width), f32)
    for k, place in enumerate(where.values()):
        grad_normed = lax.dynamic_update_slice_in_dim(
            grad_normed, grad_shards[k], place * depth, axis=1
        )
    grad_skip = jnp.sum(clock.now(grad_skip).reshape(HEADS, HEADDIM), axis=1)
    grad_tokens, grad_g_norm = pull_norm(grad_normed)
    hidden_grad = (grad_tokens + grad_out.astype(f32)).astype(bf16)
    hidden_grad, grad_g_norm = clock.tick(hidden_grad, grad_g_norm)
    grad_shift, grad_step_bias, grad_rate, grad_g_gate = (
        clock.now(part) for part in (grad_shift, grad_step_bias, grad_rate, grad_g_gate)
    )
    parts = [grad_g_norm, grad_taps, grad_shift[0], grad_step_bias[:, 0], grad_rate[:, 0]]
    parts += [grad_skip, grad_g_gate[0]]
    small_total = SmallSum(ring, pack(parts))
    total_w_out.step()
    clock.defer()
    total_first.step()
    total_last.step()
    total_w_gate.step()
    clock.tick()
    small_total.step()
    total_w_gate.halves()
    clock.defer()
    total_first.step()
    total_last.step()
    clock.tick()
    small_total.step()
    total_first.step()
    total_last.step()
    clock.tick()
    small_total.step()
    small_total.step()
    total_first.halves()
    clock.defer()
    total_last.step()
    clock.tick()
    small_total.step()
    total_last.halves()
    summed = small_total.finish().reshape(-1)
    shares, at = [], 0
    for part in parts:
        piece = summed[at : at + part.size].reshape(part.shape)
        at += part.size
        width = part.shape[-1] // ring.fsdp
        shares.append(
            lax.dynamic_slice_in_dim(piece, fsdp_index * width, width, axis=part.ndim - 1)
        )
    total_w_in = jnp.zeros((PROJ, depth), f32)
    total_w_in = place_rows(total_w_in, total_w_gate.halves(), 0, INNER)
    total_w_in = place_rows(total_w_in, total_first.halves(), INNER, FIRST)
    total_w_in = place_rows(
        total_w_in, total_last.halves(), INNER + FIRST, PROJ - INNER - FIRST
    )
    total_w_in = total_w_in.T
    total_w_out = total_w_out.finish()
    return (
        output[None],
        hidden_grad[None],
        shares[0],
        total_w_in,
        shares[1],
        shares[2],
        shares[3],
        shares[4],
        shares[5],
        shares[6],
        total_w_out,
    )


def solution(mesh):
    placed = (
        P("fsdp", "seq", None),
        P("fsdp"),
        P("fsdp"),
        P("fsdp", None),
        P(None, "fsdp"),
        P("fsdp"),
        P("fsdp"),
        P("fsdp"),
        P("fsdp"),
        P("fsdp"),
        P("fsdp", None),
        P("fsdp", "seq", None),
    )
    return jax.shard_map(
        local,
        mesh=mesh,
        in_specs=placed,
        out_specs=(
            P("fsdp", "seq", None),
            P("fsdp", "seq", None),
            P("fsdp"),
            P("fsdp", None),
            P(None, "fsdp"),
            P("fsdp"),
            P("fsdp"),
            P("fsdp"),
            P("fsdp"),
            P("fsdp"),
            P("fsdp", None),
        ),
        check_vma=False,
    )
```

```python
import functools

import jax
import jax.numpy as jnp
from jax import lax
from jax.experimental import pallas as pl
from jax.experimental.pallas import tpu as pltpu
from jax.sharding import PartitionSpec as P

HEADS = 48
HEADDIM = 64
STATE = 128
CONV = 4
INNER = 3072
CHANNELS = 3328
PROJ = 6448
PLANES = 2
CORES = 2
FIRST = 1792

f32 = jnp.float32
bf16 = jnp.bfloat16
epsilon = 1e-05
scoped = 40 * 2**20
whole_vmem = 60 * 2**20
no_cost = pl.CostEstimate(flops=0, bytes_accessed=0, transcendentals=0)


class Ring:
    def __init__(self, seq, fsdp):
        self.seq, self.fsdp = seq, fsdp
        self.clock = None
        self.line, self.row = seq // PLANES, fsdp // CORES

    def send(self, block, move):
        route = []
        for s in range(self.seq):
            for f in range(self.fsdp):
                there = move(s // PLANES, s % PLANES, f // CORES, f % CORES)
                if there is None:
                    continue
                z, x, y, c = there
                route.append((s * self.fsdp + f, (z * PLANES + x) * self.fsdp + y * CORES + c))
        arrived = lax.ppermute(block, ("seq", "fsdp"), route)
        self.clock.sent(arrived)
        return arrived

    def core(self, block):
        return self.send(block, lambda z, x, y, c: (z, x, y, 1 - c))

    def plane(self, block):
        return self.send(block, lambda z, x, y, c: (z, 1 - x, y, c))

    def from_row(self, block, distance):
        return self.send(block, lambda z, x, y, c: (z, x, (y - distance) % self.row, c))

    def far(self, block, distance):
        return self.send(block, lambda z, x, y, c: (z ^ distance, x, y, c))

    def relative(self, block, d, e):
        if not d and not e:
            return block
        return self.send(
            block, lambda z, x, y, c: (z, x, (y - d) % self.row, (c + e) % CORES)
        )

    def relative_back(self, block, d, e):
        return self.relative(block, d, e)

    def next_block(self, block, distance):
        def move(z, x, y, c):
            s = z * PLANES + x + distance
            return (s // PLANES, s % PLANES, y, c) if 0 <= s < self.seq else None

        return self.send(block, move)


def rows_of(block, index, count):
    return lax.dynamic_slice_in_dim(block, index * count, count, axis=0)


def swapped(ring, distance):
    seq_index = lax.axis_index("seq")
    if distance == 0:
        return seq_index % PLANES, ring.plane
    bit = (seq_index // PLANES // distance) % 2
    return bit, lambda block: ring.far(block, distance)


def cube(ring):
    distances, distance = [0], 1
    while distance < ring.line:
        distances.append(distance)
        distance *= 2
    return distances


class Total:
    def __init__(self, ring, grad):
        self.ring, self.value, self.other, self.merge = ring, grad, None, None
        self.steps = [(True, d) for d in cube(ring)] + [(False, d) for d in reversed(cube(ring))]

    def settle(self):
        if self.merge is not None:
            value, other = self.ring.clock.now((self.value, self.other))
            self.value, self.merge = self.merge(value, other), None
        else:
            self.value = self.ring.clock.now(self.value)

    def step(self):
        if not self.steps:
            return
        self.settle()
        halves, distance = self.steps.pop(0)
        bit, send = swapped(self.ring, distance)
        if halves:
            half = self.value.shape[0] // 2
            self.other = send(rows_of(self.value, 1 - bit, half).astype(bf16))
            self.merge = lambda value, other: rows_of(value, bit, half) + other.astype(f32)
        else:
            self.value = self.value.astype(bf16)
            self.other = send(self.value)
            self.merge = lambda value, other: jnp.concatenate(
                [jnp.where(bit == 0, value, other), jnp.where(bit == 0, other, value)], axis=0
            )

    def finish(self):
        while self.steps:
            self.step()
        self.settle()
        return self.value.astype(f32)

    def halves(self):
        while self.steps:
            self.step()
        return self.value, self.other


class Clock:
    def __init__(self, value):
        self.token = value
        self.pending = []

    def sent(self, value):
        self.pending.append([1, value])

    def tick(self, *values):
        due = [value for ticks, value in self.pending if ticks == 1]
        out = lax.optimization_barrier((self.token,) + values + tuple(due))
        self.token = out[0]
        self.pending = [[ticks - 1, value] for ticks, value in self.pending if ticks > 1]
        return out[1 : 1 + len(values)]

    def defer(self, count=1, ticks=1):
        for entry in self.pending[len(self.pending) - count :]:
            entry[0] += ticks

    def now(self, value):
        return lax.optimization_barrier((value, self.token))[0]


class Spread:
    def __init__(self, ring, source, origin=0, whole_only=False):
        self.ring, self.source, self.origin, self.whole_only = ring, source, origin, whole_only
        block = self.block = source[origin:]
        self.quarter = -(-block.shape[0] // 64) * 16
        self.cut = -(-self.quarter // 32) * 16
        seq_index = lax.axis_index("seq")
        self.place = seq_index % 2 + 2 * ((seq_index // PLANES) % 2)
        self.arrived = []

    def start(self, index):
        return jnp.minimum((self.place ^ index) * self.quarter, self.block.shape[0] - self.quarter)

    def put(self, pieces):
        sides = (pieces,)
        if not self.whole_only:
            sides += ([self.ring.core(piece) for piece in pieces],)
        self.arrived.append(sides)

    def first(self, at_once=False):
        ring = self.ring
        mine = lax.dynamic_slice_in_dim(self.source, self.origin + self.start(0), self.quarter, axis=0)
        mine = mine if at_once else ring.clock.now(mine)
        self.mine = [ring.from_row(mine, d) for d in range(1, ring.row)]

    def second(self):
        ring = self.ring
        mine = [ring.clock.now(part) for part in self.mine]
        self.beside = [ring.plane(part) for part in mine]
        self.behind = [ring.far(part, 1) for part in mine]
        self.put(mine)

    def third(self):
        ring, cut = self.ring, self.cut
        beside = [ring.clock.now(part) for part in self.beside]
        behind = [ring.clock.now(part) for part in self.behind]
        self.corner = (
            [ring.plane(part[:cut]) for part in behind],
            [ring.far(part[cut:], 1) for part in beside],
        )
        self.put(beside)
        self.put(behind)

    def fourth(self):
        now = self.ring.clock.now
        self.put([now(part) for part in self.corner[0]])
        self.put([now(part) for part in self.corner[1]])

    def whole(self, near):
        found = {(0, 0): self.block, (0, 1): near}
        index = jnp.stack([self.place ^ k for k in range(4)]).astype(jnp.int32)
        for d in range(1, self.ring.row):
            sides = [[side[d - 1] for side in pieces] for pieces in zip(*self.arrived)]
            shards = laid(self.block, self.quarter, self.cut, index, sides)
            found[d, 0] = shards[0]
            found[d, 1] = self.ring.core(shards[0]) if self.whole_only else shards[1]
        return found


def sum_body(count, *refs):
    out_ref = refs[-1]
    total = None
    for left, right in zip(refs[:count], refs[count:-1]):
        term = lax.dot_general(
            left[...], right[...], (((0,), (0,)), ((), ())), preferred_element_type=f32
        )
        total = term if total is None else total + term
    out_ref[...] = total


def weight_grad(rows_all, columns_all, tile):
    keys = list(rows_all)
    tokens, rows = rows_all[keys[0]].shape
    width = columns_all[keys[0]].shape[1]
    return pl.pallas_call(
        functools.partial(sum_body, len(keys)),
        grid=(rows // tile,),
        in_specs=[pl.BlockSpec((tokens, tile), lambda i: (0, i))] * len(keys)
        + [pl.BlockSpec((tokens, width), lambda i: (0, 0))] * len(keys),
        out_specs=pl.BlockSpec((tile, width), lambda i: (i, 0)),
        out_shape=jax.ShapeDtypeStruct((rows, width), f32),
        name="weight_grad",
        cost_estimate=no_cost,
        compiler_params=pltpu.CompilerParams(vmem_limit_bytes=scoped),
    )(*[rows_all[key] for key in keys], *[columns_all[key] for key in keys])


def to_inner_body(tiles, place_ref, grad_ref, *refs):
    out_ref = refs[-1]
    shard = pl.program_id(0) // tiles
    for k, weight in enumerate(refs[:-1]):

        @pl.when(shard == k)
        def _(weight=weight):
            out_ref[...] = dot_last(grad_ref[...], weight[...])


def to_inner(grad, weights, places):
    tokens, width = grad.shape
    rows = weights[0].shape[0]
    tile = 384
    tiles = rows // tile
    return pl.pallas_call(
        functools.partial(to_inner_body, tiles),
        grid_spec=pltpu.PrefetchScalarGridSpec(
            num_scalar_prefetch=1,
            grid=(len(weights) * tiles,),
            in_specs=[pl.BlockSpec((tokens, width), lambda i, place: (0, 0))]
            + [
                pl.BlockSpec(
                    (tile, width), lambda i, place, k=k: (jnp.clip(i - k * tiles, 0, tiles - 1), 0)
                )
                for k in range(len(weights))
            ],
            out_specs=pl.BlockSpec(
                (tokens, tile), lambda i, place: (0, place[i // tiles] * tiles + i % tiles)
            ),
        ),
        out_shape=jax.ShapeDtypeStruct((tokens, rows * len(weights)), f32),
        name="to_inner",
        cost_estimate=no_cost,
        compiler_params=pltpu.CompilerParams(vmem_limit_bytes=scoped),
    )(places, grad, *weights)


def to_model_body(terms, gate_ref, tail_ref, *refs):
    out_ref = refs[-1]
    for k, shard in enumerate(terms):
        total = None
        for tail, column, array, row, count in shard:
            left = (tail_ref if tail else gate_ref)[:, column : column + count]
            term = jnp.dot(left, refs[array][row : row + count], preferred_element_type=f32)
            total = term if total is None else total + term
        out_ref[k] = total


def to_model(grad_gate, grad_tail, gate_weights, tail_weights):
    width = grad_tail.shape[1]
    rows = grad_gate.shape[1] // len(gate_weights[0])
    flat, terms = [], []

    def place(array):
        for k, held in enumerate(flat):
            if held is array:
                return k
        flat.append(array)
        return len(flat) - 1

    for pieces, (tail, start) in zip(gate_weights, tail_weights):
        shard = [(True, 0, place(tail), start, width)]
        if pieces[0][0] is tail:
            shard.append((False, 0, place(tail), 0, grad_gate.shape[1]))
        else:
            shard += [
                (False, at * rows, place(array), block * rows, rows)
                for at, (array, block) in enumerate(pieces)
            ]
        terms.append(shard)
    inside = pl.BlockSpec(memory_space=pltpu.VMEM)
    return pl.pallas_call(
        functools.partial(to_model_body, terms),
        in_specs=[inside] * (2 + len(flat)),
        out_specs=inside,
        out_shape=jax.ShapeDtypeStruct((len(terms), grad_gate.shape[0], flat[0].shape[1]), f32),
        name="to_model",
        cost_estimate=no_cost,
        compiler_params=pltpu.CompilerParams(vmem_limit_bytes=scoped),
    )(grad_gate, grad_tail, *flat)


def output_body(count, token_ref, *refs):
    out_ref = refs[-1]
    total = token_ref[...].astype(f32)
    for columns, weight in zip(refs[:count], refs[count:-1]):
        total = total + jnp.dot(columns[...], weight[...], preferred_element_type=f32)
    out_ref[...] = total.astype(bf16)


def output_rows(tokens, columns, weights):
    inside = pl.BlockSpec(memory_space=pltpu.VMEM)
    return pl.pallas_call(
        functools.partial(output_body, len(columns)),
        in_specs=[inside] * (1 + 2 * len(columns)),
        out_specs=inside,
        out_shape=jax.ShapeDtypeStruct(tokens.shape, bf16),
        name="output_rows",
        cost_estimate=no_cost,
        compiler_params=pltpu.CompilerParams(vmem_limit_bytes=scoped),
    )(tokens, *columns, *weights)


def laid_body(quarter, cut, index_ref, *refs):
    count = len(refs) // 6
    pieces, shards = refs[:-count], refs[-count:]
    for e, shard in enumerate(shards):
        own = pieces[e * 5 : e * 5 + 5]
        for piece, quarter_of, offset in zip(own, (0, 1, 2, 3, 3), (0, 0, 0, 0, cut)):
            start = jnp.minimum(index_ref[quarter_of] * quarter, shard.shape[0] - quarter)
            start = pl.multiple_of(start + offset, 16)
            shard[pl.ds(start, piece.shape[0]), :] = piece[...]


def laid(block, quarter, cut, index, sides):
    flat = [piece for side in sides for piece in side]
    inside = pl.BlockSpec(memory_space=pltpu.VMEM)
    return pl.pallas_call(
        functools.partial(laid_body, quarter, cut),
        grid_spec=pltpu.PrefetchScalarGridSpec(
            num_scalar_prefetch=1,
            grid=(),
            in_specs=[inside] * len(flat),
            out_specs=[inside] * len(sides),
        ),
        out_shape=[jax.ShapeDtypeStruct(block.shape, block.dtype)] * len(sides),
        name="laid",
        cost_estimate=no_cost,
        compiler_params=pltpu.CompilerParams(vmem_limit_bytes=scoped),
    )(index, *flat)


def project_body(count, *refs):
    out_ref = refs[-1]
    total = None
    for columns, weight in zip(refs[:count], refs[count:-1]):
        term = lax.dot_general(
            columns[...], weight[...], (((1,), (1,)), ((), ())), preferred_element_type=f32
        )
        total = term if total is None else total + term
    out_ref[...] = total.astype(out_ref.dtype)


def project(columns, weights, tile, width):
    count = len(columns)
    tokens, depth = columns[0].shape
    return pl.pallas_call(
        functools.partial(project_body, count),
        grid=(pl.cdiv(width, tile),),
        in_specs=[pl.BlockSpec((tokens, depth), lambda i: (0, 0))] * count
        + [pl.BlockSpec((tile, depth), lambda i, k=k: (i + k, 0)) for _, k in weights],
        out_specs=pl.BlockSpec((tokens, tile), lambda i: (0, i)),
        out_shape=jax.ShapeDtypeStruct((tokens, width), bf16),
        name="project",
        cost_estimate=no_cost,
        compiler_params=pltpu.CompilerParams(vmem_limit_bytes=scoped),
    )(*columns, *[array for array, _ in weights])


class Pieces:
    def __init__(self, ring, block, count=1):
        self.ring, self.block = ring, block
        self.rows = block.shape[0] // count
        self.parts = []

    def near(self):
        self.beside = self.ring.core(self.ring.clock.now(self.block))

    def send(self, later=0):
        clock = self.ring.clock
        at = len(self.parts) * self.rows
        piece = clock.now(self.block[at : at + self.rows])
        self.parts.append([self.ring.from_row(piece, d) for d in range(1, self.ring.row)])
        clock.defer(self.ring.row - 1, later)

    def pass_on(self, at):
        far = [self.ring.clock.now(piece) for piece in self.parts[at]]
        self.parts[at] = [(piece, self.ring.core(piece)) for piece in far]

    def pieces(self, own, near):
        count = len(self.parts)
        found = {
            (0, 0): [(own, at) for at in range(count)],
            (0, 1): [(near, at) for at in range(count)],
        }
        for d in range(1, self.ring.row):
            for e in range(CORES):
                found[d, e] = [(part[d - 1][e], 0) for part in self.parts]
        return found

    def whole(self):
        found = {(0, 0): self.block, (0, 1): self.beside}
        for d in range(1, self.ring.row):
            found[d, 0] = self.ring.clock.now(self.parts[0][d - 1])
            found[d, 1] = self.ring.core(found[d, 0])
        return found


def gather_rows(ring, block):
    found = {}
    for d in range(ring.row):
        found[d, 0] = block if d == 0 else ring.from_row(block, d)
        found[d, 1] = ring.core(found[d, 0])
    return found


def places(ring):
    index = lax.axis_index("fsdp")
    y, c = index // CORES, index % CORES
    return {
        (d, e): ((y + d) % ring.row) * CORES + (c + e) % CORES
        for d in range(ring.row)
        for e in range(CORES)
    }


def columns_for(ring, block):
    index = lax.axis_index("fsdp")
    y, c = index // CORES, index % CORES
    width = block.shape[1] // ring.fsdp
    return {
        (d, e): lax.dynamic_slice_in_dim(
            block, (((y - d) % ring.row) * CORES + (c + e) % CORES) * width, width, axis=1
        )
        for d in range(ring.row)
        for e in range(CORES)
    }


def trade_columns(ring, pieces):
    return {key: ring.relative_back(piece, *key) for key, piece in pieces.items()}


class SmallSum:
    def __init__(self, ring, vector):
        self.ring, self.value = ring, vector
        self.steps = ["core", "row"] + cube(ring)[1:] + cube(ring)[:1]

    def step(self):
        if not self.steps:
            return
        kind = self.steps.pop(0)
        vector = self.ring.clock.now(self.value)
        if kind == "core":
            self.value = vector + self.ring.core(vector)
        elif kind == "row":
            self.value = sum([self.ring.from_row(vector, d) for d in range(1, self.ring.row)], vector)
        else:
            self.value = vector + swapped(self.ring, kind)[1](vector)

    def finish(self):
        while self.steps:
            self.step()
        return self.value


def head_rows(ring):
    part = INNER // ring.seq
    run = HEADDIM
    while part % run:
        run //= 2
    return part, run


def spread_factors(ring, through):
    part, run = head_rows(ring)
    factor = jnp.repeat(through, HEADDIM // run).reshape(ring.seq, part // run)
    factor = jnp.pad(factor, ((0, 0), (0, 8 - part // run)))
    return jnp.broadcast_to(factor[:, :, None], (ring.seq, 8, STATE))


def carried_body(reverse, run, blocks_ref, factor_ref, out_ref):
    count, part = out_ref.shape[0], out_ref.shape[1]
    state = jnp.zeros((part, STATE), f32)
    for k in reversed(range(count)) if reverse else range(count):
        out_ref[k] = state.astype(bf16)
        factor = factor_ref[k]
        spread = [jnp.broadcast_to(factor[j : j + 1], (run, STATE)) for j in range(part // run)]
        state = jnp.concatenate(spread, axis=0) * state + blocks_ref[k, :part]


def carried(ring, blocks, factor, reverse):
    part, run = head_rows(ring)
    return pl.pallas_call(
        functools.partial(carried_body, reverse, run),
        out_shape=jax.ShapeDtypeStruct((ring.seq, part, STATE), bf16),
        name="carried",
        cost_estimate=no_cost,
        compiler_params=pltpu.CompilerParams(vmem_limit_bytes=scoped),
    )(blocks, factor)


def returned(ring, states):
    states = lax.all_to_all(states, "seq", 0, 0, tiled=True)
    return states.reshape(HEADS, HEADDIM, STATE)


def place_rows(whole, sides, start, rows):
    mine, other = sides
    first = (lax.axis_index("seq") % PLANES) == 0
    half = mine.shape[0]
    low = jnp.where(first, mine, other).astype(f32)
    high = jnp.where(first, other, mine)[: rows - half].astype(f32)
    whole = lax.dynamic_update_slice_in_dim(whole, low, start, axis=0)
    return lax.dynamic_update_slice_in_dim(whole, high, start + half, axis=0)


def steps_body(dt_ref, bias_ref, rate_ref, cum_ref, weigh_ref, decay_ref, cum_rows, step_rows, through_ref):
    raw = dt_ref[...].astype(f32) + bias_ref[...]
    step = jnp.maximum(raw, 0.0) + jnp.log1p(jnp.exp(-jnp.abs(raw)))
    tokens = step.shape[0]
    row = lax.broadcasted_iota(jnp.int32, step.shape, 0)
    cum = step * -jnp.exp(rate_ref[...])
    distance = 1
    while distance < tokens:
        cum = cum + jnp.where(row >= distance, pltpu.roll(cum, distance, 0), 0.0)
        distance *= 2
    end = cum[tokens - 1 :]
    cum_ref[...] = cum
    weigh_ref[...] = jnp.exp(end - cum) * step
    decay_ref[...] = jnp.exp(cum)
    cum_rows[...] = cum.T[:HEADS]
    step_rows[...] = step.T[:HEADS]
    through_ref[...] = jnp.exp(end)


def steps(projected, bias, rate):
    tokens = projected.shape[0]
    row = pl.BlockSpec((1, STATE), lambda i: (0, 0))
    by_token = pl.BlockSpec((tokens, STATE), lambda i: (0, 0))
    by_head = pl.BlockSpec((HEADS, tokens), lambda i: (0, 0))
    pad = lambda v: jnp.pad(v, (0, STATE - HEADS))[None]
    return pl.pallas_call(
        steps_body,
        grid=(1,),
        in_specs=[pl.BlockSpec((tokens, STATE), lambda i: (0, CHANNELS // STATE)), row, row],
        out_specs=[by_token] * 3 + [by_head] * 2 + [row],
        out_shape=[jax.ShapeDtypeStruct((tokens, STATE), f32)] * 3
        + [jax.ShapeDtypeStruct((HEADS, tokens), f32)] * 2
        + [jax.ShapeDtypeStruct((1, STATE), f32)],
        name="steps",
        cost_estimate=no_cost,
        compiler_params=pltpu.CompilerParams(vmem_limit_bytes=scoped),
    )(projected, pad(bias), pad(rate))


def steps_back_body(
    dt_ref, bias_ref, rate_ref, step_ref, cum_ref, grad_step_ref, grad_cum_ref, factor_ref, crossed_ref,
    grad_ref, bias_grad_ref, rate_grad_ref,
):
    step, cum, factor = step_ref[...], cum_ref[...], factor_ref[...]
    tokens = step.shape[1]
    lane = lax.broadcasted_iota(jnp.int32, step.shape, 1)
    end = cum[:, tokens - 1 :]
    to_end = jnp.exp(end - cum)
    tail = factor * step * to_end
    grad_end = jnp.sum(tail, axis=1, keepdims=True) + jnp.exp(end) * jnp.sum(
        crossed_ref[...], axis=1, keepdims=True
    )
    total = grad_cum_ref[...] - tail + jnp.where(lane == tokens - 1, grad_end, 0.0)
    distance = 1
    while distance < tokens:
        moved = pltpu.roll(total, tokens - distance, 1)
        total = total + jnp.where(lane < tokens - distance, moved, 0.0)
        distance *= 2
    rate = -jnp.exp(rate_ref[...])
    rate_grad_ref[...] = rate * jnp.sum(total * step, axis=1, keepdims=True)
    raw = dt_ref[...].astype(f32).T[:HEADS] + bias_ref[...]
    grad = (grad_step_ref[...] + factor * to_end + total * rate) * jax.nn.sigmoid(raw)
    bias_grad_ref[...] = jnp.sum(grad, axis=1, keepdims=True)
    none = jnp.zeros((STATE - HEADS, tokens), f32)
    grad_ref[...] = jnp.concatenate([grad, none], axis=0).T.astype(bf16)


def steps_back(projected, bias, rate, step_rows, cum_rows, grad_step, grad_cum, factor, crossed):
    tokens = projected.shape[0]
    column = pl.BlockSpec((HEADS, 1), lambda i: (0, 0))
    by_head = pl.BlockSpec((HEADS, tokens), lambda i: (0, 0))
    return pl.pallas_call(
        steps_back_body,
        grid=(1,),
        in_specs=[pl.BlockSpec((tokens, STATE), lambda i: (0, CHANNELS // STATE)), column, column]
        + [by_head] * 5
        + [pl.BlockSpec((HEADS, STATE), lambda i: (0, 0))],
        out_specs=[pl.BlockSpec((tokens, STATE), lambda i: (0, 0)), column, column],
        out_shape=[
            jax.ShapeDtypeStruct((tokens, STATE), bf16),
            jax.ShapeDtypeStruct((HEADS, 1), f32),
            jax.ShapeDtypeStruct((HEADS, 1), f32),
        ],
        name="steps_back",
        cost_estimate=no_cost,
        compiler_params=pltpu.CompilerParams(vmem_limit_bytes=scoped),
    )(
        projected, bias[:, None], rate[:, None], step_rows, cum_rows, grad_step, grad_cum, factor,
        crossed,
    )


def group_columns(wide_ref, group, heads):
    shift = lax.rem(STATE - heads * group, STATE)
    return pltpu.roll(wide_ref[...], shift, 1)[:, :heads]


def keep_columns(wide_ref, at, columns):
    wide = wide_ref[...]
    lane = lax.broadcasted_iota(jnp.int32, wide.shape, 1)
    for k, column in enumerate(columns):
        wide = jnp.where(lane == at + k, column, wide)
    wide_ref[...] = wide


def along(column_pair):
    lane = lax.broadcasted_iota(jnp.int32, (column_pair.shape[0], 2 * HEADDIM), 1)
    return jnp.where(lane < HEADDIM, column_pair[:, :1], column_pair[:, 1:2])


def conv_sum(edge, rows, taps, shift):
    window = jnp.concatenate([edge, rows], axis=0)
    total = shift
    for k in range(CONV):
        moved = window if k == CONV - 1 else pltpu.roll(window, CONV - 1 - k, 0)
        total = total + taps[k : k + 1] * moved[8:]
    return total


def enter_body(part, proj_ref, edge_ref, taps_ref, shift_ref, weigh_ref, factor_ref, low_ref, fresh_ref):
    def conv(at, width):
        columns = slice(at, at + width)
        total = conv_sum(
            edge_ref[:, columns].astype(f32),
            proj_ref[:, columns].astype(f32),
            taps_ref[:, columns],
            shift_ref[:, columns],
        )
        low = (total * jax.nn.sigmoid(total)).astype(bf16)
        low_ref[:, columns] = low
        return low

    proj_b = conv(INNER, 2 * STATE)[:, :STATE]
    fresh_ref[:, part:] = factor_ref[...]
    for at in range(0, INNER, 2 * HEADDIM):
        low = conv(at, 2 * HEADDIM)
        head = at // HEADDIM
        weighted = (low.astype(f32) * along(weigh_ref[:, head : head + 2])).astype(bf16)
        fresh = lax.dot_general(
            weighted, proj_b, (((0,), (0,)), ((), ())), preferred_element_type=f32
        )
        row = at
        while row < at + 2 * HEADDIM:
            device, offset = row // part, row % part
            count = min(part - offset, at + 2 * HEADDIM - row)
            fresh_ref[device, offset : offset + count] = fresh[row - at : row - at + count]
            row += count


def enter(ring, projected, edge, taps, shift, weigh, factor):
    part, _ = head_rows(ring)
    return pl.pallas_call(
        functools.partial(enter_body, part),
        out_shape=[
            jax.ShapeDtypeStruct((projected.shape[0], CHANNELS), bf16),
            jax.ShapeDtypeStruct((ring.seq, part + 8, STATE), f32),
        ],
        name="enter",
        cost_estimate=no_cost,
        compiler_params=pltpu.CompilerParams(vmem_limit_bytes=scoped),
    )(projected, edge, taps, shift[None], weigh, factor)


def pairs_along(columns):
    return jnp.concatenate(
        [along(columns[:, i : i + 2]) for i in range(0, columns.shape[1], 2)], axis=1
    )


def turn_body(
    base_ref, incoming_ref, c_ref, decay_ref, grad_ref, gain_ref, *refs,
):
    count = len(refs) - 10
    gate_refs = refs[:count]
    (
    mixed_ref, grad_y_ref, grad_gate_ref, grad_reach_ref, direct_ref, gain_grad_ref,
    mixer, grads, squares, products,
    ) = refs[count:]
    later, j = pl.program_id(0), pl.program_id(1)
    gate = gate_refs[0][...]
    for k in range(1, count):
        gate = jnp.where(j * count >= k * pl.num_programs(1), gate_refs[k][...], gate)
    gate = gate.astype(f32)
    sig = jax.nn.sigmoid(gate)
    silu = gate * sig
    gain = gain_ref[...]

    @pl.when((later == 0) & (j == 0))
    def _():
        squares[...] = jnp.zeros_like(squares)
        products[...] = jnp.zeros_like(products)

    @pl.when(later == 0)
    def _():
        reached = lax.dot_general(
            c_ref[...], incoming_ref[...], (((1,), (1,)), ((), ())), preferred_element_type=f32
        )
        ssd = base_ref[...] + pairs_along(group_columns(decay_ref, j, gain.shape[1] // HEADDIM)) * reached
        gated = ssd * silu
        mixer[j] = ssd
        grads[j] = grad_ref[...]
        squares[...] += jnp.sum(gated * gated, axis=1, keepdims=True)
        products[...] += jnp.sum(gated * grad_ref[...] * gain, axis=1, keepdims=True)

    @pl.when(later == 1)
    def _():
        scale = lax.rsqrt(squares[...] / INNER + epsilon)
        ssd = mixer[j]
        grad = grads[j]
        normal = ssd * silu * scale
        mixed_ref[...] = (normal * gain).astype(bf16)
        gain_grad_ref[...] = jnp.sum(grad * normal, axis=0, keepdims=True)
        grad_gated = scale * (grad * gain - normal * (scale * products[...] / INNER))
        grad_y = (grad_gated * silu).astype(bf16)
        grad_y_ref[...] = grad_y
        grad_gate_ref[...] = (grad_gated * ssd * (sig + silu * (1.0 - sig))).astype(bf16)
        grad_reach = (grad_y.astype(f32) * pairs_along(group_columns(decay_ref, j, gain.shape[1] // HEADDIM))).astype(bf16)
        grad_reach_ref[...] = grad_reach
        direct_ref[...] = lax.dot_general(
            grad_reach, c_ref[...], (((0,), (0,)), ((), ())), preferred_element_type=f32
        )


def later_or_same(tokens):
    t = lax.broadcasted_iota(jnp.int32, (tokens, tokens), 0)
    return t >= lax.broadcasted_iota(jnp.int32, (tokens, tokens), 1)


def dot_last(a, b):
    return lax.dot_general(a, b, (((1,), (1,)), ((), ())), preferred_element_type=f32)


def dot_first(a, b):
    return lax.dot_general(a, b, (((0,), (0,)), ((), ())), preferred_element_type=f32)


def inside_body(x_ref, b_ref, c_ref, cum_ref, cum_rows_ref, step_rows_ref, skip_ref, out_ref, scores):
    tokens = x_ref.shape[0]

    @pl.when(pl.program_id(0) == 0)
    def _():
        table = dot_last(c_ref[...], b_ref[...])
        scores[...] = jnp.where(later_or_same(tokens), table, 0.0)

    x = x_ref[...]
    j = pl.program_id(0)
    same = later_or_same(tokens)
    cum = group_columns(cum_ref, j, 2)
    parts = []
    for head in range(2):
        row = pl.ds(2 * j + head, 1)
        exponent = cum[:, head : head + 1] - cum_rows_ref[row, :]
        decay = jnp.exp(jnp.where(same, exponent, 0.0))
        mixing = (scores[...] * decay * step_rows_ref[row, :]).astype(bf16)
        parts.append(jnp.dot(mixing, x, preferred_element_type=f32))
    first = lax.broadcasted_iota(jnp.int32, x.shape, 1) < HEADDIM
    out_ref[...] = jnp.where(first, parts[0], parts[1]) + skip_ref[...] * x.astype(f32)


def pair_specs(tokens):
    columns = pl.BlockSpec((tokens, 2 * HEADDIM), lambda j: (0, j))
    by_token = pl.BlockSpec((tokens, STATE), lambda j: (0, 0))
    by_head = pl.BlockSpec((HEADS, tokens), lambda j: (0, 0))
    row = pl.BlockSpec((1, 2 * HEADDIM), lambda j: (0, j))
    proj_b = pl.BlockSpec((tokens, STATE), lambda j: (0, INNER // STATE))
    proj_c = pl.BlockSpec((tokens, STATE), lambda j: (0, INNER // STATE + 1))
    return columns, by_token, by_head, row, proj_b, proj_c


def inside(conv_low, cum_pairs, cum_rows, step_rows, skip_row):
    tokens = conv_low.shape[0]
    columns, by_token, by_head, row, proj_b, proj_c = pair_specs(tokens)
    return pl.pallas_call(
        inside_body,
        grid=(HEADS // 2,),
        in_specs=[columns, proj_b, proj_c, by_token, by_head, by_head, row],
        out_specs=columns,
        out_shape=jax.ShapeDtypeStruct((tokens, INNER), f32),
        scratch_shapes=[pltpu.VMEM((tokens, tokens), f32)],
        name="inside",
        cost_estimate=no_cost,
        compiler_params=pltpu.CompilerParams(vmem_limit_bytes=scoped),
    )(conv_low, conv_low, conv_low, cum_pairs, cum_rows, step_rows, skip_row)


def inside_back_body(
    y_ref, reach_ref, x_ref, b_ref, c_ref, incoming_ref, cum_ref, cum_rows_ref, step_rows_ref, skip_ref,
    x_out, b_out, c_out, step_out, cum_out, skip_out,
    scores, grad_scores, wide_sums,
):
    tokens = x_ref.shape[0]
    j = pl.program_id(0)

    @pl.when(j == 0)
    def _():
        table = dot_last(c_ref[...], b_ref[...])
        scores[...] = jnp.where(later_or_same(tokens), table, 0.0)
        grad_scores[...] = jnp.zeros_like(grad_scores)
        c_out[...] = jnp.zeros_like(c_out)

    x, y = x_ref[...], y_ref[...]
    wide = y.astype(f32)
    incoming = incoming_ref[...]
    reached = wide * dot_last(c_ref[...], incoming)
    c_out[...] += jnp.dot(reach_ref[...], incoming, preferred_element_type=f32)
    skip_out[...] = jnp.sum(wide * x.astype(f32), axis=0, keepdims=True)
    first = lax.broadcasted_iota(jnp.int32, x.shape, 1) < HEADDIM
    wide_cum = group_columns(cum_ref, j, 2)
    middle = tokens // 2
    same = later_or_same(middle)
    parts, sums = [], []
    totals = [0.0, 0.0, 0.0]
    for head in range(2):
        row = pl.ds(2 * j + head, 1)
        steps_row, cum_row = step_rows_ref[row, :], cum_rows_ref[row, :]
        own = jnp.where(first == (head == 0), y, jnp.zeros_like(y))
        mine = jnp.sum(
            reached[:, head * HEADDIM : (head + 1) * HEADDIM], axis=1, keepdims=True
        ) * jnp.exp(wide_cum[:, head : head + 1])
        by_row, by_column, given = [0.0, 0.0], [0.0, 0.0], [0.0, 0.0]
        for k, (late, early) in enumerate(((0, 0), (1, 0), (1, 1))):
            rows = slice(late * middle, (late + 1) * middle)
            columns = slice(early * middle, (early + 1) * middle)
            step = steps_row[:, columns]
            exponent = wide_cum[rows, head : head + 1] - cum_row[:, columns]
            decay = jnp.exp(jnp.where(same, exponent, 0.0) if late == early else exponent)
            both = scores[rows, columns] * decay
            grad_mix = dot_last(own[rows], x[columns])
            totals[k] = totals[k] + grad_mix * (decay * step)
            by_source = grad_mix * both
            by_column[early] = by_column[early] + jnp.sum(by_source, axis=0, keepdims=True)
            by_row[late] = by_row[late] + jnp.sum(by_source * step, axis=1, keepdims=True)
            given[early] = given[early] + dot_first((both * step).astype(bf16), y[rows])
        step_out[row, :] = jnp.concatenate(by_column, axis=1)
        sums.append(jnp.concatenate(by_row, axis=0) + mine)
        parts.append(jnp.concatenate(given, axis=0))
    for total, (late, early) in zip(totals, ((0, 0), (1, 0), (1, 1))):
        grad_scores[late * middle : (late + 1) * middle, early * middle : (early + 1) * middle] += total
    keep_columns(wide_sums, 2 * j, sums)
    x_out[...] = jnp.where(first, parts[0], parts[1]) + skip_ref[...] * wide

    @pl.when(j == pl.num_programs(0) - 1)
    def _():
        grad = jnp.where(later_or_same(tokens), grad_scores[...], 0.0).astype(bf16)
        c_out[...] += jnp.dot(grad, b_ref[...], preferred_element_type=f32)
        b_out[...] = dot_first(grad, c_ref[...])
        cum_out[...] = wide_sums[...].T[:HEADS] - step_out[...] * step_rows_ref[...]


def inside_back(grad_y, grad_reach, conv_low, incoming, cum_pairs, cum_rows, step_rows, skip_row):
    tokens = conv_low.shape[0]
    columns, by_token, by_head, row, proj_b, proj_c = pair_specs(tokens)
    whole = pl.BlockSpec((tokens, STATE), lambda j: (0, 0))
    pairs = HEADS // 2
    return pl.pallas_call(
        inside_back_body,
        grid=(pairs,),
        in_specs=[columns, columns, columns, proj_b, proj_c]
        + [pl.BlockSpec((2 * HEADDIM, STATE), lambda j: (j, 0)), by_token, by_head, by_head, row],
        out_specs=[columns, whole, whole, by_head, by_head, row],
        out_shape=[
            jax.ShapeDtypeStruct((tokens, INNER), f32),
            jax.ShapeDtypeStruct((tokens, STATE), f32),
            jax.ShapeDtypeStruct((tokens, STATE), f32),
            jax.ShapeDtypeStruct((HEADS, tokens), f32),
            jax.ShapeDtypeStruct((HEADS, tokens), f32),
            jax.ShapeDtypeStruct((1, INNER), f32),
        ],
        scratch_shapes=[
            pltpu.VMEM((tokens, tokens), f32),
            pltpu.VMEM((tokens, tokens), f32),
            pltpu.VMEM((tokens, STATE), f32),
        ],
        name="inside_back",
        cost_estimate=no_cost,
        compiler_params=pltpu.CompilerParams(vmem_limit_bytes=scoped),
    )(
        grad_y, grad_reach, conv_low, conv_low, conv_low, incoming, cum_pairs, cum_rows, step_rows,
        skip_row,
    )


def turn(base, incoming, proj_c, decay, gate_parts, grad_mixed, gain):
    tokens, heads = base.shape[0], 8
    width = heads * HEADDIM
    groups = INNER // width
    share = groups // len(gate_parts)
    once = lambda p, j: (0, jnp.where(p == 0, j, groups - 1))
    last = lambda p, j: (0, jnp.where(p == 0, 0, j))
    wide = jax.ShapeDtypeStruct((tokens, INNER), bf16)
    return pl.pallas_call(
        turn_body,
        grid=(2, groups),
        in_specs=[
            pl.BlockSpec((tokens, width), once),
            pl.BlockSpec((width, STATE), lambda p, j: (jnp.where(p == 0, j, groups - 1), 0)),
            pl.BlockSpec((tokens, STATE), lambda p, j: (0, 0)),
            pl.BlockSpec((tokens, STATE), lambda p, j: (0, 0)),
            pl.BlockSpec((tokens, width), once),
            pl.BlockSpec((1, width), lambda p, j: (0, j)),
        ]
        + [
            pl.BlockSpec(
                (tokens, width), lambda p, j, k=k: (0, jnp.clip(j - k * share, 0, share - 1))
            )
            for k in range(len(gate_parts))
        ],
        out_specs=[pl.BlockSpec((tokens, width), last)] * 4
        + [
            pl.BlockSpec((width, STATE), lambda p, j: (jnp.where(p == 0, 0, j), 0)),
            pl.BlockSpec((1, width), last),
        ],
        out_shape=[wide] * 4
        + [jax.ShapeDtypeStruct((INNER, STATE), f32), jax.ShapeDtypeStruct((1, INNER), f32)],
        scratch_shapes=[
            pltpu.VMEM((groups, tokens, width), f32),
            pltpu.VMEM((groups, tokens, width), f32),
            pltpu.VMEM((tokens, 1), f32),
            pltpu.VMEM((tokens, 1), f32),
        ],
        name="turn",
        cost_estimate=no_cost,
        compiler_params=pltpu.CompilerParams(vmem_limit_bytes=whole_vmem),
    )(base, incoming, proj_c, decay, grad_mixed, gain[None], *gate_parts)


def ahead(rows, count, distance):
    return (pltpu.roll(rows, rows.shape[0] - distance, 0) if distance else rows)[:count]


def leave_body(
    steps, proj_ref, edge_ref, taps_ref, shift_ref, low_ref, part_ref, fresh_ref, incoming_ref, b_ref,
    weigh_ref, b_part_ref, c_part_ref,
    grad_ref, grad_more_ref, first_ref, last_ref, taps_grad_ref, shift_grad_ref, factor_ref, crossed_ref,
    b_total, wide_factor,
):
    j = pl.program_id(0)

    def conv_back(grad_out):
        rows = proj_ref[...].astype(f32)
        window = jnp.concatenate([edge_ref[...].astype(f32), rows], axis=0)
        taps = taps_ref[...]
        moved = [
            (pltpu.roll(window, CONV - 1 - k, 0) if k < CONV - 1 else window)[8:]
            for k in range(CONV)
        ]
        total = shift_ref[...]
        for k in range(CONV):
            total = total + taps[k : k + 1] * moved[k]
        sig = jax.nn.sigmoid(total)
        grad = grad_out * (sig * (1.0 + total * (1.0 - sig)))
        shift_grad_ref[...] = jnp.sum(grad, axis=0, keepdims=True)
        taps_grad_ref[...] = jnp.concatenate(
            [jnp.sum(grad * part, axis=0, keepdims=True) for part in moved], axis=0
        )
        none = jnp.zeros((8, grad.shape[1]), f32)
        after_it = jnp.concatenate([grad, none], axis=0)
        before_it = jnp.concatenate([none, grad[:8]], axis=0)
        inner, outer = 0.0, 0.0
        for k in range(CONV):
            tap = taps[k : k + 1]
            inner = inner + tap * ahead(after_it, grad.shape[0], CONV - 1 - k)
            outer = outer + tap * ahead(before_it, 8, CONV - 1 - k)
        cut = FIRST // grad.shape[1]

        @pl.when(j < cut)
        def _():
            grad_ref[...] = inner.astype(bf16)

        @pl.when(j >= cut)
        def _():
            grad_more_ref[...] = inner.astype(bf16)

        last_ref[...] = inner[grad.shape[0] - 8 :]
        first_ref[...] = outer

    @pl.when(j == 0)
    def _():
        b_total[...] = b_part_ref[...]

    @pl.when(j < steps)
    def _():
        fresh = fresh_ref[...]
        x = low_ref[...].astype(f32)
        heads = x.shape[1] // HEADDIM
        weigh = pairs_along(group_columns(weigh_ref, j, heads))
        grad_weighted = lax.dot_general(
            b_ref[...], fresh, (((1,), (1,)), ((), ())), preferred_element_type=f32
        )
        weighted = (x * weigh).astype(bf16)
        b_total[...] += jnp.dot(weighted, fresh, preferred_element_type=f32)
        product = grad_weighted * x
        keep_columns(
            wide_factor,
            heads * j,
            [
                jnp.sum(product[:, i * HEADDIM : (i + 1) * HEADDIM], axis=1, keepdims=True)
                for i in range(heads)
            ],
        )
        both = fresh.astype(f32) * incoming_ref[...].astype(f32)
        for i in range(heads):
            row = pl.ds(heads * j + i, 1)
            crossed_ref[row, :] = jnp.sum(
                both[i * HEADDIM : (i + 1) * HEADDIM], axis=0, keepdims=True
            )
        conv_back(part_ref[...] + grad_weighted * weigh)

    @pl.when(j == steps)
    def _():
        factor_ref[...] = wide_factor[...].T[:HEADS]
        conv_back(jnp.concatenate([b_total[...], c_part_ref[...]], axis=1))


def leave(projected, edge, taps, shift, conv_low, part, grad_fresh, incoming, weigh, b_part, c_part):
    tokens, heads = part.shape[0], 4
    width = heads * HEADDIM
    steps = INNER // width
    cut = FIRST // width
    inside = lambda j: jnp.minimum(j, steps - 1)
    block = lambda rows: pl.BlockSpec((rows, width), lambda j: (0, j))
    whole = lambda rows: pl.BlockSpec((rows, STATE), lambda j: (0, 0))
    state = pl.BlockSpec((width, STATE), lambda j: (inside(j), 0))
    return pl.pallas_call(
        functools.partial(leave_body, steps),
        grid=(steps + 1,),
        in_specs=[
            block(tokens),
            block(8),
            block(CONV),
            block(1),
            block(tokens),
            pl.BlockSpec((tokens, width), lambda j: (0, inside(j))),
            state,
            state,
            pl.BlockSpec((tokens, STATE), lambda j: (0, INNER // STATE)),
            whole(tokens),
            whole(tokens),
            whole(tokens),
        ],
        out_specs=[
            pl.BlockSpec((tokens, width), lambda j: (0, jnp.minimum(j, cut - 1))),
            pl.BlockSpec((tokens, width), lambda j: (0, jnp.maximum(j - cut, 0))),
            block(8),
            block(8),
            block(CONV),
            block(1),
            pl.BlockSpec((HEADS, tokens), lambda j: (0, 0)),
            whole(HEADS),
        ],
        out_shape=[
            jax.ShapeDtypeStruct((tokens, FIRST), bf16),
            jax.ShapeDtypeStruct((tokens, CHANNELS - FIRST), bf16),
            jax.ShapeDtypeStruct((8, CHANNELS), f32),
            jax.ShapeDtypeStruct((8, CHANNELS), f32),
            jax.ShapeDtypeStruct((CONV, CHANNELS), f32),
            jax.ShapeDtypeStruct((1, CHANNELS), f32),
            jax.ShapeDtypeStruct((HEADS, tokens), f32),
            jax.ShapeDtypeStruct((HEADS, STATE), f32),
        ],
        scratch_shapes=[pltpu.VMEM((tokens, STATE), f32), pltpu.VMEM((tokens, STATE), f32)],
        name="leave",
        cost_estimate=no_cost,
        compiler_params=pltpu.CompilerParams(vmem_limit_bytes=whole_vmem),
    )(
        projected, edge, taps, shift[None], conv_low, part, grad_fresh, incoming, conv_low,
        weigh, b_part, c_part,
    )


def rms_scale(values, gain):
    return values * lax.rsqrt(jnp.mean(values * values, axis=-1, keepdims=True) + epsilon) * gain


def pack(arrays):
    flat = jnp.concatenate([a.reshape(-1) for a in arrays])
    pad = -flat.shape[0] % 1024
    return jnp.pad(flat, (0, pad)).reshape(-1, 128)


def local(
    hidden,
    lengths,
    norm_gain,
    in_weight,
    conv_weight,
    conv_bias,
    dt_bias,
    a_log,
    skip_d,
    gate_gain,
    out_weight,
    out_grad,
):
    ring = Ring(lax.axis_size("seq"), lax.axis_size("fsdp"))
    ring.clock = clock = Clock(hidden[0, :8, :128])
    _, row_count, model_width = hidden.shape
    fsdp_index = lax.axis_index("fsdp")
    where = places(ring)
    tokens = hidden[0].astype(f32)

    small = [norm_gain, conv_weight, conv_bias, dt_bias, a_log, skip_d, gate_gain]
    in_rows = in_weight.T
    shared = Spread(ring, in_rows, INNER)
    shared.first(at_once=True)
    near_rows = ring.core(in_rows)
    packed = pack(small)
    spread = jnp.zeros((ring.fsdp,) + packed.shape, bf16)
    for (d, e), place in where.items():
        block = ring.relative(packed, d, e)
        spread = lax.dynamic_update_slice_in_dim(spread, block[None], place, axis=0)
    clock.defer(ring.fsdp - 1)
    spread = spread.reshape(ring.fsdp, -1)
    whole_small, at = [], 0
    for part in small:
        piece = spread[:, at : at + part.size]
        at += part.size
        if part.ndim == 2:
            piece = piece.reshape((ring.fsdp,) + part.shape).transpose(1, 0, 2)
            whole_small.append(piece.reshape(part.shape[0], -1).astype(f32))
        else:
            whole_small.append(piece.reshape(-1).astype(f32))
    gain_norm, conv_taps, conv_shift, step_bias, rate_log, skip_gain, gain_gate = whole_small

    gate_pieces = Pieces(ring, in_rows[:INNER], 3)
    out_spread = Spread(ring, out_weight, 0, whole_only=True)
    clock.tick()
    shared.second()
    out_spread.first()
    clock.tick()
    shared.third()
    gate_pieces.send(later=1)
    clock.tick()
    shared.fourth()
    gate_pieces.send(later=3)
    out_spread.second()
    clock.tick()
    tile = 768
    weight_conv = {key: (array, 0) for key, array in shared.whole(near_rows).items()}
    weight_conv[0, 0] = (in_rows, INNER // tile)
    weight_conv[0, 1] = (near_rows, INNER // tile)

    position = lax.axis_index("seq") * row_count + lax.broadcasted_iota(
        jnp.int32, (row_count, 1), 0
    )
    grad_out = jnp.where(position < lengths[0], out_grad[0], jnp.zeros_like(out_grad[0]))

    normed, pull_norm = jax.vjp(rms_scale, tokens, gain_norm)
    normed = normed.astype(bf16)
    depth = in_weight.shape[0]

    normed_columns = [
        lax.dynamic_slice_in_dim(normed, place * depth, depth, axis=1) for place in where.values()
    ]
    normed_for = columns_for(ring, normed)
    projected = project(normed_columns, list(weight_conv.values()), tile, PROJ - INNER)
    (projected,) = clock.tick(projected)
    edge_rows = ring.next_block(projected[row_count - 8 :, :CHANNELS], 1)
    near_out = ring.core(clock.now(out_weight))
    clock.defer()
    cum, weigh, decay, cum_rows, step_rows, through = steps(projected, step_bias, rate_log)
    cum, weigh, edge_rows = clock.tick(cum, weigh, edge_rows)
    gate_pieces.send(later=1)
    conv_low, fresh_state = enter(
        ring,
        projected,
        edge_rows,
        conv_taps,
        conv_shift,
        weigh,
        spread_factors(ring, through[0, :HEADS]),
    )
    proj_b = conv_low[:, INNER : INNER + STATE]
    proj_c = conv_low[:, INNER + STATE :]
    (fresh_state,) = clock.tick(fresh_state)
    blocks = lax.all_to_all(fresh_state, "seq", 0, 0, tiled=True)
    out_spread.third()
    gate_pieces.pass_on(0)
    gate_pieces.pass_on(1)
    skip_row = jnp.repeat(skip_gain, HEADDIM)[None]
    base = inside(conv_low, cum, cum_rows, step_rows, skip_row)
    blocks, base = clock.tick(blocks, base)
    factor = blocks[:, INNER // ring.seq :]
    (states,) = clock.tick(carried(ring, blocks, factor, False))
    incoming = returned(ring, states).reshape(INNER, STATE)
    gate_pieces.pass_on(2)
    out_spread.fourth()
    weight_gate = gate_pieces.pieces(in_rows, near_rows)
    weight_out = out_spread.whole(near_out)
    grad_pieces = Pieces(ring, grad_out)
    grad_pieces.send()
    gate_rows = gate_pieces.rows
    gate_parts = [
        project(normed_columns, [weight_gate[key][at] for key in where], gate_rows, gate_rows)
        for at in range(3)
    ]
    wide = out_weight.shape[0]
    place_row = jnp.stack(list(where.values())).astype(jnp.int32)
    grad_mixed = to_inner(grad_out, list(weight_out.values()), place_row)
    incoming, grad_mixed, *gate_parts = clock.tick(incoming, grad_mixed, *gate_parts)
    normed_all = trade_columns(ring, {key: clock.now(part) for key, part in normed_for.items()})
    grad_pieces.near()
    mixed, grad_y, grad_gate, grad_reach, direct, grad_g_gate = turn(
        base, incoming, proj_c, decay, gate_parts, grad_mixed, gain_gate
    )
    direct, mixed, grad_y, grad_reach, grad_gate = clock.tick(
        direct, mixed, grad_y, grad_reach, grad_gate
    )
    blocks = lax.all_to_all(direct.reshape(ring.seq, -1, STATE), "seq", 0, 0, tiled=True)
    mixed_all = trade_columns(ring, columns_for(ring, mixed))
    clock.defer(len(mixed_all) - 1, 2)
    grad_out_all = grad_pieces.whole()
    x_part, b_part, c_part, grad_step, grad_cum, grad_skip = inside_back(
        grad_y, grad_reach, conv_low, incoming, cum, cum_rows, step_rows, skip_row
    )
    gate_grads = Pieces(ring, grad_gate)
    gate_grads.send(later=2)
    blocks, x_part, b_part, c_part = clock.tick(blocks, x_part, b_part, c_part)
    states = carried(ring, blocks, factor, True)
    (states,) = clock.tick(states)
    chain_grad = returned(ring, states)
    mixed_all = {key: clock.now(block) for key, block in mixed_all.items()}
    total_w_out = Total(ring, weight_grad(mixed_all, grad_out_all, 384))
    total_w_out.step()
    clock.defer()
    gate_grads.near()
    total_w_gate = Total(ring, weight_grad(gate_grads.whole(), normed_all, 768))
    (total_w_gate.value,) = clock.tick(total_w_gate.value)
    total_w_gate.step()
    clock.defer()
    mixed = clock.now(mixed)
    mixed_columns = [
        lax.dynamic_slice_in_dim(mixed, place * wide, wide, axis=1) for place in where.values()
    ]
    output = output_rows(hidden[0], mixed_columns, list(weight_out.values()))
    chain_grad, output = clock.tick(chain_grad, output)
    total_w_out.step()
    grad_conv, grad_more, first_rows, last_rows, grad_taps, grad_shift, grad_factor, crossed = leave(
        projected,
        edge_rows,
        conv_taps,
        conv_shift,
        conv_low,
        x_part,
        chain_grad.reshape(INNER, STATE),
        incoming,
        weigh,
        b_part,
        c_part,
    )
    grad_conv, grad_more, last_rows, first_rows = clock.tick(
        grad_conv, grad_more, last_rows, first_rows
    )
    total_w_out.step()
    clock.defer()
    last_rows = (last_rows + ring.next_block(first_rows, -1)).astype(bf16)
    grad_conv = lax.dynamic_update_slice_in_dim(
        grad_conv, last_rows[:, :FIRST], row_count - 8, axis=0
    )
    (grad_conv,) = clock.tick(grad_conv)
    grad_more = lax.dynamic_update_slice_in_dim(
        grad_more, last_rows[:, FIRST:], row_count - 8, axis=0
    )
    grad_dt_raw, grad_step_bias, grad_rate = steps_back(
        projected,
        step_bias,
        rate_log,
        step_rows,
        cum_rows,
        grad_step,
        grad_cum,
        clock.now(grad_factor),
        crossed,
    )
    grad_tail = jnp.concatenate([grad_conv, grad_more, grad_dt_raw[:, :HEADS]], axis=1)

    first = Pieces(ring, grad_conv)
    last = Pieces(ring, jnp.concatenate([grad_more, grad_dt_raw], axis=1))
    first.send()
    first.near()
    total_w_gate.step()
    clock.tick()
    last.send(later=1)
    last.near()
    total_first = Total(ring, weight_grad(first.whole(), normed_all, 896))
    (total_first.value,) = clock.tick(total_first.value)
    total_first.step()
    total_w_out.step()
    total_w_gate.step()
    clock.defer(2)
    grad_shards = to_model(
        grad_gate, clock.now(grad_tail), list(weight_gate.values()), [
            (array, block * tile) for array, block in weight_conv.values()
        ]
    )
    (grad_shards,) = clock.tick(grad_shards)
    total_last = Total(ring, weight_grad(last.whole(), normed_all, 1664))
    (total_last.value,) = clock.tick(total_last.value)
    total_last.step()
    total_first.step()
    total_w_out.step()
    total_w_gate.step()
    grad_normed = jnp.zeros((row_count, model_width), f32)
    for k, place in enumerate(where.values()):
        grad_normed = lax.dynamic_update_slice_in_dim(
            grad_normed, grad_shards[k], place * depth, axis=1
        )
    grad_skip = jnp.sum(clock.now(grad_skip).reshape(HEADS, HEADDIM), axis=1)
    grad_tokens, grad_g_norm = pull_norm(grad_normed)
    hidden_grad = (grad_tokens + grad_out.astype(f32)).astype(bf16)
    hidden_grad, grad_g_norm = clock.tick(hidden_grad, grad_g_norm)
    grad_shift, grad_step_bias, grad_rate, grad_g_gate = (
        clock.now(part) for part in (grad_shift, grad_step_bias, grad_rate, grad_g_gate)
    )
    parts = [grad_g_norm, grad_taps, grad_shift[0], grad_step_bias[:, 0], grad_rate[:, 0]]
    parts += [grad_skip, grad_g_gate[0]]
    small_total = SmallSum(ring, pack(parts))
    total_w_out.step()
    clock.defer()
    total_first.step()
    total_last.step()
    total_w_gate.step()
    clock.tick()
    small_total.step()
    small_total.step()
    total_w_gate.halves()
    clock.defer()
    total_first.step()
    total_last.step()
    clock.tick()
    small_total.step()
    total_first.step()
    total_last.step()
    clock.tick()
    small_total.step()
    total_first.halves()
    clock.defer()
    total_last.step()
    clock.tick()
    small_total.step()
    total_last.halves()
    summed = small_total.finish().reshape(-1)
    shares, at = [], 0
    for part in parts:
        piece = summed[at : at + part.size].reshape(part.shape)
        at += part.size
        width = part.shape[-1] // ring.fsdp
        shares.append(
            lax.dynamic_slice_in_dim(piece, fsdp_index * width, width, axis=part.ndim - 1)
        )
    total_w_in = jnp.zeros((PROJ, depth), f32)
    total_w_in = place_rows(total_w_in, total_w_gate.halves(), 0, INNER)
    total_w_in = place_rows(total_w_in, total_first.halves(), INNER, FIRST)
    total_w_in = place_rows(
        total_w_in, total_last.halves(), INNER + FIRST, PROJ - INNER - FIRST
    )
    total_w_in = total_w_in.T
    total_w_out = total_w_out.finish()
    return (
        output[None],
        hidden_grad[None],
        shares[0],
        total_w_in,
        shares[1],
        shares[2],
        shares[3],
        shares[4],
        shares[5],
        shares[6],
        total_w_out,
    )


def solution(mesh):
    placed = (
        P("fsdp", "seq", None),
        P("fsdp"),
        P("fsdp"),
        P("fsdp", None),
        P(None, "fsdp"),
        P("fsdp"),
        P("fsdp"),
        P("fsdp"),
        P("fsdp"),
        P("fsdp"),
        P("fsdp", None),
        P("fsdp", "seq", None),
    )
    return jax.shard_map(
        local,
        mesh=mesh,
        in_specs=placed,
        out_specs=(
            P("fsdp", "seq", None),
            P("fsdp", "seq", None),
            P("fsdp"),
            P("fsdp", None),
            P(None, "fsdp"),
            P("fsdp"),
            P("fsdp"),
            P("fsdp"),
            P("fsdp"),
            P("fsdp"),
            P("fsdp", None),
        ),
        check_vma=False,
    )
```
